32 devices in a mesh: dp: 8 (over y, x, core), seq: 4 (over z).
Axes of the slice: x: 2, y: 2, z: 4, core: 2. Of those that a mesh axis runs over, the one named last changes fastest.
Arguments:
- inputs: bfloat16 [8, 1, 5120, 512], P('dp', None, 'seq'), may hold values from -6 to 6
- lengths: int32 [8, 1, 3], P('dp'), may hold values from 0 to 3072, as said below
- cotangent: bfloat16 [8, 1, 5120, 512], P('dp', None, 'seq'), may hold values from -6 to 6
- gain_one: bfloat16 [512], P('dp'), may hold values from 0.5 to 1.5
- shift_one: bfloat16 [512], P('dp'), may hold values from -3 to 3
- w_qkv: bfloat16 [512, 1536], P('dp'), may hold values from -0.25 to 0.25
- b_qk: bfloat16 [1024], P('dp'), may hold values from -3 to 3
- w_out: bfloat16 [512, 512], P('dp'), may hold values from -2 to 2
- b_out: bfloat16 [512], P('dp'), may hold values from -3 to 3
- gain_two: bfloat16 [512], P('dp'), may hold values from 0.5 to 1.5
- shift_two: bfloat16 [512], P('dp'), may hold values from -3 to 3
- w_up: bfloat16 [512, 2048], P('dp'), may hold values from -0.25 to 0.25
- b_up: bfloat16 [2048], P('dp'), may hold values from -3 to 3
- w_down: bfloat16 [2048, 512], P('dp'), may hold values from -0.125 to 0.125
- b_down: bfloat16 [512], P('dp'), may hold values from -3 to 3
Outputs:
- outputs: bfloat16 [8, 1, 5120, 512], P('dp', None, 'seq')
- grad_inputs: float32 [8, 1, 5120, 512], P('dp', None, 'seq')
- grad_gain_one: float32 [512], P('dp')
- grad_shift_one: float32 [512], P('dp')
- grad_w_qkv: float32 [512, 1536], P('dp')
- grad_b_qk: float32 [1024], P('dp')
- grad_w_out: float32 [512, 512], P('dp')
- grad_b_out: float32 [512], P('dp')
- grad_gain_two: float32 [512], P('dp')
- grad_shift_two: float32 [512], P('dp')
- grad_w_up: float32 [512, 2048], P('dp')
- grad_b_up: float32 [2048], P('dp')
- grad_w_down: float32 [2048, 512], P('dp')
- grad_b_down: float32 [512], P('dp')
The draws below stay inside these ranges and needn't reach their ends.
Inputs may be any that keep to these rules, and one draw needn't show every extreme that they name: `lengths`: each pack holds an image of 784 rows, then one of 3072 rows, then either another of 784 rows or none (length 0); the rest of the pack is one more segment.
All inputs are finite; a program needn't handle non-finite values.
Results may differ from the reference program's by a relative error of at most 0.03.
The reference program's roundings to bfloat16 on the way count: a program that leaves them out, or rounds other values in their place, can miss the bound.
Values may be sent and summed in bfloat16 or wider, within the bound.
A program may use at most 192 MiB of HBM per device.

```python
import jax
import jax.numpy as jnp
from jax import lax

D = 512
HEADS = 8
FF = 2048
SMALL_LEN = 784
BIG_LEN = 3072
BLOCK = 640
PACKS = 1
GROUP = 5120
N_DP = 8


def draw_lengths(key, part):
    key = jax.random.fold_in(key, 7)
    extra = jax.random.randint(key, (N_DP, PACKS), 0, 2).astype(jnp.int32)
    first = jnp.full((N_DP, PACKS), SMALL_LEN, jnp.int32)
    second = jnp.full((N_DP, PACKS), BIG_LEN, jnp.int32)
    return jnp.stack([first, second, extra * SMALL_LEN], axis=-1).astype(jnp.int32)


def strengthened(values, own_key, source, target, shards_of, factor):
    def block_of(position):
        return (jnp.arange(values.shape[position]) // (values.shape[position] // shards_of)).reshape((-1,) + (1,) * (values.ndim - 1 - position))

    near = jax.random.permutation(own_key, shards_of)[block_of(target)]
    far = (block_of(target) + shards_of // 2) % shards_of
    return jnp.where((block_of(source) == near) | (block_of(source) == far), factor * values, values)


def shard_levels(rng, dims, cuts, smallest, high):
    factor_of = 1.0
    for axis_at, parts in cuts:
        draws = jax.random.uniform(jax.random.fold_in(jax.random.fold_in(rng, 6), axis_at), (parts,), jnp.float32, smallest / len(cuts), high / len(cuts))
        factor_of = factor_of * jnp.repeat(jnp.exp(draws), dims[axis_at] // parts).reshape((-1,) + (1,) * (len(dims) - 1 - axis_at))
    return factor_of


def noise(stream_key, extent, spread, limit, cuts=(), held_as=jnp.bfloat16):
    entries = jax.random.normal(stream_key, extent, jnp.float32) * spread
    if len(cuts) > 0:
        entries = shard_levels(stream_key, extent, cuts, -0.22, 0.18) * entries
    return jnp.clip(entries, min=-limit, max=limit).astype(held_as)


def bell_draw_with(own_key, dims, scale, reach, pieces, heavy, kind=jnp.bfloat16):
    entries = scale * jax.random.normal(own_key, dims, jnp.float32)
    if pieces:
        entries = entries * shard_levels(own_key, dims, pieces, -0.22, 0.18)
    return jnp.clip(strengthened(entries, jax.random.fold_in(own_key, 3), *heavy), -reach, reach).astype(kind)


def setup_inputs(seed: int = 0) -> dict:
    arg_keys = jax.random.split(jax.random.key(seed), 16)
    inputs = noise(arg_keys[0], (N_DP, PACKS, GROUP, D), 1.0, 6.0, ((0, 8), (2, 4)))
    lengths = draw_lengths(jax.random.fold_in(arg_keys[15], 71), 0)
    cotangent = bell_draw_with(arg_keys[2], (N_DP, PACKS, GROUP, D), 1.0, 6.0, ((0, 8), (2, 4)), (0, 3, 8, 2.0))
    gain_one = jnp.clip(1.0 + 0.1 * jax.random.normal(arg_keys[3], (D,), jnp.float32), 0.5, 1.5).astype(jnp.bfloat16)
    shift_one = noise(arg_keys[4], (D,), 0.5, 3.0, ((0, 8),))
    w_qkv = noise(arg_keys[5], (D, 3 * D), D ** -0.5, 0.25, ((0, 8),))
    b_qk = noise(arg_keys[6], (2 * D,), 0.5, 3.0, ((0, 8),))
    w_out = noise(arg_keys[7], (D, D), (D // 64) ** -0.5, 2.0, ((0, 8),))
    b_out = noise(arg_keys[8], (D,), 0.5, 3.0, ((0, 8),))
    gain_two = jnp.clip(1.0 + 0.1 * jax.random.normal(arg_keys[9], (D,), jnp.float32), 0.5, 1.5).astype(jnp.bfloat16)
    shift_two = noise(arg_keys[10], (D,), 0.5, 3.0, ((0, 8),))
    w_up = noise(arg_keys[11], (D, FF), D ** -0.5, 0.25, ((0, 8),))
    b_up = noise(arg_keys[12], (FF,), 0.5, 3.0, ((0, 8),))
    w_down = noise(arg_keys[13], (FF, D), FF ** -0.5, 0.125, ((0, 8),))
    b_down = noise(arg_keys[14], (D,), 0.5, 3.0, ((0, 8),))
    return dict(inputs=inputs, lengths=lengths, cotangent=cotangent, gain_one=gain_one, shift_one=shift_one, w_qkv=w_qkv, b_qk=b_qk, w_out=w_out, b_out=b_out, gain_two=gain_two, shift_two=shift_two, w_up=w_up, b_up=b_up, w_down=w_down, b_down=b_down)


highest = lax.Precision.HIGHEST
eps_norm = 1e-05
eps_attn = 1e-06

@jax.custom_vjp
def low(v):
    return lax.optimization_barrier(v.astype(jnp.bfloat16)).astype(jnp.float32)

@jax.custom_vjp
def low_back(v):
    return v

def low_keep(v):
    return (low(v), None)

def low_pass(kept, grad):
    return (grad,)

def back_keep(v):
    return (v, None)

def back_low(kept, grad):
    return (low(grad),)
low.defvjp(low_keep, low_pass)
low_back.defvjp(back_keep, back_low)

def norm_layer(values, scale_gain, scale_shift):
    row_mean = lax.optimization_barrier(jnp.mean(values, axis=-1, keepdims=True))
    centred = values - row_mean
    variance = lax.optimization_barrier(jnp.mean(centred * centred, axis=-1, keepdims=True))
    return centred * lax.rsqrt(variance + eps_norm) * scale_gain + scale_shift

def feature(values):
    return jax.nn.elu(values) + 1.0

def segment_ids(lengths_row, positions):
    bounds = jnp.cumsum(lengths_row).astype(jnp.int32)
    return lax.optimization_barrier(jnp.sum((positions[:, None] >= bounds[None, :]).astype(jnp.int32), axis=1)).astype(jnp.int32)

def attend_block(carried, block_items):
    key_state, key_total, carry_segment = carried
    query_rows, key_rows, value_rows, segments = block_items
    positions = jnp.arange(segments.shape[0], dtype=jnp.int32)
    visible = (positions[None, :] <= positions[:, None]) & (segments[:, None] == segments[None, :])
    products = jnp.einsum('ihe,jhe->hij', query_rows, key_rows, precision=highest)
    scores = low_back(jnp.where(visible[None], products, 0.0))
    alive_rows = (segments == carry_segment).astype(jnp.float32)
    within = jnp.einsum('hij,jhf->ihf', low(scores), value_rows, precision=highest)
    before = jnp.einsum('ihe,hef->ihf', query_rows, key_state, precision=highest)
    numerator = low_back(within + alive_rows[:, None, None] * before)
    denominator = lax.optimization_barrier(jnp.sum(scores, axis=2)).T + alive_rows[:, None] * jnp.einsum('ihe,he->ih', query_rows, key_total, precision=highest) + eps_attn
    result = numerator / denominator[:, :, None]
    last_segment = segments[-1]
    keeping = (last_segment == carry_segment).astype(jnp.float32)
    weights = (segments == last_segment).astype(jnp.float32)
    key_state = keeping * key_state + jnp.einsum('jhe,jhf->hef', key_rows, weights[:, None, None] * value_rows, precision=highest)
    key_total = keeping * key_total + jnp.einsum('jhe,j->he', key_rows, weights, precision=highest)
    return ((key_state, key_total, last_segment), result)

def attention_pack(query_rows, key_rows, value_rows, segments):
    group_rows, model_width = query_rows.shape
    head_size = model_width // HEADS
    block_count = group_rows // BLOCK

    def blocks(array):
        return array.reshape((block_count, BLOCK) + array.shape[1:])
    shaped = tuple((blocks(array.reshape(group_rows, HEADS, head_size)) for array in (query_rows, key_rows, value_rows)))
    initial = (jnp.zeros((HEADS, head_size, head_size), jnp.float32), jnp.zeros((HEADS, head_size), jnp.float32), jnp.array(-1, jnp.int32))
    _, results = lax.scan(jax.checkpoint(attend_block), initial, shaped + (blocks(segments),))
    return results.reshape(group_rows, model_width)

def pack_forward(inputs_pack, segments, params):
    gain_a, shift_a, weight_qkv, bias_qk, weight_out, bias_out, gain_b, shift_b, weight_up, bias_up, weight_down, bias_down = params
    model_width = inputs_pack.shape[1]
    normed = low(norm_layer(inputs_pack, gain_a, shift_a))
    bias_full = jnp.concatenate([bias_qk, jnp.zeros((model_width,), bias_qk.dtype)])
    mixed_pre = low_back(jnp.dot(normed, weight_qkv, precision=highest) + bias_full)
    query_rows = low_back(low(feature(mixed_pre[:, :model_width])))
    key_rows = low_back(low(feature(mixed_pre[:, model_width:2 * model_width])))
    value_rows = low_back(low(mixed_pre[:, 2 * model_width:]))
    heard_low = low_back(low(attention_pack(query_rows, key_rows, value_rows, segments)))
    branch_one = low_back(jnp.dot(heard_low, weight_out, precision=highest) + bias_out)
    middle = inputs_pack + branch_one
    normed_two = low(norm_layer(middle, gain_b, shift_b))
    hidden = low_back(jnp.dot(normed_two, weight_up, precision=highest) + bias_up)
    active = low(jax.nn.gelu(hidden, approximate=False))
    branch_two = low_back(jnp.dot(active, weight_down, precision=highest) + bias_down)
    return middle + branch_two

def reference(inputs, lengths, cotangent, gain_one, shift_one, w_qkv, b_qk, w_out, b_out, gain_two, shift_two, w_up, b_up, w_down, b_down):
    params = tuple((array.astype(jnp.float32) for array in (gain_one, shift_one, w_qkv, b_qk, w_out, b_out, gain_two, shift_two, w_up, b_up, w_down, b_down)))
    packed = inputs.reshape(N_DP * PACKS, GROUP, D).astype(jnp.float32)
    positions = jnp.arange(GROUP, dtype=jnp.int32)

    def pack_segments(lengths_row):
        return segment_ids(lengths_row, positions)
    segments = jax.vmap(pack_segments)(lengths.reshape(N_DP * PACKS, 3))
    pack_step = jax.checkpoint(pack_forward)

    def whole_layer(packed_rows, weights_all):

        def pack_loop(carried, pack_item):
            return (carried, pack_step(pack_item[0], pack_item[1], weights_all))
        return lax.scan(pack_loop, jnp.zeros((), jnp.float32), (packed_rows, segments))[1]
    results, pullback = jax.vjp(whole_layer, packed, params)
    grad_rows, grad_params = pullback(cotangent.reshape(N_DP * PACKS, GROUP, D).astype(jnp.float32))
    return (results.reshape(inputs.shape).astype(jnp.bfloat16), grad_rows.reshape(inputs.shape), grad_params[0], grad_params[1], grad_params[2], grad_params[3], grad_params[4], grad_params[5], grad_params[6], grad_params[7], grad_params[8], grad_params[9], grad_params[10], grad_params[11])
```

```python
import functools

import jax
import jax.numpy as jnp
from jax import lax
from jax.experimental import pallas as pl
from jax.experimental.pallas import tpu as pltpu
from jax.sharding import PartitionSpec as P

HEADS = 8
CHUNK = 256
TALL = 640
LANES = 128
eps_norm = 1e-05
eps_attn = 1e-06
MESH = pl.DeviceIdType.MESH
f32 = jnp.float32
bf16 = jnp.bfloat16


def dot(a, b, ca, cb):
    return lax.dot_general(a, b, (((ca,), (cb,)), ((), ())), preferred_element_type=f32)


def nn(a, b):
    return dot(a, b, 1, 0)


def nt(a, b):
    return dot(a, b, 1, 1)


def tn(a, b):
    return dot(a, b, 0, 0)


def span(index, size):
    return pl.ds(pl.multiple_of(index * size, size), size)


def lanes_of(shape):
    return lax.broadcasted_iota(jnp.int32, shape, len(shape) - 1)


def rows_of(shape):
    return lax.broadcasted_iota(jnp.int32, shape, len(shape) - 2)


def fold_rows(values):
    rows, width = values.shape
    return jnp.sum(values.reshape(rows // 8, 8, width), axis=0)


def normalised(values):
    width = values.shape[-1]
    mean = jnp.sum(values, axis=-1, keepdims=True) * (1.0 / width)
    centred = values - mean
    variance = jnp.sum(centred * centred, axis=-1, keepdims=True) * (1.0 / width)
    scale = lax.rsqrt(variance + eps_norm)
    return centred * scale, scale


def norm_back(grad, gain, hat, scale):
    width = grad.shape[-1]
    a = grad * gain
    mean_a = jnp.sum(a, axis=-1, keepdims=True) * (1.0 / width)
    mean_ah = jnp.sum(a * hat, axis=-1, keepdims=True) * (1.0 / width)
    return (a - mean_a - hat * mean_ah) * scale


def gelu_pair(x):
    e = jnp.exp(x * x * -0.5)
    z = jnp.abs(x) * 0.7071067811865476
    t = 1.0 / (1.0 + 0.3275911 * z)
    poly = t * (
        0.254829592
        + t * (-0.284496736 + t * (1.421413741 + t * (-1.453152027 + t * 1.061405429)))
    )
    tail = 0.5 * poly * e
    cdf = jnp.where(x >= 0.0, 1.0 - tail, tail)
    return x * cdf, cdf + x * (0.3989422804014327 * e)


class Shape:
    def __init__(self, mesh, rows, width, hidden):
        self.dp = mesh.shape["dp"]
        self.seq = mesh.shape["seq"]
        self.chips = self.dp // 2
        self.side = max(k for k in range(1, self.chips + 1) if k * k <= self.chips and self.chips % k == 0)
        self.rows, self.width, self.hidden = rows, width, hidden
        self.chunks = rows // CHUNK
        self.pairs = width // LANES
        self.sizes = (width, width, 2 * width, width, width, width, hidden, width)
        self.vec_lanes = max(-(-n // self.dp // LANES) * LANES for n in self.sizes)
        w, h, d = width, hidden, self.dp
        self.weights = ((w // d, 3 * w), (w // d, w), (w // d, h), (h // d, w))
        self.gathers = (
            (0, 0, w),
            (0, w, w),
            (0, 2 * w, w),
            (1, 0, w),
            (2, 0, h // 2),
            (2, h // 2, h // 2),
            (3, 0, w),
        )
        self.scatters = (
            (3, 0, w),
            (2, 0, h),
            (1, 0, w),
            (0, 0, w),
            (0, w, w),
            (0, 2 * w, w),
        )


def kernel(
    s,
    lengths,
    x_ref,
    cot_any,
    vec_ref,
    wq_any,
    wo_any,
    wu_any,
    wd_any,
    out_any,
    gin_any,
    gq_out,
    go_out,
    gu_out,
    gd_out,
    vec_out,
    wq,
    wo,
    wu,
    wd,
    cot,
    n1,
    n1t,
    feat,
    acc,
    mask,
    state_in,
    state,
    state_b,
    n2t,
    act,
    hgrad,
    gmid,
    gone,
    vecs,
    vgot,
    vsum,
    vstage,
    vback,
    vz,
    vzback,
    msg,
    msg_in,
    rb0,
    rb1,
    zsrc,
    zr1,
    zr2,
    g_local,
    g_send,
    g_recv,
    v_send,
    v_recv,
    m_send,
    m_recv,
    r_send,
    r_recv,
    io_sem,
):
    dp, seq, chips, side = s.dp, s.seq, s.chips, s.side
    rows, width, hidden = s.rows, s.width, s.hidden
    me, z = lax.axis_index("dp"), lax.axis_index("seq")
    core, chip = lax.rem(me, 2), me // 2
    cy, cx = chip // side, lax.rem(chip, side)
    offsets = [(dy, dx) for dy in range(chips // side) for dx in range(side)][1:]

    def chip_at(dy, dx):
        ny = chips // side
        return lax.rem(cy + dy + ny, ny) * side + lax.rem(cx + dx + side, side)

    heard, dnum, stage_q = n1, cot, hgrad

    sibling = (chip * 2 + 1 - core, z)
    peers = [(chip_at(dy, dx) * 2 + core, z) for dy, dx in offsets]
    z_up, z_down = lax.rem(z + 1, seq), lax.rem(z + seq - 1, seq)

    def remote(src, dst, send, recv, device):
        return pltpu.make_async_remote_copy(
            src_ref=src,
            dst_ref=dst,
            send_sem=send,
            recv_sem=recv,
            device_id=device,
            device_id_type=MESH,
        )

    barrier = pltpu.get_barrier_semaphore()
    for step in range(1, dp):
        pl.semaphore_signal(
            barrier, inc=1, device_id=(lax.rem(me + step, dp), z), device_id_type=MESH
        )
    for step in range(1, seq):
        pl.semaphore_signal(
            barrier, inc=1, device_id=(me, lax.rem(z + step, seq)), device_id_type=MESH
        )
    pl.semaphore_wait(barrier, dp + seq - 2)

    vec_sends = []
    for step in range(1, dp):
        vec_sends.append(
            remote(
                vec_ref,
                vgot.at[me],
                v_send.at[step - 1],
                v_recv.at[step - 1],
                (lax.rem(me + step, dp), z),
            )
        )
        vec_sends[-1].start()
    vgot[me] = vec_ref[...]

    sources = (wq_any, wo_any, wu_any, wd_any)
    weights = (wq, wo, wu, wd)
    parity = lax.rem(z, 2)
    nk = len(peers)

    class Gather:
        def __init__(self, item):
            index, first, columns = s.gathers[item]
            self.buffer, self.source = weights[index], sources[index]
            self.half, self.quarter = columns // 2, columns // 4
            self.mine = first + parity * self.half
            self.other = first + (1 - parity) * self.half
            self.send, self.recv, self.local = g_send.at[item], g_recv.at[item], g_local.at[item]

        def columns(self, first, size):
            return pl.ds(pl.multiple_of(first, LANES), size)

        def part(self, owner, first, size):
            return self.buffer.at[owner // 2, lax.rem(owner, 2), :, self.columns(first, size)]

        def both(self, first, size, which):
            return self.buffer.at[:, which, :, self.columns(first, size)]

        def start(self):
            src = self.source.at[:, self.columns(self.mine, self.half)]
            dst = self.part(me, self.mine, self.half)
            self.own = pltpu.make_async_copy(src, dst, self.local)
            self.own.start()
            self.plane = [
                remote(src, dst, self.send.at[k], self.recv.at[k], peer)
                for k, peer in enumerate(peers)
            ]
            for copy in self.plane:
                copy.start()

        def middle(self):
            self.own.wait()
            for copy in self.plane:
                copy.wait_recv()
            mine, size = self.mine, self.quarter
            self.along = [
                remote(
                    self.both(mine + k * size, size, core),
                    self.both(mine + k * size, size, core),
                    self.send.at[nk + k],
                    self.recv.at[nk + k],
                    (me, (z_up, z_down)[k]),
                )
                for k in range(2)
            ]
            for copy in self.along:
                copy.start()
            self.across = [
                remote(
                    self.both(mine, self.half, core),
                    self.both(mine, self.half, core),
                    self.send.at[nk + 2],
                    self.recv.at[nk + 2],
                    sibling,
                )
            ]
            self.across[0].start()

        def late(self):
            size = self.quarter
            for k in range(2):
                there = self.both(self.other + k * size, size, core)
                remote(there, there, self.send.at[nk + k], self.recv.at[nk + k], sibling).wait_recv()
                copy = remote(there, there, self.send.at[nk + 3 + k], self.recv.at[nk + 3 + k], sibling)
                copy.start()
                self.across.append(copy)

        def finish(self):
            there = self.both(self.mine, self.half, 1 - core)
            remote(there, there, self.send.at[nk + 2], self.recv.at[nk + 2], sibling).wait_recv()
            for k in range(2):
                there = self.both(self.other + k * self.quarter, self.quarter, 1 - core)
                remote(
                    there, there, self.send.at[nk + 3 + k], self.recv.at[nk + 3 + k], sibling
                ).wait_recv()

        def drain(self):
            for copy in self.plane + self.along + self.across:
                copy.wait_send()

    gathers = [Gather(item) for item in range(len(s.gathers))]
    for item in range(3):
        gathers[item].start()
    cot_copy = pltpu.make_async_copy(cot_any, cot, io_sem.at[0])
    cot_copy.start()

    bound_0 = lengths[0]
    bound_1 = bound_0 + lengths[1]
    bound_2 = bound_1 + lengths[2]
    first_row = z * rows

    def segment(position):
        return sum((position >= bound).astype(jnp.int32) for bound in (bound_0, bound_1, bound_2))

    def same(a, b):
        return (a == b).astype(f32)

    prior = jnp.where(first_row > 0, segment(first_row - 1), -1)
    last = segment(first_row + rows - 1)

    def before(c):
        return jnp.where(first_row + c * CHUNK > 0, segment(first_row + c * CHUNK - 1), -1)

    def ending(c):
        return segment(first_row + (c + 1) * CHUNK - 1)

    def in_segment(c, which):
        shape = (CHUNK, LANES)
        return (segment(first_row + c * CHUNK + rows_of(shape)) == which).astype(f32)

    square = (CHUNK, CHUNK)
    pair = (LANES, LANES)
    lane_low = lanes_of((CHUNK, LANES)) < 64
    block_diag = (
        (lanes_of((LANES, 2 * LANES)) // 64) % 2 == rows_of((LANES, 2 * LANES)) // 64
    ).astype(f32)
    low_pair = lanes_of(pair) < 64
    low_half = (lanes_of(pair) & 63) < 32
    ones_low = lane_low.astype(bf16)
    ones_high = 1.0 - ones_low

    def mask_body(c, carry):
        down, across = rows_of(square), lanes_of(square)
        base = first_row + c * CHUNK
        alike = segment(base + down) == segment(base + across)
        mask[c] = (alike & (across <= down)).astype(f32).astype(bf16)
        return carry

    lax.fori_loop(0, s.chunks, mask_body, 0)

    for step in range(1, dp):
        source = lax.rem(me - step + dp, dp)
        remote(
            vec_ref, vgot.at[source], v_send.at[step - 1], v_recv.at[step - 1], (source, z)
        ).wait_recv()

    def one_hot(n):
        piece = n // dp
        tall = -(-piece // LANES) * LANES
        shape = (tall, n)
        return ((lanes_of(shape) & (piece - 1)) == rows_of(shape)).astype(f32).astype(bf16)

    def owner_mask(n):
        piece = n // dp
        shape = (dp, n)
        low = rows_of(shape) * piece
        return (lanes_of(shape) >= low) & (lanes_of(shape) < low + piece)

    for k, n in enumerate(s.sizes):
        table = one_hot(n)
        pieces = vgot[:, k, : table.shape[0]].astype(bf16)
        spread = jnp.where(owner_mask(n), nn(pieces, table), 0.0)
        vecs[k : k + 1, :n] = jnp.sum(spread, axis=0, keepdims=True)

    starts = [sum(s.sizes[:k]) for k in range(len(s.sizes))]

    def collect(k, first, values):
        at = starts[k] + first
        vsum[:, at : at + values.shape[1]] += fold_rows(values)

    gain_one, shift_one = vecs[0:1, :width], vecs[1:2, :width]
    for k, n in enumerate(s.sizes):
        vsum[:, starts[k] : starts[k] + n] = jnp.zeros((8, n), f32)

    def norm_body(c, carry):
        here = span(c, CHUNK)
        hat, _ = normalised(x_ref[here, :].astype(f32))
        normed = (hat * gain_one + shift_one).astype(bf16)
        n1[here, :] = normed
        n1t[:, here] = normed.T
        return carry

    lax.fori_loop(0, s.chunks, norm_body, 0)

    for item in range(3):
        gathers[item].middle()
    for item in range(3, len(gathers)):
        gathers[item].start()
    for item in range(3):
        gathers[item].late()
    for item in range(3):
        gathers[item].finish()
        weight = wq[:, :, :, item * width : (item + 1) * width].reshape(width, width)
        if item < 2:
            bias = vecs[2:3, item * width : (item + 1) * width]

        def project_body(c, carry):
            here = span(c, TALL)
            mixed = nn(n1[here, :], weight)
            if item < 2:
                mixed = mixed + bias
                mixed = jnp.where(mixed > 0.0, mixed + 1.0, jnp.exp(jnp.minimum(mixed, 0.0)))
            feat[here, item * width : (item + 1) * width] = mixed.astype(bf16)
            return carry

        lax.fori_loop(0, rows // TALL, project_body, 0)

    def cut(here, part, p):
        first = part * width + p * LANES
        return feat[here, first : first + LANES]

    for p in range(s.pairs):
        state[p] = jnp.zeros((LANES, 2 * LANES), f32)

    def state_body(c, carry):
        here = span(c, CHUNK)
        keep = same(ending(c), before(c))
        chosen = in_segment(c, ending(c)).astype(bf16)
        for p in range(s.pairs):
            wide = jnp.concatenate([cut(here, 2, p) * chosen, chosen], axis=1)
            now = state[p]
            state_in[c, p] = now
            state[p] = keep * now + tn(cut(here, 1, p), wide) * block_diag
        return carry

    lax.fori_loop(0, s.chunks, state_body, 0)

    def spread_ends(right):
        return 0.5 * (right + pltpu.roll(right, 32, 1))

    def packed(slot):
        halves = []
        ends = []
        for p in range(s.pairs):
            left = state[p, :, :LANES]
            right = state[p, :, LANES:]
            halves.append(left + pltpu.roll(left, 64, 1))
            ends.append(spread_ends(right + pltpu.roll(right, 64, 1)))
        for q in range(s.pairs // 2):
            msg[slot, q] = jnp.where(low_pair, halves[2 * q], halves[2 * q + 1]).astype(bf16)
        total = ends[0]
        lanes = LANES // s.pairs
        for p in range(1, s.pairs):
            total = jnp.where(lanes_of(pair) // lanes == p, ends[p], total)
        upper = total.astype(bf16).astype(f32)
        total = jnp.where(lanes_of(pair) % lanes < lanes // 2, upper, total - upper)
        msg[slot, s.pairs // 2] = total.astype(bf16)

    def unpacked(slot, step, p):
        sums = msg_in[slot, step, p // 2].astype(f32)
        turned = pltpu.roll(sums, 64, 1)
        left = jnp.where(low_pair, sums, turned) if p % 2 == 0 else jnp.where(low_pair, turned, sums)
        first = p * (LANES // s.pairs)
        middle = first + LANES // s.pairs // 2
        ends = msg_in[slot, step, s.pairs // 2].astype(f32)
        right = ends[:, first : first + 1] + ends[:, middle : middle + 1]
        return jnp.concatenate([left, jnp.broadcast_to(right, pair)], axis=1) * block_diag

    def message(slot, step, forward):
        target = lax.rem(z + step, seq) if forward else lax.rem(z - step + seq, seq)
        return remote(
            msg.at[slot],
            msg_in.at[slot, step - 1],
            m_send.at[slot, step - 1],
            m_recv.at[slot, step - 1],
            (me, target),
        )

    def send_states(slot, forward):
        packed(slot)
        for step in range(1, seq):

            @pl.when((z + step < seq) if forward else (z - step >= 0))
            def _():
                message(slot, step, forward).start()

    def take_states(slot, forward):
        for p in range(s.pairs):
            state[p] = jnp.zeros((LANES, 2 * LANES), f32)
        for step in range(1, seq):

            @pl.when((z - step >= 0) if forward else (z + step < seq))
            def _():
                message(slot, step, forward).wait_recv()
                if forward:
                    weight = same(segment((z - step + 1) * rows - 1), prior)
                else:
                    weight = same(segment((z + step) * rows - 1), last)
                for p in range(s.pairs):
                    state[p] = state[p] + weight * unpacked(slot, step - 1, p)

    def drain_states(slot, forward):
        for step in range(1, seq):

            @pl.when((z + step < seq) if forward else (z - step >= 0))
            def _():
                message(slot, step, forward).wait_send()

    send_states(0, True)
    gathers[3].middle()

    def inside_body(c, carry):
        here = span(c, CHUNK)
        seen = mask[c]
        for p in range(s.pairs):
            q, k, v = cut(here, 0, p), cut(here, 1, p), cut(here, 2, p)
            k_low, v_low = k * ones_low, v * ones_low
            k_high, v_high = k * ones_high, v * ones_high
            s_low = nt(q, k_low).astype(bf16) * seen
            s_high = nt(q, k_high).astype(bf16) * seen
            acc[here, 2 * p * LANES : (2 * p + 2) * LANES] = nn(
                s_low, jnp.concatenate([v_low, ones_low], axis=1)
            ) + nn(s_high, jnp.concatenate([v_high, ones_high], axis=1))
        return carry

    lax.fori_loop(0, s.chunks, inside_body, 0)
    gathers[3].late()
    for item in range(4, len(gathers)):
        gathers[item].middle()
    take_states(0, True)

    def join_body(c, carry):
        here = span(c, CHUNK)
        live = in_segment(c, before(c))
        carried = same(before(c), prior)
        for p in range(s.pairs):
            whole = state_in[c, p] + carried * state[p]
            upper = whole.astype(bf16)
            lower = (whole - upper.astype(f32)).astype(bf16)
            state_b[c, p, :LANES] = upper
            state_b[c, p, LANES:] = lower
            q = cut(here, 0, p)
            extra = nn(jnp.concatenate([q, q], axis=1), state_b[c, p])
            first = 2 * p * LANES
            numerator = acc[here, first : first + LANES] + live * extra[:, :LANES]
            denominator = acc[here, first + LANES : first + 2 * LANES] + live * extra[:, LANES:]
            inverse = 1.0 / (denominator + eps_attn)
            result = numerator * inverse
            acc[here, first : first + LANES] = result
            acc[here, first + LANES : first + 2 * LANES] = inverse
            heard[here, p * LANES : (p + 1) * LANES] = result.astype(bf16)
        return carry

    lax.fori_loop(0, s.chunks, join_body, 0)
    gathers[3].finish()
    for item in range(4, len(gathers)):
        gathers[item].late()
    for item in range(4, len(gathers)):
        gathers[item].finish()
    cot_copy.wait()

    bias_out, gain_two, shift_two = (vecs[k : k + 1, :width] for k in (3, 4, 5))
    bias_down = vecs[7:8, :width]
    tile = 512
    tall = s.weights[0][0]

    def forward_body(c, carry):
        here = span(c, TALL)
        middle = (
            x_ref[here, :].astype(f32)
            + nn(heard[here, :], wo[...].reshape(width, width))
            + bias_out
        )
        hat, scale = normalised(middle)
        normed = (hat * gain_two + shift_two).astype(bf16)
        n2t[:, here] = normed.T
        branch = cot[here, :]
        collect(7, 0, branch.astype(f32))
        total = middle + bias_down
        back = jnp.zeros((TALL, width), f32)
        for t in range(hidden // tile):
            cols = slice(t * tile, (t + 1) * tile)
            up = wu[:, :, :, cols].reshape(width, tile)
            per = chips * tile // hidden
            down = wd[t * per : (t + 1) * per].reshape(tile, width)
            active, slope = gelu_pair(nn(normed, up) + vecs[6:7, cols])
            active = active.astype(bf16)
            act[here, cols] = active
            grad = (slope * nt(branch, down)).astype(bf16)
            hgrad[span(c, TALL // (2 * tall)), :, :, cols] = grad.reshape(TALL // (2 * tall), 2, tall, tile)
            collect(6, t * tile, grad.astype(f32))
            total = total + nn(active, down)
            back = back + nt(grad, up)
        out_any_rows = total.astype(bf16)
        gone[here, :] = out_any_rows
        copy = pltpu.make_async_copy(gone.at[here, :], out_any.at[here, :], io_sem.at[1])
        copy.start()
        collect(4, 0, back * hat)
        collect(5, 0, back)
        grad_middle = branch.astype(f32) + norm_back(back, gain_two, hat, scale)
        gmid[here, :] = grad_middle
        copy.wait()
        low = grad_middle.astype(bf16)
        gone[here, :] = low
        collect(3, 0, low.astype(f32))
        return carry

    lax.fori_loop(0, rows // TALL, forward_body, 0)
    for gather in gathers:
        gather.drain()

    stages = (stage_q, wo, wu, wd)
    results = (gq_out, go_out, gu_out, gd_out)

    class Scatter:
        def __init__(self, item):
            index, first, columns = s.scatters[item]
            self.stage, self.result = stages[index], results[index]
            self.first, self.count, self.height = first, columns, s.weights[index][0]
            self.cols = pl.ds(first, columns)
            shared = item - len(s.scatters) + 3
            if shared >= 0:
                here = pl.ds(shared * self.height, self.height)
                self.rb0, self.rb1 = rb0[0].at[:, here], rb1[0].at[:, here]
            else:
                self.rb0, self.rb1 = rb0[item], rb1[item]
            self.zsrc, self.zr1, self.zr2 = zsrc[item], zr1[item], zr2[item]
            self.send, self.recv = r_send.at[item], r_recv.at[item]

        def start(self):
            self.across = remote(
                self.stage.at[pl.ds(0, chips), 1 - core, :, self.cols],
                self.rb0,
                self.send.at[0],
                self.recv.at[0],
                sibling,
            )
            self.across.start()

        def plane(self):
            self.across.wait_recv()

            def add(k, carry):
                here = (k, core, slice(None), self.cols)
                self.stage[here] = (
                    self.stage[here].astype(f32) + self.rb0[k].astype(f32)
                ).astype(bf16)
                return carry

            lax.fori_loop(0, chips, add, 0)
            self.sends = [
                remote(
                    self.stage.at[peer[0] // 2, core, :, self.cols],
                    self.rb1.at[k],
                    self.send.at[1 + k],
                    self.recv.at[1 + k],
                    peer,
                )
                for k, peer in enumerate(peers)
            ]
            for copy in self.sends:
                copy.start()

        def exchange(self, source, target, base, swap):
            half = self.count // 2
            partners = (z + 1 - 2 * parity, seq - 1 - z)
            copies = [
                remote(
                    source.at[:, k * half : (k + 1) * half],
                    target.at[:, k * half : (k + 1) * half],
                    self.send.at[base + k],
                    self.recv.at[base + k],
                    (me, partners[1 - k if swap else k]),
                )
                for k in range(2)
            ]
            for copy in copies:
                copy.start()
            return copies

        def along(self):
            for copy in self.sends:
                copy.wait_recv()
            total = self.stage[chip, core, :, self.cols].astype(f32)
            for k in range(nk):
                total = total + self.rb1[k].astype(f32)
            self.zsrc[...] = total.astype(bf16)
            self.first_pair = self.exchange(self.zsrc, self.zr1, nk + 1, False)

        def along_again(self):
            for copy in self.first_pair:
                copy.wait()
            self.zsrc[...] = (self.zsrc[...].astype(f32) + self.zr1[...].astype(f32)).astype(bf16)
            self.second_pair = self.exchange(self.zsrc, self.zr2, nk + 3, True)

        def finish(self):
            for copy in self.second_pair:
                copy.wait_recv()
            self.result[:, self.cols] = (
                self.zsrc[...].astype(f32) + self.zr2[...].astype(f32)
            ).astype(bf16)

        def drain(self):
            self.across.wait_send()
            for copy in self.sends + self.second_pair:
                copy.wait_send()

    scatters = [Scatter(item) for item in range(len(s.scatters))]
    down_item, up_item, out_item = scatters[:3]
    qkv_items = scatters[3:]

    def down_body(c, carry):
        per = chips * tile // hidden
        grad = tn(act[:, span(c, tile)], cot[...]).astype(bf16)
        wd[pl.ds(c * per, per)] = grad.reshape(per, 2, hidden // dp, width)
        return carry

    lax.fori_loop(0, hidden // tile, down_body, 0)
    down_item.start()

    bd_square = block_diag[:, :LANES].astype(bf16)
    head_sum = jnp.concatenate([bd_square, bd_square], axis=0)
    lane_hi = (lanes_of((CHUNK, LANES)) & 63) < 32

    def heads_body(c, carry):
        here = span(c, CHUNK)
        back = nt(gone[here, :], wo[...].reshape(width, width)).astype(bf16).astype(f32)
        for p in range(s.pairs):
            first = 2 * p * LANES
            result = acc[here, first : first + LANES]
            inverse = acc[here, first + LANES : first + 2 * LANES]
            grad = back[:, p * LANES : (p + 1) * LANES]
            dnum[here, p * LANES : (p + 1) * LANES] = (grad * inverse).astype(bf16)
            product = grad * result
            upper = product.astype(bf16)
            lower = (product - upper.astype(f32)).astype(bf16)
            total = nn(jnp.concatenate([upper, lower], axis=1), head_sum)
            value = total * inverse * (-1.0 / 32.0)
            upper = value.astype(bf16)
            lower = value - upper.astype(f32)
            act[here, 3 * width + p * LANES : 3 * width + (p + 1) * LANES] = jnp.where(
                lane_hi, upper.astype(f32), lower
            ).astype(bf16)
        return carry

    lax.fori_loop(0, s.chunks, heads_body, 0)

    def grads_of(here, p):
        first = 3 * width + p * LANES
        return dnum[here, p * LANES : (p + 1) * LANES], act[here, first : first + LANES]

    for p in range(s.pairs):
        state[p] = jnp.zeros((LANES, 2 * LANES), f32)

    def gstate_body(step, carry):
        c = s.chunks - 1 - step
        here = span(c, CHUNK)
        keep = same(ending(c), before(c))
        live = in_segment(c, before(c)).astype(bf16)
        for p in range(s.pairs):
            now = state[p]
            state_in[c, p] = now
            wide = jnp.concatenate(grads_of(here, p), axis=1)
            state[p] = keep * now + tn(cut(here, 0, p) * live, wide) * block_diag
        return carry

    lax.fori_loop(0, s.chunks, gstate_body, 0)
    send_states(1, False)
    down_item.plane()

    def up_body(c, carry):
        cols = span(c, tile)
        grad = nn(n2t[...], hgrad[:, :, :, cols].reshape(rows, tile)).astype(bf16)
        wu[:, :, :, cols] = grad.reshape(chips, 2, width // dp, tile)
        return carry

    lax.fori_loop(0, hidden // tile, up_body, 0)
    up_item.start()
    wo[...] = tn(heard[...], gone[...]).astype(bf16).reshape(chips, 2, width // dp, width)
    out_item.start()
    down_item.along()
    up_item.plane()
    out_item.plane()
    down_item.along_again()
    take_states(1, False)

    def back_body(c, carry):
        here = span(c, CHUNK)
        seen = mask[c]
        seen_t = seen.T
        live = in_segment(c, before(c))
        chosen = in_segment(c, ending(c))
        carried = same(ending(c), last)
        for p in range(s.pairs):
            q, k, v = cut(here, 0, p), cut(here, 1, p), cut(here, 2, p)
            dn, dd = grads_of(here, p)
            wide = jnp.concatenate([dn, dd], axis=1)
            k_low, k_high = k * ones_low, k * ones_high
            v_low = jnp.concatenate([v * ones_low, ones_low], axis=1)
            v_high = jnp.concatenate([v * ones_high, ones_high], axis=1)
            q_low, q_high = q * ones_low, q * ones_high
            dn_low, dn_high = dn * ones_low, dn * ones_high
            ahead = state_in[c, p] + carried * state[p]
            sums = ahead[:, LANES:]
            sums = 2.0 * spread_ends(sums + pltpu.roll(sums, 64, 1)) * block_diag[:, LANES:]
            upper = sums.astype(bf16).astype(f32)
            sums = jnp.where(low_half, upper, sums - upper)
            ahead = jnp.concatenate([ahead[:, :LANES], sums], axis=1).astype(bf16)
            ds_low = nt(wide, v_low).astype(bf16) * seen
            ds_high = nt(wide, v_high).astype(bf16) * seen
            gq = nn(ds_low, k_low) + nn(ds_high, k_high) + live * (
                nt(wide, state_b[c, p, :LANES]) + nt(wide, state_b[c, p, LANES:])
            )
            dst_low = nt(v_low, wide).astype(bf16) * seen_t
            dst_high = nt(v_high, wide).astype(bf16) * seen_t
            v_ones = jnp.concatenate([v, jnp.ones_like(v)], axis=1)
            gk = nn(dst_low, q_low) + nn(dst_high, q_high) + chosen * nt(v_ones, ahead)
            st_low = nt(k_low, q).astype(bf16) * seen_t
            st_high = nt(k_high, q).astype(bf16) * seen_t
            gv = nn(st_low, dn_low) + nn(st_high, dn_high) + chosen * nn(k, ahead[:, :LANES])
            for part, grad in ((0, gq), (1, gk), (2, gv)):
                grad = grad.astype(bf16)
                first = part * width + p * LANES
                if part < 2:
                    slope = jnp.minimum((q, k)[part].astype(f32), 1.0)
                    grad = (grad.astype(f32) * slope).astype(bf16)
                    collect(2, first, grad.astype(f32))
                act[here, first : first + LANES] = grad
        return carry

    lax.fori_loop(0, s.chunks, back_body, 0)
    down_item.finish()
    up_item.along()
    out_item.along()

    for part in range(3):
        cols = slice(part * width, (part + 1) * width)
        grad = nn(n1t[...], act[:, cols]).astype(bf16)
        stage_q[:chips, :, :, cols] = grad.reshape(chips, 2, width // dp, width)
        qkv_items[part].start()
    up_item.along_again()
    out_item.along_again()
    for item in qkv_items:
        item.plane()

    def input_body(c, carry):
        here = span(c, TALL)
        grad = nt(act[here, : 3 * width], wq[...].reshape(width, 3 * width))
        hat, scale = normalised(x_ref[here, :].astype(f32))
        collect(0, 0, grad * hat)
        collect(1, 0, grad)
        gmid[here, :] = gmid[here, :] + norm_back(grad, gain_one, hat, scale)
        pltpu.make_async_copy(gmid.at[here, :], gin_any.at[here, :], io_sem.at[2 + c]).start()
        return carry

    lax.fori_loop(0, rows // TALL, input_body, 0)

    for k, n in enumerate(s.sizes):
        table = one_hot(n)
        row = jnp.sum(vsum[:, starts[k] : starts[k] + n], axis=0, keepdims=True)
        spread = jnp.where(owner_mask(n), jnp.broadcast_to(row, (dp, n)), 0.0).astype(bf16)
        pieces = nt(spread, table)
        if pieces.shape[1] < s.vec_lanes:
            pad = jnp.zeros((dp, s.vec_lanes - pieces.shape[1]), f32)
            pieces = jnp.concatenate([pieces, pad], axis=1)
        vstage[:, k, :] = pieces
    vec_back = []
    for step in range(1, dp):
        target = lax.rem(me + step, dp)
        vec_back.append(
            remote(
                vstage.at[target],
                vback.at[step - 1],
                v_send.at[dp - 2 + step],
                v_recv.at[dp - 2 + step],
                (target, z),
            )
        )
        vec_back[-1].start()
    up_item.finish()
    out_item.finish()
    for item in qkv_items:
        item.along()
    for copy in vec_back:
        copy.wait_recv()
    total = vstage[me]
    for step in range(dp - 1):
        total = total + vback[step]
    vz[...] = total
    vec_z = []
    for step in range(1, seq):
        vec_z.append(
            remote(
                vz,
                vzback.at[step - 1],
                v_send.at[2 * dp - 3 + step],
                v_recv.at[2 * dp - 3 + step],
                (me, lax.rem(z + step, seq)),
            )
        )
        vec_z[-1].start()
    for item in qkv_items:
        item.along_again()
    for copy in vec_z:
        copy.wait_recv()
    terms = [vz[...]] + [vzback[step] for step in range(seq - 1)]
    while len(terms) > 1:
        half = len(terms) // 2
        terms = [terms[i] + terms[i + half] for i in range(half)]
    vec_out[...] = terms[0]
    for item in qkv_items:
        item.finish()

    for c in range(rows // TALL):
        here = pl.ds(c * TALL, TALL)
        pltpu.make_async_copy(gmid.at[here, :], gin_any.at[here, :], io_sem.at[2 + c]).wait()
    drain_states(0, True)
    drain_states(1, False)
    for copy in vec_sends + vec_back + vec_z:
        copy.wait_send()
    for item in scatters:
        item.drain()


def solution(mesh):
    def body(inputs, lengths, cotangent, *params):
        gain_one, shift_one, w_qkv, b_qk, w_out, b_out, gain_two, shift_two, w_up, b_up, w_down, b_down = params
        packs, rows, width = inputs.shape[1:]
        hidden = w_up.shape[1]
        s = Shape(mesh, rows, width, hidden)
        dp, seq, chips, pairs = s.dp, s.seq, s.chips, s.pairs
        nk = chips - 1
        vectors = (gain_one, shift_one, b_qk, b_out, gain_two, shift_two, b_up, b_down)
        vec = jnp.stack(
            [jnp.pad(v.astype(f32), (0, s.vec_lanes - v.shape[0])) for v in vectors]
        )
        vmem = pl.BlockSpec(memory_space=pltpu.VMEM)
        anywhere = pl.BlockSpec(memory_space=pl.ANY)
        grids = [(chips, 2) + shape for shape in s.weights]
        shapes = [(s.weights[index][0], columns) for index, _, columns in s.scatters]
        dma = pltpu.SemaphoreType.DMA
        tall = s.weights[0][0]
        scratch = (
            [pltpu.VMEM(grid, bf16) for grid in grids]
            + [
                pltpu.VMEM((rows, width), bf16),
                pltpu.VMEM((rows, width), bf16),
                pltpu.VMEM((width, rows), bf16),
                pltpu.VMEM((rows, 3 * width), bf16),
                pltpu.VMEM((rows, 2 * width), f32),
                pltpu.VMEM((s.chunks, CHUNK, CHUNK), bf16),
                pltpu.VMEM((s.chunks, pairs, LANES, 2 * LANES), f32),
                pltpu.VMEM((pairs, LANES, 2 * LANES), f32),
                pltpu.VMEM((s.chunks, pairs, 2 * LANES, 2 * LANES), bf16),
                pltpu.VMEM((width, rows), bf16),
                pltpu.VMEM((rows, hidden), bf16),
                pltpu.VMEM((rows // (2 * tall), 2, tall, hidden), bf16),
                pltpu.VMEM((rows, width), f32),
                pltpu.VMEM((rows, width), bf16),
                pltpu.VMEM((8, hidden), f32),
                pltpu.VMEM((dp, 8, s.vec_lanes), f32),
                pltpu.VMEM((8, sum(s.sizes)), f32),
                pltpu.VMEM((dp, 8, s.vec_lanes), f32),
                pltpu.VMEM((dp - 1, 8, s.vec_lanes), f32),
                pltpu.VMEM((8, s.vec_lanes), f32),
                pltpu.VMEM((seq - 1, 8, s.vec_lanes), f32),
                pltpu.VMEM((2, pairs // 2 + 1, LANES, LANES), bf16),
                pltpu.VMEM((2, seq - 1, pairs // 2 + 1, LANES, LANES), bf16),
                [pltpu.VMEM((chips,) + shape, bf16) for shape in shapes[:3]],
                [pltpu.VMEM((nk,) + shape, bf16) for shape in shapes[:3]],
                [pltpu.VMEM(shape, bf16) for shape in shapes],
                [pltpu.VMEM(shape, bf16) for shape in shapes],
                [pltpu.VMEM(shape, bf16) for shape in shapes],
                dma((len(s.gathers),)),
                dma((len(s.gathers), nk + 5)),
                dma((len(s.gathers), nk + 5)),
                dma((2 * dp - 2 + seq - 1,)),
                dma((2 * dp - 2 + seq - 1,)),
                dma((2, seq - 1)),
                dma((2, seq - 1)),
                dma((len(s.scatters), nk + 5)),
                dma((len(s.scatters), nk + 5)),
                dma((2 + rows // TALL,)),
            ]
        )
        outs = pl.pallas_call(
            functools.partial(kernel, s),
            out_shape=(
                jax.ShapeDtypeStruct((rows, width), bf16),
                jax.ShapeDtypeStruct((rows, width), f32),
            )
            + tuple(jax.ShapeDtypeStruct(shape, bf16) for shape in s.weights)
            + (jax.ShapeDtypeStruct((8, s.vec_lanes), f32),),
            in_specs=[pl.BlockSpec(memory_space=pltpu.SMEM), vmem, anywhere, vmem]
            + [anywhere] * 4,
            out_specs=(anywhere, anywhere) + (vmem,) * 5,
            scratch_shapes=scratch,
            compiler_params=pltpu.CompilerParams(
                collective_id=0, has_side_effects=True, vmem_limit_bytes=63 << 20
            ),
            name="layer",
        )(
            lengths.reshape(3),
            inputs.reshape(rows, width),
            cotangent.reshape(rows, width),
            vec,
            w_qkv,
            w_out,
            w_up,
            w_down,
        )
        out, gin, g_qkv, g_out, g_up, g_down, g_vec = outs
        pieces = [g_vec[k, : v.shape[0]] for k, v in enumerate(vectors)]
        return (
            out.reshape(inputs.shape),
            gin.reshape(inputs.shape),
            pieces[0],
            pieces[1],
            g_qkv.astype(f32),
            pieces[2],
            g_out.astype(f32),
            pieces[3],
            pieces[4],
            pieces[5],
            g_up.astype(f32),
            pieces[6],
            g_down.astype(f32),
            pieces[7],
        )

    rows_spec = P("dp", None, "seq", None)
    one, two = P("dp"), P("dp", None)
    params = (one, one, two, one, two, one, one, one, two, one, two, one)
    return jax.shard_map(
        body,
        mesh=mesh,
        in_specs=(rows_spec, P("dp", None, None), rows_spec) + params,
        out_specs=(rows_spec, rows_spec) + params,
        check_vma=False,
    )
```

```python
import functools

import jax
import jax.numpy as jnp
from jax import lax
from jax.experimental import pallas as pl
from jax.experimental.pallas import tpu as pltpu
from jax.sharding import PartitionSpec as P

HEADS = 8
CHUNK = 256
TALL = 640
LANES = 128
eps_norm = 1e-05
eps_attn = 1e-06
MESH = pl.DeviceIdType.MESH
f32 = jnp.float32
bf16 = jnp.bfloat16


def dot(a, b, ca, cb):
    return lax.dot_general(a, b, (((ca,), (cb,)), ((), ())), preferred_element_type=f32)


def nn(a, b):
    return dot(a, b, 1, 0)


def nt(a, b):
    return dot(a, b, 1, 1)


def tn(a, b):
    return dot(a, b, 0, 0)


def span(index, size):
    return pl.ds(pl.multiple_of(index * size, size), size)


def lanes_of(shape):
    return lax.broadcasted_iota(jnp.int32, shape, len(shape) - 1)


def rows_of(shape):
    return lax.broadcasted_iota(jnp.int32, shape, len(shape) - 2)


def fold_rows(values):
    rows, width = values.shape
    return jnp.sum(values.reshape(rows // 8, 8, width), axis=0)


def normalised(values):
    width = values.shape[-1]
    mean = jnp.sum(values, axis=-1, keepdims=True) * (1.0 / width)
    centred = values - mean
    variance = jnp.sum(centred * centred, axis=-1, keepdims=True) * (1.0 / width)
    scale = lax.rsqrt(variance + eps_norm)
    return centred * scale, scale


def norm_back(grad, gain, hat, scale):
    width = grad.shape[-1]
    a = grad * gain
    mean_a = jnp.sum(a, axis=-1, keepdims=True) * (1.0 / width)
    mean_ah = jnp.sum(a * hat, axis=-1, keepdims=True) * (1.0 / width)
    return (a - mean_a - hat * mean_ah) * scale


def gelu_pair(x):
    e = jnp.exp(x * x * -0.5)
    z = jnp.abs(x) * 0.7071067811865476
    t = 1.0 / (1.0 + 0.3275911 * z)
    poly = t * (
        0.254829592
        + t * (-0.284496736 + t * (1.421413741 + t * (-1.453152027 + t * 1.061405429)))
    )
    tail = 0.5 * poly * e
    cdf = jnp.where(x >= 0.0, 1.0 - tail, tail)
    return x * cdf, cdf + x * (0.3989422804014327 * e)


class Shape:
    def __init__(self, mesh, rows, width, hidden):
        self.dp = mesh.shape["dp"]
        self.seq = mesh.shape["seq"]
        self.chips = self.dp // 2
        self.side = max(k for k in range(1, self.chips + 1) if k * k <= self.chips and self.chips % k == 0)
        self.rows, self.width, self.hidden = rows, width, hidden
        self.chunks = rows // CHUNK
        self.pairs = width // LANES
        self.sizes = (width, width, 2 * width, width, width, width, hidden, width)
        self.vec_lanes = max(-(-n // self.dp // LANES) * LANES for n in self.sizes)
        w, h, d = width, hidden, self.dp
        self.weights = ((w // d, 3 * w), (w // d, w), (w // d, h), (h // d, w))
        self.gathers = (
            (0, 0, w),
            (0, w, w),
            (0, 2 * w, w),
            (3, 0, w),
            (1, 0, w),
        ) + tuple((2, t * (h // 4), h // 4) for t in range(4))
        self.scatters = (
            (3, 0, w),
            (2, 0, h),
            (1, 0, w),
            (0, 0, w),
            (0, w, w),
            (0, 2 * w, w),
        )


def kernel(
    s,
    lengths,
    x_ref,
    cot_any,
    vec_refs,
    wq_any,
    wo_any,
    wu_any,
    wd_any,
    out_any,
    gin_any,
    gq_out,
    go_out,
    gu_out,
    gd_out,
    vec_out,
    wq,
    wo,
    wu,
    wd,
    cot,
    n1,
    n1t,
    feat,
    acc,
    mask,
    state_in,
    state,
    state_b,
    n2t,
    act,
    hgrad,
    gmid,
    gone,
    vecs,
    vec_ref,
    vgot,
    vsum,
    vstage,
    vback,
    vz,
    vzback,
    msg,
    msg_in,
    rb0,
    rb1,
    zsrc,
    zr1,
    zr2,
    g_local,
    g_send,
    g_recv,
    v_send,
    v_recv,
    m_send,
    m_recv,
    r_send,
    r_recv,
    io_sem,
):
    dp, seq, chips, side = s.dp, s.seq, s.chips, s.side
    rows, width, hidden = s.rows, s.width, s.hidden
    me, z = lax.axis_index("dp"), lax.axis_index("seq")
    core, chip = lax.rem(me, 2), me // 2
    cy, cx = chip // side, lax.rem(chip, side)
    offsets = [(dy, dx) for dy in range(chips // side) for dx in range(side)][1:]

    def chip_at(dy, dx):
        ny = chips // side
        return lax.rem(cy + dy + ny, ny) * side + lax.rem(cx + dx + side, side)

    heard, dnum, stage_q = n1, cot, hgrad

    sibling = (chip * 2 + 1 - core, z)
    peers = [(chip_at(dy, dx) * 2 + core, z) for dy, dx in offsets]
    z_up, z_down = lax.rem(z + 1, seq), lax.rem(z + seq - 1, seq)

    def remote(src, dst, send, recv, device):
        return pltpu.make_async_remote_copy(
            src_ref=src,
            dst_ref=dst,
            send_sem=send,
            recv_sem=recv,
            device_id=device,
            device_id_type=MESH,
        )

    barrier = pltpu.get_barrier_semaphore()
    for step in range(1, dp):
        pl.semaphore_signal(
            barrier, inc=1, device_id=(lax.rem(me + step, dp), z), device_id_type=MESH
        )
    for step in range(1, seq):
        pl.semaphore_signal(
            barrier, inc=1, device_id=(me, lax.rem(z + step, seq)), device_id_type=MESH
        )
    pl.semaphore_wait(barrier, dp + seq - 2)

    vec_ref[...] = jnp.zeros_like(vec_ref)
    for k, ref in enumerate(vec_refs):
        lanes = ref.shape[1]
        for row in range(ref.shape[0]):
            vec_ref[k : k + 1, row * lanes : (row + 1) * lanes] = ref[row : row + 1, :].astype(f32)
    vec_sends = []
    for step in range(1, dp):
        vec_sends.append(
            remote(
                vec_ref,
                vgot.at[me],
                v_send.at[step - 1],
                v_recv.at[step - 1],
                (lax.rem(me + step, dp), z),
            )
        )
        vec_sends[-1].start()
    vgot[me] = vec_ref[...]

    sources = (wq_any, wo_any, wu_any, wd_any)
    weights = (wq, wo, wu, wd)
    nk = len(peers)

    class Gather:
        def __init__(self, item):
            index, first, columns = s.gathers[item]
            self.buffer, self.source = weights[index], sources[index]
            self.columns = pl.ds(first, columns)
            self.send, self.recv, self.local = g_send.at[item], g_recv.at[item], g_local.at[item]

        def start(self):
            src = self.source.at[:, self.columns]
            dst = self.buffer.at[chip, core, :, self.columns]
            self.own = pltpu.make_async_copy(src, dst, self.local)
            self.own.start()
            self.plane = [
                remote(src, dst, self.send.at[k], self.recv.at[k], peer)
                for k, peer in enumerate(peers)
            ]
            for copy in self.plane:
                copy.start()

        def hand_on(self):
            self.own.wait()
            for copy in self.plane:
                copy.wait_recv()
            mine = self.buffer.at[:, core, :, self.columns]
            self.across = remote(mine, mine, self.send.at[nk], self.recv.at[nk], sibling)
            self.across.start()

        def finish(self):
            theirs = self.buffer.at[:, 1 - core, :, self.columns]
            remote(theirs, theirs, self.send.at[nk], self.recv.at[nk], sibling).wait_recv()

        def drain(self):
            for copy in self.plane + [self.across]:
                copy.wait_send()

    gathers = [Gather(item) for item in range(len(s.gathers))]
    for item in range(3):
        gathers[item].start()
    cot_copy = pltpu.make_async_copy(cot_any, cot, io_sem.at[0])
    cot_copy.start()

    bound_0 = lengths[0]
    bound_1 = bound_0 + lengths[1]
    bound_2 = bound_1 + lengths[2]
    first_row = z * rows

    def segment(position):
        return sum((position >= bound).astype(jnp.int32) for bound in (bound_0, bound_1, bound_2))

    def same(a, b):
        return (a == b).astype(f32)

    prior = jnp.where(first_row > 0, segment(first_row - 1), -1)
    last = segment(first_row + rows - 1)

    def before(c):
        return jnp.where(first_row + c * CHUNK > 0, segment(first_row + c * CHUNK - 1), -1)

    def ending(c):
        return segment(first_row + (c + 1) * CHUNK - 1)

    def in_segment(c, which):
        shape = (CHUNK, LANES)
        return (segment(first_row + c * CHUNK + rows_of(shape)) == which).astype(f32)

    square = (CHUNK, CHUNK)
    pair = (LANES, LANES)
    lane_low = lanes_of((CHUNK, LANES)) < 64
    block_diag = (
        (lanes_of((LANES, 2 * LANES)) // 64) % 2 == rows_of((LANES, 2 * LANES)) // 64
    ).astype(f32)
    low_pair = lanes_of(pair) < 64
    low_half = (lanes_of(pair) & 63) < 32
    ones_low = lane_low.astype(bf16)
    ones_high = 1.0 - ones_low

    def mask_body(c, carry):
        down, across = rows_of(square), lanes_of(square)
        base = first_row + c * CHUNK
        alike = segment(base + down) == segment(base + across)
        mask[c] = (alike & (across <= down)).astype(f32).astype(bf16)
        return carry

    lax.fori_loop(0, s.chunks, mask_body, 0)

    for step in range(1, dp):
        source = lax.rem(me - step + dp, dp)
        remote(
            vec_ref, vgot.at[source], v_send.at[step - 1], v_recv.at[step - 1], (source, z)
        ).wait_recv()

    def one_hot(n):
        piece = n // dp
        tall = -(-piece // LANES) * LANES
        shape = (tall, n)
        return ((lanes_of(shape) & (piece - 1)) == rows_of(shape)).astype(f32).astype(bf16)

    def owner_mask(n):
        piece = n // dp
        shape = (dp, n)
        low = rows_of(shape) * piece
        return (lanes_of(shape) >= low) & (lanes_of(shape) < low + piece)

    for k, n in enumerate(s.sizes):
        table = one_hot(n)
        pieces = vgot[:, k, : table.shape[0]].astype(bf16)
        spread = jnp.where(owner_mask(n), nn(pieces, table), 0.0)
        vecs[k : k + 1, :n] = jnp.sum(spread, axis=0, keepdims=True)

    starts = [sum(s.sizes[:k]) for k in range(len(s.sizes))]

    def collect(k, first, values):
        at = starts[k] + first
        vsum[:, at : at + values.shape[1]] += fold_rows(values)

    gain_one, shift_one = vecs[0:1, :width], vecs[1:2, :width]
    for k, n in enumerate(s.sizes):
        vsum[:, starts[k] : starts[k] + n] = jnp.zeros((8, n), f32)

    def norm_body(c, carry):
        here = span(c, CHUNK)
        hat, _ = normalised(x_ref[here, :].astype(f32))
        normed = (hat * gain_one + shift_one).astype(bf16)
        n1[here, :] = normed
        n1t[:, here] = normed.T
        return carry

    lax.fori_loop(0, s.chunks, norm_body, 0)

    get_q, get_k, get_v, get_down, get_out = gathers[:5]
    get_up = gathers[5:]
    get_q.hand_on()
    get_down.start()
    get_k.hand_on()
    get_out.start()
    for item in range(3):
        if item == 1:
            get_v.hand_on()
            get_up[0].start()
        gathers[item].finish()
        weight = wq[:, :, :, item * width : (item + 1) * width].reshape(width, width)
        if item < 2:
            bias = vecs[2:3, item * width : (item + 1) * width]

        def project_body(c, carry):
            here = span(c, TALL)
            mixed = nn(n1[here, :], weight)
            if item < 2:
                mixed = mixed + bias
                mixed = jnp.where(mixed > 0.0, mixed + 1.0, jnp.exp(jnp.minimum(mixed, 0.0)))
            feat[here, item * width : (item + 1) * width] = mixed.astype(bf16)
            return carry

        lax.fori_loop(0, rows // TALL, project_body, 0)

    def cut(here, part, p):
        first = part * width + p * LANES
        return feat[here, first : first + LANES]

    for p in range(s.pairs):
        state[p] = jnp.zeros((LANES, 2 * LANES), f32)

    def state_at(c, p):
        first = pl.multiple_of(c * (s.pairs // 2 * LANES), LANES) + p // 2 * LANES
        return pl.ds(first, LANES), slice(p % 2 * 2 * LANES, (p % 2 + 1) * 2 * LANES)

    def state_body(c, carry):
        here = span(c, CHUNK)
        keep = same(ending(c), before(c))
        chosen = in_segment(c, ending(c)).astype(bf16)
        for p in range(s.pairs):
            wide = jnp.concatenate([cut(here, 2, p) * chosen, chosen], axis=1)
            now = state[p]
            state_in[state_at(c, p)] = now
            state[p] = keep * now + tn(cut(here, 1, p), wide) * block_diag
        return carry

    lax.fori_loop(0, s.chunks, state_body, 0)

    def spread_ends(right):
        return 0.5 * (right + pltpu.roll(right, 32, 1))

    def packed(slot):
        halves = []
        ends = []
        for p in range(s.pairs):
            left = state[p, :, :LANES]
            right = state[p, :, LANES:]
            halves.append(left + pltpu.roll(left, 64, 1))
            ends.append(spread_ends(right + pltpu.roll(right, 64, 1)))
        for q in range(s.pairs // 2):
            msg[slot, q] = jnp.where(low_pair, halves[2 * q], halves[2 * q + 1]).astype(bf16)
        total = ends[0]
        lanes = LANES // s.pairs
        for p in range(1, s.pairs):
            total = jnp.where(lanes_of(pair) // lanes == p, ends[p], total)
        upper = total.astype(bf16).astype(f32)
        total = jnp.where(lanes_of(pair) % lanes < lanes // 2, upper, total - upper)
        msg[slot, s.pairs // 2] = total.astype(bf16)

    def unpacked(slot, step, p):
        sums = msg_in[slot, step, p // 2].astype(f32)
        turned = pltpu.roll(sums, 64, 1)
        left = jnp.where(low_pair, sums, turned) if p % 2 == 0 else jnp.where(low_pair, turned, sums)
        first = p * (LANES // s.pairs)
        middle = first + LANES // s.pairs // 2
        ends = msg_in[slot, step, s.pairs // 2].astype(f32)
        right = ends[:, first : first + 1] + ends[:, middle : middle + 1]
        return jnp.concatenate([left, jnp.broadcast_to(right, pair)], axis=1) * block_diag

    def message(slot, step, forward):
        target = lax.rem(z + step, seq) if forward else lax.rem(z - step + seq, seq)
        return remote(
            msg.at[slot],
            msg_in.at[slot, step - 1],
            m_send.at[slot, step - 1],
            m_recv.at[slot, step - 1],
            (me, target),
        )

    def send_states(slot, forward):
        packed(slot)
        for step in range(1, seq):

            @pl.when((z + step < seq) if forward else (z - step >= 0))
            def _():
                message(slot, step, forward).start()

    def take_states(slot, forward):
        for p in range(s.pairs):
            state[p] = jnp.zeros((LANES, 2 * LANES), f32)
        for step in range(1, seq):

            @pl.when((z - step >= 0) if forward else (z + step < seq))
            def _():
                message(slot, step, forward).wait_recv()
                if forward:
                    weight = same(segment((z - step + 1) * rows - 1), prior)
                else:
                    weight = same(segment((z + step) * rows - 1), last)
                for p in range(s.pairs):
                    state[p] = state[p] + weight * unpacked(slot, step - 1, p)

    def drain_states(slot, forward):
        for step in range(1, seq):

            @pl.when((z + step < seq) if forward else (z - step >= 0))
            def _():
                message(slot, step, forward).wait_send()

    send_states(0, True)

    def inside_body(c, carry):
        here = span(c, CHUNK)
        seen = mask[c]
        for p in range(s.pairs):
            q, k, v = cut(here, 0, p), cut(here, 1, p), cut(here, 2, p)
            k_low, v_low = k * ones_low, v * ones_low
            k_high, v_high = k * ones_high, v * ones_high
            s_low = nt(q, k_low).astype(bf16) * seen
            s_high = nt(q, k_high).astype(bf16) * seen
            acc[here, 2 * p * LANES : (2 * p + 2) * LANES] = nn(
                s_low, jnp.concatenate([v_low, ones_low], axis=1)
            ) + nn(s_high, jnp.concatenate([v_high, ones_high], axis=1))
        return carry

    lax.fori_loop(0, s.chunks, inside_body, 0)
    get_down.hand_on()
    get_up[1].start()
    get_out.hand_on()
    get_up[2].start()
    get_down.finish()
    cot_copy.wait()

    tile = hidden // 4
    tall = s.weights[0][0]
    per = chips // 4
    blocks = TALL // (2 * tall)

    def hidden_body(c, carry):
        here = span(c, TALL)
        branch = cot[here, :]
        collect(7, 0, branch.astype(f32))
        for t in range(4):
            down = wd[t * per : (t + 1) * per].reshape(tile, width)
            grad = nt(branch, down).astype(bf16).reshape(blocks, 2, tall, tile)
            hgrad[span(c, blocks), :, :, t * tile : (t + 1) * tile] = grad
        return carry

    lax.fori_loop(0, rows // TALL, hidden_body, 0)
    get_up[0].hand_on()
    get_up[3].start()
    take_states(0, True)

    def join_body(c, carry):
        here = span(c, CHUNK)
        live = in_segment(c, before(c))
        carried = same(before(c), prior)
        for p in range(s.pairs):
            whole = state_in[state_at(c, p)] + carried * state[p]
            upper = whole.astype(bf16)
            lower = (whole - upper.astype(f32)).astype(bf16)
            state_b[c, p, :LANES] = upper
            state_b[c, p, LANES:] = lower
            q = cut(here, 0, p)
            extra = nn(jnp.concatenate([q, q], axis=1), state_b[c, p])
            first = 2 * p * LANES
            numerator = acc[here, first : first + LANES] + live * extra[:, :LANES]
            denominator = acc[here, first + LANES : first + 2 * LANES] + live * extra[:, LANES:]
            inverse = 1.0 / (denominator + eps_attn)
            result = numerator * inverse
            acc[here, first : first + LANES] = result
            acc[here, first + LANES : first + 2 * LANES] = inverse
            heard[here, p * LANES : (p + 1) * LANES] = result.astype(bf16)
        return carry

    lax.fori_loop(0, s.chunks, join_body, 0)
    get_out.finish()
    get_up[1].hand_on()

    bias_out, gain_two, shift_two = (vecs[k : k + 1, :width] for k in (3, 4, 5))
    bias_down = vecs[7:8, :width]
    total = state_in

    def middle_of(here):
        projected = nn(heard[here, :], wo[...].reshape(width, width))
        return x_ref[here, :].astype(f32) + projected + bias_out

    def middle_body(c, carry):
        here = span(c, TALL)
        middle = middle_of(here)
        hat, _ = normalised(middle)
        n2t[:, here] = (hat * gain_two + shift_two).astype(bf16).T
        total[here, :] = middle + bias_down
        return carry

    lax.fori_loop(0, rows // TALL, middle_body, 0)

    for t in range(4):
        if t == 1:
            get_up[2].hand_on()
        if t == 2:
            get_up[3].hand_on()
        get_up[t].finish()
        cols = slice(t * tile, (t + 1) * tile)

        def hidden_pass(c, carry):
            here = span(c, TALL)
            up = wu[:, :, :, cols].reshape(width, tile)
            down = wd[t * per : (t + 1) * per].reshape(tile, width)
            active, slope = gelu_pair(tn(n2t[:, here], up) + vecs[6:7, cols])
            active = active.astype(bf16)
            act[here, cols] = active
            there = (span(c, blocks), slice(None), slice(None), cols)
            grad = (slope * hgrad[there].reshape(TALL, tile).astype(f32)).astype(bf16)
            hgrad[there] = grad.reshape(blocks, 2, tall, tile)
            collect(6, t * tile, grad.astype(f32))
            total[here, :] += nn(active, down)
            back = nt(grad, up)
            gmid[here, :] = back if t == 0 else gmid[here, :] + back
            return carry

        lax.fori_loop(0, rows // TALL, hidden_pass, 0)

    def output_copy(c):
        here = span(c, TALL)
        return pltpu.make_async_copy(gone.at[here, :], out_any.at[here, :], io_sem.at[1 + c])

    def second_body(c, carry):
        here = span(c, TALL)
        gone[here, :] = total[here, :].astype(bf16)
        output_copy(c).start()
        hat, scale = normalised(middle_of(here))
        back = gmid[here, :]
        collect(4, 0, back * hat)
        collect(5, 0, back)
        gmid[here, :] = cot[here, :].astype(f32) + norm_back(back, gain_two, hat, scale)
        return carry

    lax.fori_loop(0, rows // TALL, second_body, 0)
    for gather in gathers:
        gather.drain()

    stages = (stage_q, wo, wu, wd)
    results = (gq_out, go_out, gu_out, gd_out)

    class Scatter:
        def __init__(self, item):
            index, first, columns = s.scatters[item]
            self.stage, self.result = stages[index], results[index]
            self.first, self.count, self.height = first, columns, s.weights[index][0]
            self.cols = pl.ds(first, columns)
            shared = item - len(s.scatters) + 3
            if shared >= 0:
                self.rb0 = rb0[0].at[:, pl.ds(shared * self.height, self.height)]
            else:
                self.rb0 = rb0[item]
            self.rb1 = rb1[item]
            self.zsrc, self.zr1, self.zr2 = zsrc[item], zr1[item], zr2[item]
            self.part = columns // seq
            self.send, self.recv = r_send.at[item], r_recv.at[item]

        def start(self):
            self.across = remote(
                self.stage.at[pl.ds(0, chips), 1 - core, :, self.cols],
                self.rb0,
                self.send.at[0],
                self.recv.at[0],
                sibling,
            )
            self.across.start()

        def plane(self):
            self.across.wait_recv()

            def add(k, carry):
                here = (k, core, slice(None), self.cols)
                self.stage[here] = (
                    self.stage[here].astype(f32) + self.rb0[k].astype(f32)
                ).astype(bf16)
                return carry

            lax.fori_loop(0, chips, add, 0)
            self.sends = [
                remote(
                    self.stage.at[peer[0] // 2, core, :, self.cols],
                    self.rb1.at[k],
                    self.send.at[1 + k],
                    self.recv.at[1 + k],
                    peer,
                )
                for k, peer in enumerate(peers)
            ]
            for copy in self.sends:
                copy.start()

        def along(self):
            for copy in self.sends:
                copy.wait_recv()
            total = self.stage[chip, core, :, self.cols].astype(f32)
            for k in range(nk):
                total = total + self.rb1[k].astype(f32)
            self.zsrc[...] = total.astype(bf16)
            self.first = []
            for step in range(1, seq):
                target = lax.rem(z + step, seq)
                copy = remote(
                    self.zsrc.at[:, span(target, self.part)],
                    self.zr1.at[step - 1],
                    self.send.at[nk + step],
                    self.recv.at[nk + step],
                    (me, target),
                )
                copy.start()
                self.first.append(copy)

        def along_again(self):
            for copy in self.first:
                copy.wait_recv()
            mine = span(z, self.part)
            total = self.zsrc[:, mine].astype(f32)
            for step in range(seq - 1):
                total = total + self.zr1[step].astype(f32)
            self.zr2[:, mine] = total.astype(bf16)
            self.second = []
            for step in range(1, seq):
                copy = remote(
                    self.zr2.at[:, mine],
                    self.zr2.at[:, mine],
                    self.send.at[nk + seq - 1 + step],
                    self.recv.at[nk + seq - 1 + step],
                    (me, lax.rem(z + step, seq)),
                )
                copy.start()
                self.second.append(copy)

        def finish(self):
            for step in range(1, seq):
                theirs = self.zr2.at[:, span(lax.rem(z - step + seq, seq), self.part)]
                remote(
                    theirs,
                    theirs,
                    self.send.at[nk + seq - 1 + step],
                    self.recv.at[nk + seq - 1 + step],
                    sibling,
                ).wait_recv()
            self.result[:, self.cols] = self.zr2[...]

        def drain(self):
            self.across.wait_send()
            for copy in self.sends + self.first + self.second:
                copy.wait_send()

    scatters = [Scatter(item) for item in range(len(s.scatters))]
    down_item, up_item, out_item = scatters[:3]
    qkv_items = scatters[3:]

    def down_body(c, carry):
        grad = tn(act[:, span(c, tile)], cot[...]).astype(bf16)
        wd[pl.ds(c * per, per)] = grad.reshape(per, 2, hidden // dp, width)
        return carry

    lax.fori_loop(0, hidden // tile, down_body, 0)
    down_item.start()

    bd_square = block_diag[:, :LANES].astype(bf16)
    head_sum = jnp.concatenate([bd_square, bd_square], axis=0)
    lane_hi = (lanes_of((CHUNK, LANES)) & 63) < 32

    def heads_body(c, carry):
        here = span(c, CHUNK)
        low = gmid[here, :].astype(bf16)
        gone[here, :] = low
        collect(3, 0, low.astype(f32))
        back = nt(low, wo[...].reshape(width, width)).astype(bf16).astype(f32)
        for p in range(s.pairs):
            first = 2 * p * LANES
            result = acc[here, first : first + LANES]
            inverse = acc[here, first + LANES : first + 2 * LANES]
            grad = back[:, p * LANES : (p + 1) * LANES]
            dnum[here, p * LANES : (p + 1) * LANES] = (grad * inverse).astype(bf16)
            product = grad * result
            upper = product.astype(bf16)
            lower = (product - upper.astype(f32)).astype(bf16)
            total = nn(jnp.concatenate([upper, lower], axis=1), head_sum)
            value = total * inverse * (-1.0 / 32.0)
            upper = value.astype(bf16)
            lower = value - upper.astype(f32)
            act[here, 3 * width + p * LANES : 3 * width + (p + 1) * LANES] = jnp.where(
                lane_hi, upper.astype(f32), lower
            ).astype(bf16)
        return carry

    for c in range(rows // TALL):
        output_copy(c).wait()
    lax.fori_loop(0, s.chunks, heads_body, 0)

    def grads_of(here, p):
        first = 3 * width + p * LANES
        return dnum[here, p * LANES : (p + 1) * LANES], act[here, first : first + LANES]

    for p in range(s.pairs):
        state[p] = jnp.zeros((LANES, 2 * LANES), f32)

    def gstate_body(step, carry):
        c = s.chunks - 1 - step
        here = span(c, CHUNK)
        keep = same(ending(c), before(c))
        live = in_segment(c, before(c)).astype(bf16)
        for p in range(s.pairs):
            now = state[p]
            state_in[state_at(c, p)] = now
            wide = jnp.concatenate(grads_of(here, p), axis=1)
            state[p] = keep * now + tn(cut(here, 0, p) * live, wide) * block_diag
        return carry

    lax.fori_loop(0, s.chunks, gstate_body, 0)
    send_states(1, False)
    down_item.plane()

    def up_body(c, carry):
        cols = span(c, tile)
        grad = nn(n2t[...], hgrad[:, :, :, cols].reshape(rows, tile)).astype(bf16)
        wu[:, :, :, cols] = grad.reshape(chips, 2, width // dp, tile)
        return carry

    lax.fori_loop(0, hidden // tile, up_body, 0)
    up_item.start()
    wo[...] = tn(heard[...], gone[...]).astype(bf16).reshape(chips, 2, width // dp, width)
    out_item.start()
    down_item.along()
    up_item.plane()
    out_item.plane()
    down_item.along_again()
    take_states(1, False)

    def back_body(c, carry):
        here = span(c, CHUNK)
        seen = mask[c]
        seen_t = seen.T
        live = in_segment(c, before(c))
        chosen = in_segment(c, ending(c))
        carried = same(ending(c), last)
        for p in range(s.pairs):
            q, k, v = cut(here, 0, p), cut(here, 1, p), cut(here, 2, p)
            dn, dd = grads_of(here, p)
            wide = jnp.concatenate([dn, dd], axis=1)
            k_low, k_high = k * ones_low, k * ones_high
            v_low = jnp.concatenate([v * ones_low, ones_low], axis=1)
            v_high = jnp.concatenate([v * ones_high, ones_high], axis=1)
            q_low, q_high = q * ones_low, q * ones_high
            dn_low, dn_high = dn * ones_low, dn * ones_high
            ahead = state_in[state_at(c, p)] + carried * state[p]
            sums = ahead[:, LANES:]
            sums = 2.0 * spread_ends(sums + pltpu.roll(sums, 64, 1)) * block_diag[:, LANES:]
            upper = sums.astype(bf16).astype(f32)
            sums = jnp.where(low_half, upper, sums - upper)
            ahead = jnp.concatenate([ahead[:, :LANES], sums], axis=1).astype(bf16)
            ds_low = nt(wide, v_low).astype(bf16) * seen
            ds_high = nt(wide, v_high).astype(bf16) * seen
            gq = nn(ds_low, k_low) + nn(ds_high, k_high) + live * (
                nt(wide, state_b[c, p, :LANES]) + nt(wide, state_b[c, p, LANES:])
            )
            dst_low = nt(v_low, wide).astype(bf16) * seen_t
            dst_high = nt(v_high, wide).astype(bf16) * seen_t
            v_ones = jnp.concatenate([v, jnp.ones_like(v)], axis=1)
            gk = nn(dst_low, q_low) + nn(dst_high, q_high) + chosen * nt(v_ones, ahead)
            st_low = nt(k_low, q).astype(bf16) * seen_t
            st_high = nt(k_high, q).astype(bf16) * seen_t
            gv = nn(st_low, dn_low) + nn(st_high, dn_high) + chosen * nn(k, ahead[:, :LANES])
            for part, grad in ((0, gq), (1, gk), (2, gv)):
                grad = grad.astype(bf16)
                first = part * width + p * LANES
                if part < 2:
                    slope = jnp.minimum((q, k)[part].astype(f32), 1.0)
                    grad = (grad.astype(f32) * slope).astype(bf16)
                    collect(2, first, grad.astype(f32))
                act[here, first : first + LANES] = grad
        return carry

    lax.fori_loop(0, s.chunks, back_body, 0)
    down_item.finish()
    up_item.along()
    out_item.along()

    for part in range(3):
        cols = slice(part * width, (part + 1) * width)
        grad = nn(n1t[...], act[:, cols]).astype(bf16)
        stage_q[:chips, :, :, cols] = grad.reshape(chips, 2, width // dp, width)
        qkv_items[part].start()
    up_item.along_again()
    out_item.along_again()
    for item in qkv_items:
        item.plane()

    def input_body(c, carry):
        here = span(c, TALL)
        grad = nt(act[here, : 3 * width], wq[...].reshape(width, 3 * width))
        hat, scale = normalised(x_ref[here, :].astype(f32))
        collect(0, 0, grad * hat)
        collect(1, 0, grad)
        gone[here, :] = (gmid[here, :] + norm_back(grad, gain_one, hat, scale)).astype(bf16)
        pltpu.make_async_copy(gone.at[here, :], gin_any.at[here, :], io_sem.at[1 + rows // TALL + c]).start()
        return carry

    lax.fori_loop(0, rows // TALL, input_body, 0)

    for k, n in enumerate(s.sizes):
        table = one_hot(n)
        row = jnp.sum(vsum[:, starts[k] : starts[k] + n], axis=0, keepdims=True)
        spread = jnp.where(owner_mask(n), jnp.broadcast_to(row, (dp, n)), 0.0).astype(bf16)
        pieces = nt(spread, table)
        if pieces.shape[1] < s.vec_lanes:
            pad = jnp.zeros((dp, s.vec_lanes - pieces.shape[1]), f32)
            pieces = jnp.concatenate([pieces, pad], axis=1)
        vstage[:, k, :] = pieces
    vec_back = []
    for step in range(1, dp):
        target = lax.rem(me + step, dp)
        vec_back.append(
            remote(
                vstage.at[target],
                vback.at[step - 1],
                v_send.at[dp - 2 + step],
                v_recv.at[dp - 2 + step],
                (target, z),
            )
        )
        vec_back[-1].start()
    up_item.finish()
    out_item.finish()
    for item in qkv_items:
        item.along()
    for copy in vec_back:
        copy.wait_recv()
    total = vstage[me]
    for step in range(dp - 1):
        total = total + vback[step]
    vz[...] = total
    vec_z = []
    for step in range(1, seq):
        vec_z.append(
            remote(
                vz,
                vzback.at[step - 1],
                v_send.at[2 * dp - 3 + step],
                v_recv.at[2 * dp - 3 + step],
                (me, lax.rem(z + step, seq)),
            )
        )
        vec_z[-1].start()
    for item in qkv_items:
        item.along_again()
    for copy in vec_z:
        copy.wait_recv()
    terms = [vz[...]] + [vzback[step] for step in range(seq - 1)]
    while len(terms) > 1:
        half = len(terms) // 2
        terms = [terms[i] + terms[i + half] for i in range(half)]
    vec_out[...] = terms[0]
    for item in qkv_items:
        item.finish()

    for c in range(rows // TALL):
        here = pl.ds(c * TALL, TALL)
        pltpu.make_async_copy(gone.at[here, :], gin_any.at[here, :], io_sem.at[1 + rows // TALL + c]).wait()
    drain_states(0, True)
    drain_states(1, False)
    for copy in vec_sends + vec_back + vec_z:
        copy.wait_send()
    for item in scatters:
        item.drain()


def widen_kernel(parts, *refs):
    count = 7
    ins, outs = refs[:count], refs[count : count + 14]
    got, made, in_sem, out_sem = refs[count + 14 :]
    out_in, gin_in, *grads_in, vec_in = ins
    out_out, gin_out, *rest = outs
    rows = out_in.shape[0] // parts
    here = [pl.ds(k * rows, rows) for k in range(parts)]
    loads = [
        [pltpu.make_async_copy(source.at[at], got.at[i, at], in_sem.at[i, k]) for k, at in enumerate(here)]
        for i, source in enumerate((gin_in, out_in))
    ]
    for copy in loads[0] + loads[1]:
        copy.start()
    stores = []
    for k, at in enumerate(here):
        loads[0][k].wait()
        made[at] = got[0, at].astype(f32)
        stores.append(pltpu.make_async_copy(made.at[at], gin_out.at[at], out_sem.at[0, k]))
        stores[-1].start()
    for k, at in enumerate(here):
        loads[1][k].wait()
        stores.append(pltpu.make_async_copy(got.at[1, at], out_out.at[at], out_sem.at[1, k]))
        stores[-1].start()
    for grad, result in zip(grads_in, rest[:4]):
        result[...] = grad[...].astype(f32)
    for k, result in enumerate(rest[4:]):
        result[...] = vec_in[k : k + 1, : result.shape[1]]
    for copy in stores:
        copy.wait()


def widen(s, vectors, results):
    parts = 4
    out, gin, *grads, vec = results
    vmem = pl.BlockSpec(memory_space=pltpu.VMEM)
    anywhere = pl.BlockSpec(memory_space=pl.ANY)
    return pl.pallas_call(
        functools.partial(widen_kernel, parts),
        out_shape=[jax.ShapeDtypeStruct(out.shape, bf16)]
        + [jax.ShapeDtypeStruct(value.shape, f32) for value in (gin, *grads)]
        + [jax.ShapeDtypeStruct((1, v.shape[0]), f32) for v in vectors],
        in_specs=[anywhere] * 2 + [vmem] * 5,
        out_specs=[anywhere] * 2 + [vmem] * 12,
        scratch_shapes=[
            pltpu.VMEM((2,) + out.shape, bf16),
            pltpu.VMEM(out.shape, f32),
            pltpu.SemaphoreType.DMA((2, parts)),
            pltpu.SemaphoreType.DMA((2, parts)),
        ],
        compiler_params=pltpu.CompilerParams(vmem_limit_bytes=63 << 20),
        name="widen",
    )(out, gin, *grads, vec)


def solution(mesh):
    def body(inputs, lengths, cotangent, *params):
        gain_one, shift_one, w_qkv, b_qk, w_out, b_out, gain_two, shift_two, w_up, b_up, w_down, b_down = params
        packs, rows, width = inputs.shape[1:]
        hidden = w_up.shape[1]
        s = Shape(mesh, rows, width, hidden)
        dp, seq, chips, pairs = s.dp, s.seq, s.chips, s.pairs
        nk = chips - 1
        vectors = (gain_one, shift_one, b_qk, b_out, gain_two, shift_two, b_up, b_down)
        vmem = pl.BlockSpec(memory_space=pltpu.VMEM)
        anywhere = pl.BlockSpec(memory_space=pl.ANY)
        grids = [(chips, 2) + shape for shape in s.weights]
        shapes = [(s.weights[index][0], columns) for index, _, columns in s.scatters]
        dma = pltpu.SemaphoreType.DMA
        tall = s.weights[0][0]
        scratch = (
            [pltpu.VMEM(grid, bf16) for grid in grids]
            + [
                pltpu.VMEM((rows, width), bf16),
                pltpu.VMEM((rows, width), bf16),
                pltpu.VMEM((width, rows), bf16),
                pltpu.VMEM((rows, 3 * width), bf16),
                pltpu.VMEM((rows, 2 * width), f32),
                pltpu.VMEM((s.chunks, CHUNK, CHUNK), bf16),
                pltpu.VMEM((rows, width), f32),
                pltpu.VMEM((pairs, LANES, 2 * LANES), f32),
                pltpu.VMEM((s.chunks, pairs, 2 * LANES, 2 * LANES), bf16),
                pltpu.VMEM((width, rows), bf16),
                pltpu.VMEM((rows, hidden), bf16),
                pltpu.VMEM((rows // (2 * tall), 2, tall, hidden), bf16),
                pltpu.VMEM((rows, width), f32),
                pltpu.VMEM((rows, width), bf16),
                pltpu.VMEM((8, hidden), f32),
                pltpu.VMEM((8, s.vec_lanes), f32),
                pltpu.VMEM((dp, 8, s.vec_lanes), f32),
                pltpu.VMEM((8, sum(s.sizes)), f32),
                pltpu.VMEM((dp, 8, s.vec_lanes), f32),
                pltpu.VMEM((dp - 1, 8, s.vec_lanes), f32),
                pltpu.VMEM((8, s.vec_lanes), f32),
                pltpu.VMEM((seq - 1, 8, s.vec_lanes), f32),
                pltpu.VMEM((2, pairs // 2 + 1, LANES, LANES), bf16),
                pltpu.VMEM((2, seq - 1, pairs // 2 + 1, LANES, LANES), bf16),
                [pltpu.VMEM((chips,) + shape, bf16) for shape in shapes[:3]],
                [pltpu.VMEM((nk,) + shape, bf16) for shape in shapes],
                [pltpu.VMEM(shape, bf16) for shape in shapes],
                [pltpu.VMEM((seq - 1, tall_, n // seq), bf16) for tall_, n in shapes],
                [pltpu.VMEM(shape, bf16) for shape in shapes],
                dma((len(s.gathers),)),
                dma((len(s.gathers), nk + 1)),
                dma((len(s.gathers), nk + 1)),
                dma((2 * dp - 2 + seq - 1,)),
                dma((2 * dp - 2 + seq - 1,)),
                dma((2, seq - 1)),
                dma((2, seq - 1)),
                dma((len(s.scatters), nk + 2 * seq - 1)),
                dma((len(s.scatters), nk + 2 * seq - 1)),
                dma((1 + 2 * (rows // TALL),)),
            ]
        )
        outs = pl.pallas_call(
            functools.partial(kernel, s),
            out_shape=(
                jax.ShapeDtypeStruct((rows, width), bf16),
                jax.ShapeDtypeStruct((rows, width), bf16),
            )
            + tuple(jax.ShapeDtypeStruct(shape, bf16) for shape in s.weights)
            + (jax.ShapeDtypeStruct((8, s.vec_lanes), f32),),
            in_specs=[pl.BlockSpec(memory_space=pltpu.SMEM), vmem, anywhere, [vmem] * 8]
            + [anywhere] * 4,
            out_specs=(anywhere, anywhere) + (vmem,) * 5,
            scratch_shapes=scratch,
            compiler_params=pltpu.CompilerParams(
                collective_id=0, has_side_effects=True, vmem_limit_bytes=63 << 20
            ),
            name="layer",
        )(
            lengths.reshape(3),
            inputs.reshape(rows, width),
            cotangent.reshape(rows, width),
            [v.reshape(-1, min(v.shape[0], LANES)) for v in vectors],
            w_qkv,
            w_out,
            w_up,
            w_down,
        )
        out, gin, *grads = widen(s, vectors, outs)
        g_qkv, g_out, g_up, g_down, *pieces = grads
        pieces = [piece.reshape(piece.shape[1]) for piece in pieces]
        return (
            out.reshape(inputs.shape),
            gin.reshape(inputs.shape),
            pieces[0],
            pieces[1],
            g_qkv,
            pieces[2],
            g_out,
            pieces[3],
            pieces[4],
            pieces[5],
            g_up,
            pieces[6],
            g_down,
            pieces[7],
        )

    rows_spec = P("dp", None, "seq", None)
    one, two = P("dp"), P("dp", None)
    params = (one, one, two, one, two, one, one, one, two, one, two, one)
    return jax.shard_map(
        body,
        mesh=mesh,
        in_specs=(rows_spec, P("dp", None, None), rows_spec) + params,
        out_specs=(rows_spec, rows_spec) + params,
        check_vma=False,
    )
```

```python
import functools

import jax
import jax.numpy as jnp
from jax import lax
from jax.experimental import pallas as pl
from jax.experimental.pallas import tpu as pltpu
from jax.sharding import PartitionSpec as P

HEADS = 8
CHUNK = 256
TALL = 640
LANES = 128
eps_norm = 1e-05
eps_attn = 1e-06
MESH = pl.DeviceIdType.MESH
f32 = jnp.float32
bf16 = jnp.bfloat16


def dot(a, b, ca, cb):
    return lax.dot_general(a, b, (((ca,), (cb,)), ((), ())), preferred_element_type=f32)


def nn(a, b):
    return dot(a, b, 1, 0)


def nt(a, b):
    return dot(a, b, 1, 1)


def tn(a, b):
    return dot(a, b, 0, 0)


def span(index, size):
    return pl.ds(pl.multiple_of(index * size, size), size)


def lanes_of(shape):
    return lax.broadcasted_iota(jnp.int32, shape, len(shape) - 1)


def rows_of(shape):
    return lax.broadcasted_iota(jnp.int32, shape, len(shape) - 2)


def fold_rows(values):
    rows, width = values.shape
    return jnp.sum(values.reshape(rows // 8, 8, width), axis=0)


def normalised(values):
    width = values.shape[-1]
    mean = jnp.sum(values, axis=-1, keepdims=True) * (1.0 / width)
    centred = values - mean
    variance = jnp.sum(centred * centred, axis=-1, keepdims=True) * (1.0 / width)
    scale = lax.rsqrt(variance + eps_norm)
    return centred * scale, scale


def norm_back(grad, gain, hat, scale):
    width = grad.shape[-1]
    a = grad * gain
    mean_a = jnp.sum(a, axis=-1, keepdims=True) * (1.0 / width)
    mean_ah = jnp.sum(a * hat, axis=-1, keepdims=True) * (1.0 / width)
    return (a - mean_a - hat * mean_ah) * scale


def gelu_pair(x):
    cdf = 0.5 + 0.5 * lax.erf(x * 0.7071067811865476)
    return x * cdf, cdf + x * (0.3989422804014327 * jnp.exp2(x * x * -0.7213475204444817))


class Shape:
    def __init__(self, mesh, rows, width, hidden):
        self.dp = mesh.shape["dp"]
        self.seq = mesh.shape["seq"]
        self.chips = self.dp // 2
        self.side = max(k for k in range(1, self.chips + 1) if k * k <= self.chips and self.chips % k == 0)
        self.rows, self.width, self.hidden = rows, width, hidden
        self.chunks = rows // CHUNK
        self.pairs = width // LANES
        self.sizes = (width, width, 2 * width, width, width, width, hidden, width)
        self.vec_lanes = max(-(-n // self.dp // LANES) * LANES for n in self.sizes)
        w, h, d = width, hidden, self.dp
        self.weights = ((w // d, 3 * w), (w // d, w), (w // d, h), (h // d, w))
        self.gathers = (
            (0, w, w),
            (0, 2 * w, w),
            (0, 0, w),
            (3, 0, w),
            (1, 0, w),
        ) + tuple((2, t * (h // 4), h // 4) for t in range(4))
        self.scatters = (
            (3, 0, w),
            (2, 0, h),
            (1, 0, w),
            (0, 0, w),
            (0, w, w),
            (0, 2 * w, w),
        )


def kernel(
    s,
    lengths,
    x_ref,
    cot_any,
    vec_refs,
    wq_any,
    wo_any,
    wu_any,
    wd_any,
    out_any,
    gin_any,
    gq_out,
    go_out,
    gu_out,
    gd_out,
    vec_out,
    wq,
    wo,
    wu,
    wd,
    cot,
    n1,
    n1t,
    feat,
    acc,
    mask,
    state_in,
    state,
    state_b,
    n2t,
    act,
    hgrad,
    gmid,
    gone,
    vecs,
    vec_ref,
    vgot,
    vsum,
    vstage,
    vback,
    vz,
    vzback,
    msg,
    msg_in,
    rb0,
    rb1,
    zsrc,
    zr1,
    zr2,
    g_local,
    g_send,
    g_recv,
    v_send,
    v_recv,
    m_send,
    m_recv,
    r_send,
    r_recv,
    io_sem,
):
    dp, seq, chips, side = s.dp, s.seq, s.chips, s.side
    rows, width, hidden = s.rows, s.width, s.hidden
    me, z = lax.axis_index("dp"), lax.axis_index("seq")
    core, chip = lax.rem(me, 2), me // 2
    cy, cx = chip // side, lax.rem(chip, side)
    offsets = [(dy, dx) for dy in range(chips // side) for dx in range(side)][1:]

    def chip_at(dy, dx):
        ny = chips // side
        return lax.rem(cy + dy + ny, ny) * side + lax.rem(cx + dx + side, side)

    heard, dnum, stage_q = n1, cot, hgrad

    sibling = (chip * 2 + 1 - core, z)
    peers = [(chip_at(dy, dx) * 2 + core, z) for dy, dx in offsets]
    z_up, z_down = lax.rem(z + 1, seq), lax.rem(z + seq - 1, seq)

    def remote(src, dst, send, recv, device):
        return pltpu.make_async_remote_copy(
            src_ref=src,
            dst_ref=dst,
            send_sem=send,
            recv_sem=recv,
            device_id=device,
            device_id_type=MESH,
        )

    barrier = pltpu.get_barrier_semaphore()
    for step in range(1, dp):
        pl.semaphore_signal(
            barrier, inc=1, device_id=(lax.rem(me + step, dp), z), device_id_type=MESH
        )
    for step in range(1, seq):
        pl.semaphore_signal(
            barrier, inc=1, device_id=(me, lax.rem(z + step, seq)), device_id_type=MESH
        )
    pl.semaphore_wait(barrier, dp + seq - 2)

    vec_ref[...] = jnp.zeros_like(vec_ref)
    for k, ref in enumerate(vec_refs):
        lanes = ref.shape[1]
        for row in range(ref.shape[0]):
            vec_ref[k : k + 1, row * lanes : (row + 1) * lanes] = ref[row : row + 1, :].astype(f32)
    vec_sends = []
    for step in range(1, dp):
        vec_sends.append(
            remote(
                vec_ref,
                vgot.at[me],
                v_send.at[step - 1],
                v_recv.at[step - 1],
                (lax.rem(me + step, dp), z),
            )
        )
        vec_sends[-1].start()
    vgot[me] = vec_ref[...]

    sources = (wq_any, wo_any, wu_any, wd_any)
    weights = (wq, wo, wu, wd)
    nk = len(peers)

    class Gather:
        def __init__(self, item):
            index, first, columns = s.gathers[item]
            self.buffer, self.source = weights[index], sources[index]
            self.columns = pl.ds(first, columns)
            self.send, self.recv, self.local = g_send.at[item], g_recv.at[item], g_local.at[item]

        def start(self):
            src = self.source.at[:, self.columns]
            dst = self.buffer.at[chip, core, :, self.columns]
            self.own = pltpu.make_async_copy(src, dst, self.local)
            self.own.start()
            self.plane = [
                remote(src, dst, self.send.at[k], self.recv.at[k], peer)
                for k, peer in enumerate(peers)
            ]
            for copy in self.plane:
                copy.start()

        def hand_on(self):
            self.own.wait()
            for copy in self.plane:
                copy.wait_recv()
            mine = self.buffer.at[:, core, :, self.columns]
            self.across = remote(mine, mine, self.send.at[nk], self.recv.at[nk], sibling)
            self.across.start()

        def finish(self):
            theirs = self.buffer.at[:, 1 - core, :, self.columns]
            remote(theirs, theirs, self.send.at[nk], self.recv.at[nk], sibling).wait_recv()

        def drain(self):
            for copy in self.plane + [self.across]:
                copy.wait_send()

    gathers = [Gather(item) for item in range(len(s.gathers))]
    for item in range(3):
        gathers[item].start()
    cot_copy = pltpu.make_async_copy(cot_any, cot, io_sem.at[0])
    cot_copy.start()

    bound_0 = lengths[0]
    bound_1 = bound_0 + lengths[1]
    bound_2 = bound_1 + lengths[2]
    first_row = z * rows

    def segment(position):
        return sum((position >= bound).astype(jnp.int32) for bound in (bound_0, bound_1, bound_2))

    def same(a, b):
        return (a == b).astype(f32)

    prior = jnp.where(first_row > 0, segment(first_row - 1), -1)
    last = segment(first_row + rows - 1)

    def before(c):
        return jnp.where(first_row + c * CHUNK > 0, segment(first_row + c * CHUNK - 1), -1)

    def ending(c):
        return segment(first_row + (c + 1) * CHUNK - 1)

    def in_segment(c, which):
        shape = (CHUNK, LANES)
        return (segment(first_row + c * CHUNK + rows_of(shape)) == which).astype(f32)

    square = (CHUNK, CHUNK)
    pair = (LANES, LANES)
    lane_low = lanes_of((CHUNK, LANES)) < 64
    block_diag = (
        (lanes_of((LANES, 2 * LANES)) // 64) % 2 == rows_of((LANES, 2 * LANES)) // 64
    ).astype(f32)
    low_pair = lanes_of(pair) < 64
    diagonal = lanes_of(pair) == rows_of(pair)
    low_half = (lanes_of(pair) & 63) < 32
    ones_low = lane_low.astype(bf16)
    ones_high = 1.0 - ones_low

    def mask_body(c, carry):
        down, across = rows_of(square), lanes_of(square)
        base = first_row + c * CHUNK
        alike = segment(base + down) == segment(base + across)
        mask[c] = (alike & (across <= down)).astype(f32).astype(bf16)
        return carry

    lax.fori_loop(0, s.chunks, mask_body, 0)

    for step in range(1, dp):
        source = lax.rem(me - step + dp, dp)
        remote(
            vec_ref, vgot.at[source], v_send.at[step - 1], v_recv.at[step - 1], (source, z)
        ).wait_recv()

    def one_hot(n):
        piece = n // dp
        tall = -(-piece // LANES) * LANES
        shape = (tall, n)
        return ((lanes_of(shape) & (piece - 1)) == rows_of(shape)).astype(f32).astype(bf16)

    def owner_mask(n):
        piece = n // dp
        shape = (dp, n)
        low = rows_of(shape) * piece
        return (lanes_of(shape) >= low) & (lanes_of(shape) < low + piece)

    for k, n in enumerate(s.sizes):
        table = one_hot(n)
        pieces = vgot[:, k, : table.shape[0]].astype(bf16)
        spread = jnp.where(owner_mask(n), nn(pieces, table), 0.0)
        vecs[k : k + 1, :n] = jnp.sum(spread, axis=0, keepdims=True)

    starts = [sum(s.sizes[:k]) for k in range(len(s.sizes))]

    def collect(k, first, values):
        at = starts[k] + first
        vsum[:, at : at + values.shape[1]] += fold_rows(values)

    gain_one, shift_one = vecs[0:1, :width], vecs[1:2, :width]
    for k, n in enumerate(s.sizes):
        vsum[:, starts[k] : starts[k] + n] = jnp.zeros((8, n), f32)

    def norm_body(c, carry):
        here = span(c, CHUNK)
        hat, _ = normalised(x_ref[here, :].astype(f32))
        normed = (hat * gain_one + shift_one).astype(bf16)
        n1[here, :] = normed
        n1t[:, here] = normed.T
        return carry

    lax.fori_loop(0, s.chunks, norm_body, 0)

    get_down, get_out = gathers[3:5]
    get_up = gathers[5:]

    def project(get, part):
        get.finish()
        cols = slice(part * width, (part + 1) * width)
        weight = wq[:, :, :, cols].reshape(width, width)

        def project_body(c, carry):
            here = span(c, TALL)
            mixed = nn(n1[here, :], weight)
            if part < 2:
                mixed = mixed + vecs[2:3, cols]
                mixed = jnp.where(mixed > 0.0, mixed + 1.0, jnp.exp(jnp.minimum(mixed, 0.0)))
            feat[here, cols] = mixed.astype(bf16)
            return carry

        lax.fori_loop(0, rows // TALL, project_body, 0)

    gathers[0].hand_on()
    get_down.start()
    gathers[1].hand_on()
    get_out.start()
    project(gathers[0], 1)
    project(gathers[1], 2)

    def cut(here, part, p):
        first = part * width + p * LANES
        return feat[here, first : first + LANES]

    for p in range(s.pairs):
        state[p] = jnp.zeros((LANES, 2 * LANES), f32)

    def state_at(c, p):
        first = pl.multiple_of(c * (s.pairs // 2 * LANES), LANES) + p // 2 * LANES
        return pl.ds(first, LANES), slice(p % 2 * 2 * LANES, (p % 2 + 1) * 2 * LANES)

    def state_body(c, carry):
        here = span(c, CHUNK)
        keep = same(ending(c), before(c))
        chosen = in_segment(c, ending(c)).astype(bf16)
        for p in range(s.pairs):
            wide = jnp.concatenate([cut(here, 2, p) * chosen, chosen], axis=1)
            now = state[p]
            state_in[state_at(c, p)] = now
            state[p] = keep * now + tn(cut(here, 1, p), wide) * block_diag
        return carry

    lax.fori_loop(0, s.chunks, state_body, 0)

    def spread_ends(right):
        return 0.5 * (right + pltpu.roll(right, 32, 1))

    def packed(slot):
        halves = []
        ends = []
        for p in range(s.pairs):
            left = state[p, :, :LANES]
            right = state[p, :, LANES:]
            halves.append(left + pltpu.roll(left, 64, 1))
            ends.append(spread_ends(right + pltpu.roll(right, 64, 1)))
        for q in range(s.pairs // 2):
            msg[slot, q * LANES : (q + 1) * LANES] = jnp.where(
                low_pair, halves[2 * q], halves[2 * q + 1]
            )
        ends = [jnp.sum(jnp.where(diagonal, end, 0.0), axis=0, keepdims=True) for end in ends]
        ends.append(jnp.zeros((msg.shape[1] - s.pairs // 2 * LANES - s.pairs, LANES), f32))
        msg[slot, s.pairs // 2 * LANES :] = jnp.concatenate(ends, axis=0)

    def unpacked(slot, step, p):
        sums = msg_in[slot, step, p // 2 * LANES : (p // 2 + 1) * LANES]
        turned = pltpu.roll(sums, 64, 1)
        left = jnp.where(low_pair, sums, turned) if p % 2 == 0 else jnp.where(low_pair, turned, sums)
        first = s.pairs // 2 * LANES + p
        ends = jnp.where(diagonal, msg_in[slot, step, first : first + 1], 0.0)
        right = jnp.sum(ends, axis=1, keepdims=True)
        return jnp.concatenate([left, jnp.broadcast_to(right, pair)], axis=1) * block_diag

    def message(slot, step, forward):
        target = lax.rem(z + step, seq) if forward else lax.rem(z - step + seq, seq)
        return remote(
            msg.at[slot],
            msg_in.at[slot, step - 1],
            m_send.at[slot, step - 1],
            m_recv.at[slot, step - 1],
            (me, target),
        )

    def send_states(slot, forward):
        packed(slot)
        for step in range(1, seq):

            @pl.when((z + step < seq) if forward else (z - step >= 0))
            def _():
                message(slot, step, forward).start()

    def take_states(slot, forward):
        for p in range(s.pairs):
            state[p] = jnp.zeros((LANES, 2 * LANES), f32)
        for step in range(1, seq):

            @pl.when((z - step >= 0) if forward else (z + step < seq))
            def _():
                message(slot, step, forward).wait_recv()
                if forward:
                    weight = same(segment((z - step + 1) * rows - 1), prior)
                else:
                    weight = same(segment((z + step) * rows - 1), last)
                for p in range(s.pairs):
                    state[p] = state[p] + weight * unpacked(slot, step - 1, p)

    def drain_states(slot, forward):
        for step in range(1, seq):

            @pl.when((z + step < seq) if forward else (z - step >= 0))
            def _():
                message(slot, step, forward).wait_send()

    send_states(0, True)
    gathers[2].hand_on()
    get_up[0].start()
    project(gathers[2], 0)

    def inside_body(c, carry):
        here = span(c, CHUNK)
        seen = mask[c]
        raw = []
        for p in range(s.pairs):
            q, k = cut(here, 0, p), cut(here, 1, p)
            raw.append((nt(q, k * ones_low), nt(q, k * ones_high)))
        for p in range(s.pairs):
            v = cut(here, 2, p)
            scores = jnp.concatenate([part.astype(bf16) * seen for part in raw[p]], axis=1)
            low = jnp.concatenate([v * ones_low, ones_low], axis=1)
            high = jnp.concatenate([v * ones_high, ones_high], axis=1)
            acc[here, 2 * p * LANES : (2 * p + 2) * LANES] = nn(
                scores, jnp.concatenate([low, high], axis=0)
            )
        return carry

    lax.fori_loop(0, s.chunks, inside_body, 0)
    get_down.hand_on()
    get_up[1].start()
    get_out.hand_on()
    get_up[2].start()
    get_down.finish()
    cot_copy.wait()

    tile = hidden // 4
    tall = s.weights[0][0]
    per = chips // 4
    blocks = TALL // (2 * tall)

    def hidden_body(c, carry):
        here = span(c, TALL)
        branch = cot[here, :]
        collect(7, 0, branch.astype(f32))
        for t in range(4):
            down = wd[t * per : (t + 1) * per].reshape(tile, width)
            grad = nt(branch, down).astype(bf16).reshape(blocks, 2, tall, tile)
            hgrad[span(c, blocks), :, :, t * tile : (t + 1) * tile] = grad
        return carry

    lax.fori_loop(0, rows // TALL, hidden_body, 0)
    get_up[0].hand_on()
    get_up[3].start()
    take_states(0, True)

    def join_body(c, carry):
        here = span(c, CHUNK)
        live = in_segment(c, before(c))
        carried = same(before(c), prior)
        for p in range(s.pairs):
            whole = state_in[state_at(c, p)] + carried * state[p]
            upper = whole.astype(bf16)
            lower = (whole - upper.astype(f32)).astype(bf16)
            state_b[c, p, :LANES] = upper
            state_b[c, p, LANES:] = lower
            q = cut(here, 0, p)
            extra = nn(jnp.concatenate([q, q], axis=1), state_b[c, p])
            first = 2 * p * LANES
            numerator = acc[here, first : first + LANES] + live * extra[:, :LANES]
            denominator = acc[here, first + LANES : first + 2 * LANES] + live * extra[:, LANES:]
            inverse = 1.0 / (denominator + eps_attn)
            result = numerator * inverse
            acc[here, first : first + LANES] = result
            acc[here, first + LANES : first + 2 * LANES] = inverse
            heard[here, p * LANES : (p + 1) * LANES] = result.astype(bf16)
        return carry

    lax.fori_loop(0, s.chunks, join_body, 0)
    get_out.finish()
    get_up[1].hand_on()

    bias_out, gain_two, shift_two = (vecs[k : k + 1, :width] for k in (3, 4, 5))
    bias_down = vecs[7:8, :width]
    total = state_in

    def middle_of(here):
        projected = nn(heard[here, :], wo[...].reshape(width, width))
        return x_ref[here, :].astype(f32) + projected + bias_out

    def middle_body(c, carry):
        here = span(c, TALL)
        middle = middle_of(here)
        hat, _ = normalised(middle)
        n2t[:, here] = (hat * gain_two + shift_two).astype(bf16).T
        total[here, :] = middle + bias_down
        return carry

    lax.fori_loop(0, rows // TALL, middle_body, 0)

    for t in range(4):
        if t == 1:
            get_up[2].hand_on()
        if t == 2:
            get_up[3].hand_on()
        get_up[t].finish()
        cols = slice(t * tile, (t + 1) * tile)

        up = wu[:, :, :, cols].reshape(width, tile)
        down = wd[t * per : (t + 1) * per].reshape(tile, width)
        active, slope = gelu_pair(tn(n2t[...], up) + vecs[6:7, cols])
        active = active.astype(bf16)
        act[:, cols] = active
        grad = slope * hgrad[:, :, :, cols].reshape(rows, tile).astype(f32)
        grad = grad.astype(bf16)
        hgrad[:, :, :, cols] = grad.reshape(rows // (2 * tall), 2, tall, tile)
        collect(6, t * tile, grad.astype(f32))
        total[...] += nn(active, down)
        back = nt(grad, up)
        gmid[...] = back if t == 0 else gmid[...] + back

    def output_copy(c):
        here = span(c, TALL)
        return pltpu.make_async_copy(gone.at[here, :], out_any.at[here, :], io_sem.at[1 + c])

    def second_body(c, carry):
        here = span(c, TALL)
        gone[here, :] = total[here, :].astype(bf16)
        output_copy(c).start()
        hat, scale = normalised(middle_of(here))
        back = gmid[here, :]
        collect(4, 0, back * hat)
        collect(5, 0, back)
        gmid[here, :] = cot[here, :].astype(f32) + norm_back(back, gain_two, hat, scale)
        return carry

    lax.fori_loop(0, rows // TALL, second_body, 0)
    for gather in gathers:
        gather.drain()

    stages = (stage_q, wo, wu, wd)
    results = (gq_out, go_out, gu_out, gd_out)

    class Scatter:
        def __init__(self, item):
            index, first, columns = s.scatters[item]
            self.stage, self.result = stages[index], results[index]
            self.first, self.count, self.height = first, columns, s.weights[index][0]
            self.cols = pl.ds(first, columns)
            shared = item - len(s.scatters) + 3
            if shared >= 0:
                self.rb0 = rb0[0].at[:, pl.ds(shared * self.height, self.height)]
            else:
                self.rb0 = rb0[item]
            self.rb1 = rb1[item]
            self.zsrc, self.zr1, self.zr2 = zsrc[item], zr1[item], zr2[item]
            self.part = columns // seq
            self.send, self.recv = r_send.at[item], r_recv.at[item]

        def across(self):
            return remote(
                self.stage.at[pl.ds(0, chips), 1 - core, :, self.cols],
                self.rb0,
                self.send.at[0],
                self.recv.at[0],
                sibling,
            )

        def sends(self):
            return [
                remote(
                    self.stage.at[peer[0] // 2, core, :, self.cols],
                    self.rb1.at[k],
                    self.send.at[1 + k],
                    self.recv.at[1 + k],
                    peer,
                )
                for k, peer in enumerate(peers)
            ]

        def quarters(self):
            return [
                remote(
                    self.zsrc.at[:, span(lax.rem(z + step, seq), self.part)],
                    self.zr1.at[step - 1],
                    self.send.at[nk + step],
                    self.recv.at[nk + step],
                    (me, lax.rem(z + step, seq)),
                )
                for step in range(1, seq)
            ]

        def totals(self, arriving=False):
            copies = []
            for step in range(1, seq):
                owner = lax.rem(z - step + seq, seq) if arriving else z
                piece = self.zr2.at[:, span(owner, self.part)]
                k = nk + seq - 1 + step
                target = (me, lax.rem(z + step, seq))
                copies.append(remote(piece, piece, self.send.at[k], self.recv.at[k], target))
            return copies

        def start(self):
            self.across().start()

        def plane(self):
            self.across().wait_recv()

            def add(k, carry):
                here = (k, core, slice(None), self.cols)
                self.stage[here] = (
                    self.stage[here].astype(f32) + self.rb0[k].astype(f32)
                ).astype(bf16)
                return carry

            lax.fori_loop(0, chips, add, 0)
            for copy in self.sends():
                copy.start()

        def along(self):
            for copy in self.sends():
                copy.wait_recv()
            total = self.stage[chip, core, :, self.cols].astype(f32)
            for k in range(nk):
                total = total + self.rb1[k].astype(f32)
            self.zsrc[...] = total.astype(bf16)
            for copy in self.quarters():
                copy.start()

        def along_again(self):
            for copy in self.quarters():
                copy.wait_recv()
            mine = span(z, self.part)
            total = self.zsrc[:, mine].astype(f32)
            for step in range(seq - 1):
                total = total + self.zr1[step].astype(f32)
            self.zr2[:, mine] = total.astype(bf16)
            for copy in self.totals():
                copy.start()

        def finish(self):
            for copy in self.totals(True):
                copy.wait_recv()
            self.result[:, self.cols] = self.zr2[...]

        def drain(self):
            for copy in [self.across()] + self.sends() + self.quarters() + self.totals():
                copy.wait_send()

    scatters = [Scatter(item) for item in range(len(s.scatters))]
    down_item, up_item, out_item = scatters[:3]

    def down_body(c, carry):
        grad = tn(act[:, span(c, tile)], cot[...]).astype(bf16)
        wd[pl.ds(c * per, per)] = grad.reshape(per, 2, hidden // dp, width)
        return carry

    lax.fori_loop(0, hidden // tile, down_body, 0)
    down_item.start()

    bd_square = block_diag[:, :LANES].astype(bf16)
    head_sum = jnp.concatenate([bd_square, bd_square], axis=0)
    lane_hi = (lanes_of((CHUNK, LANES)) & 63) < 32

    def heads_body(c, carry):
        here = span(c, CHUNK)
        low = gmid[here, :].astype(bf16)
        gone[here, :] = low
        collect(3, 0, low.astype(f32))
        back = nt(low, wo[...].reshape(width, width)).astype(bf16).astype(f32)
        for p in range(s.pairs):
            first = 2 * p * LANES
            result = acc[here, first : first + LANES]
            inverse = acc[here, first + LANES : first + 2 * LANES]
            grad = back[:, p * LANES : (p + 1) * LANES]
            dnum[here, p * LANES : (p + 1) * LANES] = (grad * inverse).astype(bf16)
            product = grad * result
            upper = product.astype(bf16)
            lower = (product - upper.astype(f32)).astype(bf16)
            total = nn(jnp.concatenate([upper, lower], axis=1), head_sum)
            value = total * inverse * (-1.0 / 32.0)
            upper = value.astype(bf16)
            lower = value - upper.astype(f32)
            act[here, 3 * width + p * LANES : 3 * width + (p + 1) * LANES] = jnp.where(
                lane_hi, upper.astype(f32), lower
            ).astype(bf16)
        return carry

    for c in range(rows // TALL):
        output_copy(c).wait()
    lax.fori_loop(0, s.chunks, heads_body, 0)

    def grads_of(here, p):
        first = 3 * width + p * LANES
        return dnum[here, p * LANES : (p + 1) * LANES], act[here, first : first + LANES]

    for p in range(s.pairs):
        state[p] = jnp.zeros((LANES, 2 * LANES), f32)

    def gstate_body(step, carry):
        c = s.chunks - 1 - step
        here = span(c, CHUNK)
        keep = same(ending(c), before(c))
        live = in_segment(c, before(c)).astype(bf16)
        for p in range(s.pairs):
            now = state[p]
            state_in[state_at(c, p)] = now
            wide = jnp.concatenate(grads_of(here, p), axis=1)
            state[p] = keep * now + tn(cut(here, 0, p) * live, wide) * block_diag
        return carry

    down_item.plane()
    lax.fori_loop(0, s.chunks, gstate_body, 0)
    send_states(1, False)

    def up_body(c, carry):
        cols = span(c, tile)
        grad = nn(n2t[...], hgrad[:, :, :, cols].reshape(rows, tile)).astype(bf16)
        wu[:, :, :, cols] = grad.reshape(chips, 2, width // dp, tile)
        return carry

    lax.fori_loop(0, hidden // tile, up_body, 0)
    up_item.start()
    wo[...] = tn(heard[...], gone[...]).astype(bf16).reshape(chips, 2, width // dp, width)
    out_item.start()
    up_item.plane()
    out_item.plane()

    q_item, k_item, v_item = scatters[3:]

    def projection_grad(part):
        cols = slice(part * width, (part + 1) * width)
        grad = nn(n1t[...], act[:, cols]).astype(bf16)
        stage_q[:chips, :, :, cols] = grad.reshape(chips, 2, width // dp, width)

    def value_body(c, carry):
        here = span(c, CHUNK)
        seen_t = mask[c].T
        raw = []
        for p in range(s.pairs):
            q, k = cut(here, 0, p), cut(here, 1, p)
            raw.append((nt(k * ones_low, q), nt(k * ones_high, q)))
        for p in range(s.pairs):
            dn, _ = grads_of(here, p)
            scores = jnp.concatenate([part.astype(bf16) * seen_t for part in raw[p]], axis=1)
            acc[here, p * LANES : (p + 1) * LANES] = nn(
                scores, jnp.concatenate([dn * ones_low, dn * ones_high], axis=0)
            )
        return carry

    lax.fori_loop(0, s.chunks, value_body, 0)
    take_states(1, False)

    def ahead_body(c, carry):
        here = span(c, CHUNK)
        chosen = in_segment(c, ending(c))
        carried = same(ending(c), last)
        for p in range(s.pairs):
            ahead = state_in[state_at(c, p)] + carried * state[p]
            sums = ahead[:, LANES:]
            sums = 2.0 * spread_ends(sums + pltpu.roll(sums, 64, 1)) * block_diag[:, LANES:]
            upper = sums.astype(bf16).astype(f32)
            sums = jnp.where(low_half, upper, sums - upper)
            state_in[state_at(c, p)] = jnp.concatenate([ahead[:, :LANES], sums], axis=1)
            grad = acc[here, p * LANES : (p + 1) * LANES] + chosen * nn(
                cut(here, 1, p), ahead[:, :LANES].astype(bf16)
            )
            first = 2 * width + p * LANES
            act[here, first : first + LANES] = grad.astype(bf16)
        return carry

    lax.fori_loop(0, s.chunks, ahead_body, 0)
    projection_grad(2)
    v_item.start()
    down_item.along()

    def back_body(c, carry):
        here = span(c, CHUNK)
        for at, work in ((0, v_item.plane), (2, down_item.along_again), (3, up_item.along)):
            pl.when(c == min(at, s.chunks - 1))(work)
        seen = mask[c]
        live = in_segment(c, before(c))
        chosen = in_segment(c, ending(c))
        raw = []
        extra = []
        for p in range(s.pairs):
            v = cut(here, 2, p)
            wide = jnp.concatenate(grads_of(here, p), axis=1)
            low = jnp.concatenate([v * ones_low, ones_low], axis=1)
            high = jnp.concatenate([v * ones_high, ones_high], axis=1)
            raw.append((nt(wide, low), nt(wide, high)))
            both = jnp.concatenate([v, jnp.ones_like(v)], axis=1)
            ahead = state_in[state_at(c, p)]
            upper = ahead.astype(bf16)
            lower = (ahead - upper.astype(f32)).astype(bf16)
            extra.append(
                (
                    nt(wide, state_b[c, p, :LANES]) + nt(wide, state_b[c, p, LANES:]),
                    nt(both, upper) + nt(v, lower[:, :LANES]),
                )
            )
        for p in range(s.pairs):
            q, k = cut(here, 0, p), cut(here, 1, p)
            low, high = (part.astype(bf16) * seen for part in raw[p])
            gq = live * extra[p][0] + nn(
                jnp.concatenate([low, high], axis=1),
                jnp.concatenate([k * ones_low, k * ones_high], axis=0),
            )
            gk = chosen * extra[p][1] + tn(
                jnp.concatenate([low, high], axis=0),
                jnp.concatenate([q * ones_low, q * ones_high], axis=0),
            )
            for part, grad in ((0, gq), (1, gk)):
                grad = grad.astype(bf16)
                first = part * width + p * LANES
                slope = jnp.minimum((q, k)[part].astype(f32), 1.0)
                grad = (grad.astype(f32) * slope).astype(bf16)
                collect(2, first, grad.astype(f32))
                act[here, first : first + LANES] = grad
        return carry

    lax.fori_loop(0, s.chunks, back_body, 0)
    projection_grad(0)
    q_item.start()
    projection_grad(1)
    k_item.start()
    out_item.along()
    up_item.along_again()
    q_item.plane()
    k_item.plane()
    v_item.along()
    out_item.along_again()
    down_item.finish()

    def input_body(c, carry):
        here = span(c, TALL)
        grad = nt(act[here, : 3 * width], wq[...].reshape(width, 3 * width))
        hat, scale = normalised(x_ref[here, :].astype(f32))
        collect(0, 0, grad * hat)
        collect(1, 0, grad)
        gone[here, :] = (gmid[here, :] + norm_back(grad, gain_one, hat, scale)).astype(bf16)
        pltpu.make_async_copy(gone.at[here, :], gin_any.at[here, :], io_sem.at[1 + rows // TALL + c]).start()
        return carry

    lax.fori_loop(0, rows // TALL, input_body, 0)

    for k, n in enumerate(s.sizes):
        table = one_hot(n)
        row = jnp.sum(vsum[:, starts[k] : starts[k] + n], axis=0, keepdims=True)
        spread = jnp.where(owner_mask(n), jnp.broadcast_to(row, (dp, n)), 0.0).astype(bf16)
        pieces = nt(spread, table)
        if pieces.shape[1] < s.vec_lanes:
            pad = jnp.zeros((dp, s.vec_lanes - pieces.shape[1]), f32)
            pieces = jnp.concatenate([pieces, pad], axis=1)
        vstage[:, k, :] = pieces
    vec_back = []
    for step in range(1, dp):
        target = lax.rem(me + step, dp)
        vec_back.append(
            remote(
                vstage.at[target],
                vback.at[step - 1],
                v_send.at[dp - 2 + step],
                v_recv.at[dp - 2 + step],
                (target, z),
            )
        )
        vec_back[-1].start()
    v_item.along_again()
    q_item.along()
    k_item.along()
    for copy in vec_back:
        copy.wait_recv()
    total = vstage[me]
    for step in range(dp - 1):
        total = total + vback[step]
    vz[...] = total
    vec_z = []
    for step in range(1, seq):
        vec_z.append(
            remote(
                vz,
                vzback.at[step - 1],
                v_send.at[2 * dp - 3 + step],
                v_recv.at[2 * dp - 3 + step],
                (me, lax.rem(z + step, seq)),
            )
        )
        vec_z[-1].start()
    q_item.along_again()
    k_item.along_again()
    up_item.finish()
    out_item.finish()
    v_item.finish()
    for copy in vec_z:
        copy.wait_recv()
    terms = [vz[...]] + [vzback[step] for step in range(seq - 1)]
    while len(terms) > 1:
        half = len(terms) // 2
        terms = [terms[i] + terms[i + half] for i in range(half)]
    vec_out[...] = terms[0]
    q_item.finish()
    k_item.finish()

    for c in range(rows // TALL):
        here = pl.ds(c * TALL, TALL)
        pltpu.make_async_copy(gone.at[here, :], gin_any.at[here, :], io_sem.at[1 + rows // TALL + c]).wait()
    drain_states(0, True)
    drain_states(1, False)
    for copy in vec_sends + vec_back + vec_z:
        copy.wait_send()
    for item in scatters:
        item.drain()


def widen_kernel(parts, *refs):
    count = 7
    ins, outs = refs[:count], refs[count : count + 14]
    got, made, in_sem, out_sem = refs[count + 14 :]
    out_in, gin_in, *grads_in, vec_in = ins
    out_out, gin_out, *rest = outs
    rows = out_in.shape[0] // parts
    here = [pl.ds(k * rows, rows) for k in range(parts)]
    loads = [
        [pltpu.make_async_copy(source.at[at], got.at[i, at], in_sem.at[i, k]) for k, at in enumerate(here)]
        for i, source in enumerate((gin_in, out_in))
    ]
    for copy in loads[0] + loads[1]:
        copy.start()
    stores = []
    for k, at in enumerate(here):
        loads[0][k].wait()
        made[at] = got[0, at].astype(f32)
        stores.append(pltpu.make_async_copy(made.at[at], gin_out.at[at], out_sem.at[0, k]))
        stores[-1].start()
    for k, at in enumerate(here):
        loads[1][k].wait()
        stores.append(pltpu.make_async_copy(got.at[1, at], out_out.at[at], out_sem.at[1, k]))
        stores[-1].start()
    for grad, result in zip(grads_in, rest[:4]):
        result[...] = grad[...].astype(f32)
    for k, result in enumerate(rest[4:]):
        result[...] = vec_in[k : k + 1, : result.shape[1]]
    for copy in stores:
        copy.wait()


def widen(s, vectors, results):
    parts = 4
    out, gin, *grads, vec = results
    vmem = pl.BlockSpec(memory_space=pltpu.VMEM)
    anywhere = pl.BlockSpec(memory_space=pl.ANY)
    return pl.pallas_call(
        functools.partial(widen_kernel, parts),
        out_shape=[jax.ShapeDtypeStruct(out.shape, bf16)]
        + [jax.ShapeDtypeStruct(value.shape, f32) for value in (gin, *grads)]
        + [jax.ShapeDtypeStruct((1, v.shape[0]), f32) for v in vectors],
        in_specs=[anywhere] * 2 + [vmem] * 5,
        out_specs=[anywhere] * 2 + [vmem] * 12,
        scratch_shapes=[
            pltpu.VMEM((2,) + out.shape, bf16),
            pltpu.VMEM(out.shape, f32),
            pltpu.SemaphoreType.DMA((2, parts)),
            pltpu.SemaphoreType.DMA((2, parts)),
        ],
        compiler_params=pltpu.CompilerParams(vmem_limit_bytes=63 << 20),
        name="widen",
    )(out, gin, *grads, vec)


def solution(mesh):
    def body(inputs, lengths, cotangent, *params):
        gain_one, shift_one, w_qkv, b_qk, w_out, b_out, gain_two, shift_two, w_up, b_up, w_down, b_down = params
        packs, rows, width = inputs.shape[1:]
        hidden = w_up.shape[1]
        s = Shape(mesh, rows, width, hidden)
        dp, seq, chips, pairs = s.dp, s.seq, s.chips, s.pairs
        nk = chips - 1
        vectors = (gain_one, shift_one, b_qk, b_out, gain_two, shift_two, b_up, b_down)
        vmem = pl.BlockSpec(memory_space=pltpu.VMEM)
        anywhere = pl.BlockSpec(memory_space=pl.ANY)
        grids = [(chips, 2) + shape for shape in s.weights]
        shapes = [(s.weights[index][0], columns) for index, _, columns in s.scatters]
        dma = pltpu.SemaphoreType.DMA
        tall = s.weights[0][0]
        message_rows = pairs // 2 * LANES + -(-pairs // 8) * 8
        scratch = (
            [pltpu.VMEM(grid, bf16) for grid in grids]
            + [
                pltpu.VMEM((rows, width), bf16),
                pltpu.VMEM((rows, width), bf16),
                pltpu.VMEM((width, rows), bf16),
                pltpu.VMEM((rows, 3 * width), bf16),
                pltpu.VMEM((rows, 2 * width), f32),
                pltpu.VMEM((s.chunks, CHUNK, CHUNK), bf16),
                pltpu.VMEM((rows, width), f32),
                pltpu.VMEM((pairs, LANES, 2 * LANES), f32),
                pltpu.VMEM((s.chunks, pairs, 2 * LANES, 2 * LANES), bf16),
                pltpu.VMEM((width, rows), bf16),
                pltpu.VMEM((rows, hidden), bf16),
                pltpu.VMEM((rows // (2 * tall), 2, tall, hidden), bf16),
                pltpu.VMEM((rows, width), f32),
                pltpu.VMEM((rows, width), bf16),
                pltpu.VMEM((8, hidden), f32),
                pltpu.VMEM((8, s.vec_lanes), f32),
                pltpu.VMEM((dp, 8, s.vec_lanes), f32),
                pltpu.VMEM((8, sum(s.sizes)), f32),
                pltpu.VMEM((dp, 8, s.vec_lanes), f32),
                pltpu.VMEM((dp - 1, 8, s.vec_lanes), f32),
                pltpu.VMEM((8, s.vec_lanes), f32),
                pltpu.VMEM((seq - 1, 8, s.vec_lanes), f32),
                pltpu.VMEM((2, message_rows, LANES), f32),
                pltpu.VMEM((2, seq - 1, message_rows, LANES), f32),
                [pltpu.VMEM((chips,) + shape, bf16) for shape in shapes[:3]],
                [pltpu.VMEM((nk,) + shape, bf16) for shape in shapes],
                [pltpu.VMEM(shape, bf16) for shape in shapes],
                [pltpu.VMEM((seq - 1, tall_, n // seq), bf16) for tall_, n in shapes],
                [pltpu.VMEM(shape, bf16) for shape in shapes],
                dma((len(s.gathers),)),
                dma((len(s.gathers), nk + 1)),
                dma((len(s.gathers), nk + 1)),
                dma((2 * dp - 2 + seq - 1,)),
                dma((2 * dp - 2 + seq - 1,)),
                dma((2, seq - 1)),
                dma((2, seq - 1)),
                dma((len(s.scatters), nk + 2 * seq - 1)),
                dma((len(s.scatters), nk + 2 * seq - 1)),
                dma((1 + 2 * (rows // TALL),)),
            ]
        )
        outs = pl.pallas_call(
            functools.partial(kernel, s),
            out_shape=(
                jax.ShapeDtypeStruct((rows, width), bf16),
                jax.ShapeDtypeStruct((rows, width), bf16),
            )
            + tuple(jax.ShapeDtypeStruct(shape, bf16) for shape in s.weights)
            + (jax.ShapeDtypeStruct((8, s.vec_lanes), f32),),
            in_specs=[pl.BlockSpec(memory_space=pltpu.SMEM), vmem, anywhere, [vmem] * 8]
            + [anywhere] * 4,
            out_specs=(anywhere, anywhere) + (vmem,) * 5,
            scratch_shapes=scratch,
            compiler_params=pltpu.CompilerParams(
                collective_id=0, has_side_effects=True, vmem_limit_bytes=63 << 20
            ),
            name="layer",
        )(
            lengths.reshape(3),
            inputs.reshape(rows, width),
            cotangent.reshape(rows, width),
            [v.reshape(-1, min(v.shape[0], LANES)) for v in vectors],
            w_qkv,
            w_out,
            w_up,
            w_down,
        )
        out, gin, *grads = widen(s, vectors, outs)
        g_qkv, g_out, g_up, g_down, *pieces = grads
        pieces = [piece.reshape(piece.shape[1]) for piece in pieces]
        return (
            out.reshape(inputs.shape),
            gin.reshape(inputs.shape),
            pieces[0],
            pieces[1],
            g_qkv,
            pieces[2],
            g_out,
            pieces[3],
            pieces[4],
            pieces[5],
            g_up,
            pieces[6],
            g_down,
            pieces[7],
        )

    rows_spec = P("dp", None, "seq", None)
    one, two = P("dp"), P("dp", None)
    params = (one, one, two, one, two, one, one, one, two, one, two, one)
    return jax.shard_map(
        body,
        mesh=mesh,
        in_specs=(rows_spec, P("dp", None, None), rows_spec) + params,
        out_specs=(rows_spec, rows_spec) + params,
        check_vma=False,
    )
```

```python
import functools

import jax
import jax.numpy as jnp
from jax import lax
from jax.experimental import pallas as pl
from jax.experimental.pallas import tpu as pltpu
from jax.sharding import PartitionSpec as P

HEADS = 8
CHUNK = 256
TALL = 640
LANES = 128
eps_norm = 1e-05
eps_attn = 1e-06
MESH = pl.DeviceIdType.MESH
f32 = jnp.float32
bf16 = jnp.bfloat16


def dot(a, b, ca, cb):
    return lax.dot_general(a, b, (((ca,), (cb,)), ((), ())), preferred_element_type=f32)


def nn(a, b):
    return dot(a, b, 1, 0)


def nt(a, b):
    return dot(a, b, 1, 1)


def tn(a, b):
    return dot(a, b, 0, 0)


def span(index, size):
    return pl.ds(pl.multiple_of(index * size, size), size)


def lanes_of(shape):
    return lax.broadcasted_iota(jnp.int32, shape, len(shape) - 1)


def rows_of(shape):
    return lax.broadcasted_iota(jnp.int32, shape, len(shape) - 2)


def fold_rows(values):
    rows, width = values.shape
    return jnp.sum(values.reshape(rows // 8, 8, width), axis=0)


def normalised(values):
    width = values.shape[-1]
    mean = jnp.sum(values, axis=-1, keepdims=True) * (1.0 / width)
    centred = values - mean
    variance = jnp.sum(centred * centred, axis=-1, keepdims=True) * (1.0 / width)
    scale = lax.rsqrt(variance + eps_norm)
    return centred * scale, scale


def norm_back(grad, gain, hat, scale):
    width = grad.shape[-1]
    a = grad * gain
    mean_a = jnp.sum(a, axis=-1, keepdims=True) * (1.0 / width)
    mean_ah = jnp.sum(a * hat, axis=-1, keepdims=True) * (1.0 / width)
    return (a - mean_a - hat * mean_ah) * scale


def gelu_pair(x):
    cdf = 0.5 + 0.5 * lax.erf(x * 0.7071067811865476)
    return x * cdf, cdf + x * (0.3989422804014327 * jnp.exp2(x * x * -0.7213475204444817))


class Shape:
    def __init__(self, mesh, rows, width, hidden):
        self.dp = mesh.shape["dp"]
        self.seq = mesh.shape["seq"]
        self.chips = self.dp // 2
        self.side = max(k for k in range(1, self.chips + 1) if k * k <= self.chips and self.chips % k == 0)
        self.rows, self.width, self.hidden = rows, width, hidden
        self.chunks = rows // CHUNK
        self.pairs = width // LANES
        self.sizes = (width, width, 2 * width, width, width, width, hidden, width)
        self.vec_lanes = max(-(-n // self.dp // LANES) * LANES for n in self.sizes)
        w, h, d = width, hidden, self.dp
        self.weights = ((w // d, 3 * w), (w // d, w), (w // d, h), (h // d, w))
        self.gathers = (
            (0, w, w),
            (0, 2 * w, w),
            (0, 0, w),
            (3, 0, w),
            (1, 0, w),
        ) + tuple((2, t * (h // 4), h // 4) for t in range(4))
        self.scatters = tuple((2, t * (h // 4), h // 4) for t in range(4)) + (
            (3, 0, w),
            (1, 0, w),
            (0, 0, w),
            (0, w, w),
            (0, 2 * w, w),
        )


def kernel(
    s,
    lengths,
    x_ref,
    cot_any,
    vec_refs,
    wq_any,
    wo_any,
    wu_any,
    wd_any,
    out_any,
    gin_any,
    gq_out,
    go_out,
    gu_out,
    gd_out,
    vec_out,
    wq,
    wo,
    wu,
    wd,
    cot,
    n1,
    n1t,
    feat,
    acc,
    mask,
    state_in,
    state,
    state_b,
    n2t,
    act,
    hgrad,
    gmid,
    gone,
    vecs,
    vec_ref,
    vgot,
    vsum,
    vstage,
    vback,
    vz,
    vzback,
    msg,
    msg_in,
    rb0,
    rb1,
    zsrc,
    zr1,
    zr2,
    g_local,
    g_send,
    g_recv,
    v_send,
    v_recv,
    m_send,
    m_recv,
    r_send,
    r_recv,
    io_sem,
):
    dp, seq, chips, side = s.dp, s.seq, s.chips, s.side
    rows, width, hidden = s.rows, s.width, s.hidden
    me, z = lax.axis_index("dp"), lax.axis_index("seq")
    core, chip = lax.rem(me, 2), me // 2
    cy, cx = chip // side, lax.rem(chip, side)
    offsets = [(dy, dx) for dy in range(chips // side) for dx in range(side)][1:]

    def chip_at(dy, dx):
        ny = chips // side
        return lax.rem(cy + dy + ny, ny) * side + lax.rem(cx + dx + side, side)

    heard, dnum, stage_q = n1, cot, hgrad

    sibling = (chip * 2 + 1 - core, z)
    peers = [(chip_at(dy, dx) * 2 + core, z) for dy, dx in offsets]
    z_up, z_down = lax.rem(z + 1, seq), lax.rem(z + seq - 1, seq)

    def remote(src, dst, send, recv, device):
        return pltpu.make_async_remote_copy(
            src_ref=src,
            dst_ref=dst,
            send_sem=send,
            recv_sem=recv,
            device_id=device,
            device_id_type=MESH,
        )

    barrier = pltpu.get_barrier_semaphore()
    for step in range(1, dp):
        pl.semaphore_signal(
            barrier, inc=1, device_id=(lax.rem(me + step, dp), z), device_id_type=MESH
        )
    for step in range(1, seq):
        pl.semaphore_signal(
            barrier, inc=1, device_id=(me, lax.rem(z + step, seq)), device_id_type=MESH
        )
    pl.semaphore_wait(barrier, dp + seq - 2)

    vec_ref[...] = jnp.zeros_like(vec_ref)
    for k, ref in enumerate(vec_refs):
        lanes = ref.shape[1]
        for row in range(ref.shape[0]):
            vec_ref[k : k + 1, row * lanes : (row + 1) * lanes] = ref[row : row + 1, :].astype(f32)
    vec_sends = []
    for step in range(1, dp):
        vec_sends.append(
            remote(
                vec_ref,
                vgot.at[me],
                v_send.at[step - 1],
                v_recv.at[step - 1],
                (lax.rem(me + step, dp), z),
            )
        )
        vec_sends[-1].start()
    vgot[me] = vec_ref[...]

    sources = (wq_any, wo_any, wu_any, wd_any)
    weights = (wq, wo, wu, wd)
    nk = len(peers)

    class Gather:
        def __init__(self, item):
            index, first, columns = s.gathers[item]
            self.buffer, self.source = weights[index], sources[index]
            self.columns = pl.ds(first, columns)
            self.send, self.recv, self.local = g_send.at[item], g_recv.at[item], g_local.at[item]

        def start(self):
            src = self.source.at[:, self.columns]
            dst = self.buffer.at[chip, core, :, self.columns]
            self.own = pltpu.make_async_copy(src, dst, self.local)
            self.own.start()
            self.plane = [
                remote(src, dst, self.send.at[k], self.recv.at[k], peer)
                for k, peer in enumerate(peers)
            ]
            for copy in self.plane:
                copy.start()

        def hand_on(self):
            self.own.wait()
            for copy in self.plane:
                copy.wait_recv()
            mine = self.buffer.at[:, core, :, self.columns]
            self.across = remote(mine, mine, self.send.at[nk], self.recv.at[nk], sibling)
            self.across.start()

        def finish(self):
            theirs = self.buffer.at[:, 1 - core, :, self.columns]
            remote(theirs, theirs, self.send.at[nk], self.recv.at[nk], sibling).wait_recv()

        def drain(self):
            for copy in self.plane + [self.across]:
                copy.wait_send()

    gathers = [Gather(item) for item in range(len(s.gathers))]
    for item in range(3):
        gathers[item].start()
    cot_copy = pltpu.make_async_copy(cot_any, cot, io_sem.at[0])
    cot_copy.start()

    bound_0 = lengths[0]
    bound_1 = bound_0 + lengths[1]
    bound_2 = bound_1 + lengths[2]
    first_row = z * rows

    def segment(position):
        return sum((position >= bound).astype(jnp.int32) for bound in (bound_0, bound_1, bound_2))

    def same(a, b):
        return (a == b).astype(f32)

    prior = jnp.where(first_row > 0, segment(first_row - 1), -1)
    last = segment(first_row + rows - 1)

    def before(c):
        return jnp.where(first_row + c * CHUNK > 0, segment(first_row + c * CHUNK - 1), -1)

    def ending(c):
        return segment(first_row + (c + 1) * CHUNK - 1)

    def in_segment(c, which):
        shape = (CHUNK, LANES)
        return (segment(first_row + c * CHUNK + rows_of(shape)) == which).astype(f32)

    square = (CHUNK, CHUNK)
    pair = (LANES, LANES)
    lane_low = lanes_of((CHUNK, LANES)) < 64
    block_diag = (
        (lanes_of((LANES, 2 * LANES)) // 64) % 2 == rows_of((LANES, 2 * LANES)) // 64
    ).astype(f32)
    low_pair = lanes_of(pair) < 64
    diagonal = lanes_of(pair) == rows_of(pair)
    low_half = (lanes_of(pair) & 63) < 32
    ones_low = lane_low.astype(bf16)
    ones_high = 1.0 - ones_low

    def mask_body(c, carry):
        down, across = rows_of(square), lanes_of(square)
        base = first_row + c * CHUNK
        alike = segment(base + down) == segment(base + across)
        mask[c] = (alike & (across <= down)).astype(f32).astype(bf16)
        return carry

    lax.fori_loop(0, s.chunks, mask_body, 0)

    for step in range(1, dp):
        source = lax.rem(me - step + dp, dp)
        remote(
            vec_ref, vgot.at[source], v_send.at[step - 1], v_recv.at[step - 1], (source, z)
        ).wait_recv()

    def one_hot(n):
        piece = n // dp
        tall = -(-piece // LANES) * LANES
        shape = (tall, n)
        return ((lanes_of(shape) & (piece - 1)) == rows_of(shape)).astype(f32).astype(bf16)

    def owner_mask(n):
        piece = n // dp
        shape = (dp, n)
        low = rows_of(shape) * piece
        return (lanes_of(shape) >= low) & (lanes_of(shape) < low + piece)

    for k, n in enumerate(s.sizes):
        table = one_hot(n)
        pieces = vgot[:, k, : table.shape[0]].astype(bf16)
        spread = jnp.where(owner_mask(n), nn(pieces, table), 0.0)
        vecs[k : k + 1, :n] = jnp.sum(spread, axis=0, keepdims=True)

    starts = [sum(s.sizes[:k]) for k in range(len(s.sizes))]

    def collect(k, first, values):
        at = starts[k] + first
        vsum[:, at : at + values.shape[1]] += fold_rows(values)

    gain_one, shift_one = vecs[0:1, :width], vecs[1:2, :width]
    for k, n in enumerate(s.sizes):
        vsum[:, starts[k] : starts[k] + n] = jnp.zeros((8, n), f32)

    def norm_body(c, carry):
        here = span(c, CHUNK)
        hat, _ = normalised(x_ref[here, :].astype(f32))
        normed = (hat * gain_one + shift_one).astype(bf16)
        n1[here, :] = normed
        n1t[:, here] = normed.T
        return carry

    lax.fori_loop(0, s.chunks, norm_body, 0)

    get_down, get_out = gathers[3:5]
    get_up = gathers[5:]

    def project(get, part):
        get.finish()
        cols = slice(part * width, (part + 1) * width)
        weight = wq[:, :, :, cols].reshape(width, width)

        def project_body(c, carry):
            here = span(c, TALL)
            mixed = nn(n1[here, :], weight)
            if part < 2:
                mixed = mixed + vecs[2:3, cols]
                mixed = jnp.where(mixed > 0.0, mixed + 1.0, jnp.exp(jnp.minimum(mixed, 0.0)))
            feat[here, cols] = mixed.astype(bf16)
            return carry

        lax.fori_loop(0, rows // TALL, project_body, 0)

    gathers[0].hand_on()
    get_down.start()
    gathers[1].hand_on()
    get_out.start()
    project(gathers[0], 1)
    project(gathers[1], 2)

    def cut(here, part, p):
        first = part * width + p * LANES
        return feat[here, first : first + LANES]

    for p in range(s.pairs):
        state[p] = jnp.zeros((LANES, 2 * LANES), f32)

    def state_at(c, p):
        first = pl.multiple_of(c * (s.pairs // 2 * LANES), LANES) + p // 2 * LANES
        return pl.ds(first, LANES), slice(p % 2 * 2 * LANES, (p % 2 + 1) * 2 * LANES)

    def state_body(c, carry):
        here = span(c, CHUNK)
        keep = same(ending(c), before(c))
        chosen = in_segment(c, ending(c)).astype(bf16)
        for p in range(s.pairs):
            wide = jnp.concatenate([cut(here, 2, p) * chosen, chosen], axis=1)
            now = state[p]
            state_in[state_at(c, p)] = now
            state[p] = keep * now + tn(cut(here, 1, p), wide) * block_diag
        return carry

    lax.fori_loop(0, s.chunks, state_body, 0)

    def spread_ends(right):
        return 0.5 * (right + pltpu.roll(right, 32, 1))

    def packed(slot):
        halves = []
        ends = []
        for p in range(s.pairs):
            left = state[p, :, :LANES]
            right = state[p, :, LANES:]
            halves.append(left + pltpu.roll(left, 64, 1))
            ends.append(spread_ends(right + pltpu.roll(right, 64, 1)))
        for q in range(s.pairs // 2):
            msg[slot, q * LANES : (q + 1) * LANES] = jnp.where(
                low_pair, halves[2 * q], halves[2 * q + 1]
            )
        ends = [jnp.sum(jnp.where(diagonal, end, 0.0), axis=0, keepdims=True) for end in ends]
        ends.append(jnp.zeros((msg.shape[1] - s.pairs // 2 * LANES - s.pairs, LANES), f32))
        msg[slot, s.pairs // 2 * LANES :] = jnp.concatenate(ends, axis=0)

    def unpacked(slot, step, p):
        sums = msg_in[slot, step, p // 2 * LANES : (p // 2 + 1) * LANES]
        turned = pltpu.roll(sums, 64, 1)
        left = jnp.where(low_pair, sums, turned) if p % 2 == 0 else jnp.where(low_pair, turned, sums)
        first = s.pairs // 2 * LANES + p
        ends = jnp.where(diagonal, msg_in[slot, step, first : first + 1], 0.0)
        right = jnp.sum(ends, axis=1, keepdims=True)
        return jnp.concatenate([left, jnp.broadcast_to(right, pair)], axis=1) * block_diag

    def message(slot, step, forward):
        target = lax.rem(z + step, seq) if forward else lax.rem(z - step + seq, seq)
        return remote(
            msg.at[slot],
            msg_in.at[slot, step - 1],
            m_send.at[slot, step - 1],
            m_recv.at[slot, step - 1],
            (me, target),
        )

    def send_states(slot, forward):
        packed(slot)
        for step in range(1, seq):

            @pl.when((z + step < seq) if forward else (z - step >= 0))
            def _():
                message(slot, step, forward).start()

    def take_states(slot, forward):
        for p in range(s.pairs):
            state[p] = jnp.zeros((LANES, 2 * LANES), f32)
        for step in range(1, seq):

            @pl.when((z - step >= 0) if forward else (z + step < seq))
            def _():
                message(slot, step, forward).wait_recv()
                if forward:
                    weight = same(segment((z - step + 1) * rows - 1), prior)
                else:
                    weight = same(segment((z + step) * rows - 1), last)
                for p in range(s.pairs):
                    state[p] = state[p] + weight * unpacked(slot, step - 1, p)

    def drain_states(slot, forward):
        for step in range(1, seq):

            @pl.when((z + step < seq) if forward else (z - step >= 0))
            def _():
                message(slot, step, forward).wait_send()

    send_states(0, True)
    gathers[2].hand_on()
    get_up[0].start()
    project(gathers[2], 0)

    def inside_body(c, carry):
        here = span(c, CHUNK)
        seen = mask[c]
        raw = []
        for p in range(s.pairs):
            q, k = cut(here, 0, p), cut(here, 1, p)
            raw.append((nt(q, k * ones_low), nt(q, k * ones_high)))
        for p in range(s.pairs):
            v = cut(here, 2, p)
            scores = jnp.concatenate([part.astype(bf16) * seen for part in raw[p]], axis=1)
            low = jnp.concatenate([v * ones_low, ones_low], axis=1)
            high = jnp.concatenate([v * ones_high, ones_high], axis=1)
            acc[here, 2 * p * LANES : (2 * p + 2) * LANES] = nn(
                scores, jnp.concatenate([low, high], axis=0)
            )
        return carry

    lax.fori_loop(0, s.chunks, inside_body, 0)
    get_down.hand_on()
    get_up[1].start()
    get_out.hand_on()
    get_up[2].start()
    get_down.finish()
    cot_copy.wait()

    tile = hidden // 4
    tall = s.weights[0][0]
    per = chips // 4
    blocks = TALL // (2 * tall)

    def hidden_body(c, carry):
        here = span(c, TALL)
        branch = cot[here, :]
        collect(7, 0, branch.astype(f32))
        for t in range(4):
            down = wd[t * per : (t + 1) * per].reshape(tile, width)
            grad = nt(branch, down).astype(bf16).reshape(blocks, 2, tall, tile)
            hgrad[span(c, blocks), :, :, t * tile : (t + 1) * tile] = grad
        return carry

    lax.fori_loop(0, rows // TALL, hidden_body, 0)
    get_up[0].hand_on()
    get_up[3].start()
    take_states(0, True)

    def join_body(c, carry):
        here = span(c, CHUNK)
        live = in_segment(c, before(c))
        carried = same(before(c), prior)
        for p in range(s.pairs):
            whole = state_in[state_at(c, p)] + carried * state[p]
            upper = whole.astype(bf16)
            lower = (whole - upper.astype(f32)).astype(bf16)
            state_b[c, p, :LANES] = upper
            state_b[c, p, LANES:] = lower
            q = cut(here, 0, p)
            extra = nn(jnp.concatenate([q, q], axis=1), state_b[c, p])
            first = 2 * p * LANES
            numerator = acc[here, first : first + LANES] + live * extra[:, :LANES]
            denominator = acc[here, first + LANES : first + 2 * LANES] + live * extra[:, LANES:]
            inverse = 1.0 / (denominator + eps_attn)
            result = numerator * inverse
            acc[here, first : first + LANES] = result
            acc[here, first + LANES : first + 2 * LANES] = inverse
            heard[here, p * LANES : (p + 1) * LANES] = result.astype(bf16)
        return carry

    lax.fori_loop(0, s.chunks, join_body, 0)
    get_out.finish()
    get_up[1].hand_on()

    bias_out, gain_two, shift_two = (vecs[k : k + 1, :width] for k in (3, 4, 5))
    bias_down = vecs[7:8, :width]
    total = state_in

    def middle_of(here):
        projected = nn(heard[here, :], wo[...].reshape(width, width))
        return x_ref[here, :].astype(f32) + projected + bias_out

    def middle_body(c, carry):
        here = span(c, TALL)
        middle = middle_of(here)
        hat, _ = normalised(middle)
        n2t[:, here] = (hat * gain_two + shift_two).astype(bf16).T
        total[here, :] = middle + bias_down
        return carry

    lax.fori_loop(0, rows // TALL, middle_body, 0)

    outer = (z == 0) | (z == seq - 1)
    inward = jnp.where(z < seq // 2, z + 1, z - 1)
    outward = jnp.where(z < seq // 2, z - 1, z + 1)
    across = seq - 1 - z
    stages = (stage_q, wo, wu, wd)
    results = (gq_out, go_out, gu_out, gd_out)

    class Scatter:
        def __init__(self, item):
            index, first, columns = s.scatters[item]
            self.stage, self.result = stages[index], results[index]
            self.first, self.count, self.height = first, columns, s.weights[index][0]
            self.cols = pl.ds(first, columns)
            shared = item - len(s.scatters) + 3
            self.rb0 = rb0[shared if shared >= 0 else item]
            self.rb1 = rb1[item]
            self.zsrc, self.zr1, self.zr2 = zsrc[item], zr1[item], zr2[item]
            self.part = columns // seq
            self.short = seq != 4 or item >= len(s.scatters) - 2
            self.send, self.recv = r_send.at[item], r_recv.at[item]

        def across(self):
            return remote(
                self.stage.at[pl.ds(0, chips), 1 - core, :, self.cols],
                self.rb0,
                self.send.at[0],
                self.recv.at[0],
                sibling,
            )

        def sends(self):
            return [
                remote(
                    self.stage.at[peer[0] // 2, core, :, self.cols],
                    self.rb1.at[k],
                    self.send.at[1 + k],
                    self.recv.at[1 + k],
                    peer,
                )
                for k, peer in enumerate(peers)
            ]

        def quarters(self):
            return [
                remote(
                    self.zsrc.at[:, span(lax.rem(z + step, seq), self.part)],
                    self.zr1.at[pl.ds((step - 1) * self.height, self.height)],
                    self.send.at[nk + step],
                    self.recv.at[nk + step],
                    (me, lax.rem(z + step, seq)),
                )
                for step in range(1, seq)
            ]

        def totals(self, arriving=False):
            copies = []
            for step in range(1, seq):
                owner = lax.rem(z - step + seq, seq) if arriving else z
                piece = self.zr2.at[:, span(owner, self.part)]
                k = nk + seq - 1 + step
                target = (me, lax.rem(z + step, seq))
                copies.append(remote(piece, piece, self.send.at[k], self.recv.at[k], target))
            return copies

        def start(self):
            self.across().start()

        def plane(self):
            self.across().wait_recv()

            def add(k, carry):
                here = (k, core, slice(None), self.cols)
                self.stage[here] = (
                    self.stage[here].astype(f32) + self.rb0[k].astype(f32)
                ).astype(bf16)
                return carry

            lax.fori_loop(0, chips, add, 0)
            for copy in self.sends():
                copy.start()

        def along(self):
            for copy in self.sends():
                copy.wait_recv()
            total = self.stage[chip, core, :, self.cols].astype(f32)
            for k in range(nk):
                total = total + self.rb1[k].astype(f32)
            self.zsrc[...] = total.astype(bf16)
            if self.short:
                for copy in self.quarters():
                    copy.start()
            else:

                @pl.when(outer)
                def _():
                    self.step(0).start()

        def step(self, k):
            source, target = ((self.zsrc, self.zr1), (self.zsrc, self.zr2), (self.zsrc, self.zr2))[k]
            there = (inward, across, outward)[k]
            return remote(
                source, target, self.send.at[nk + 1 + k], self.recv.at[nk + 1 + k], (me, there)
            )

        def inner(self):
            @pl.when(jnp.logical_not(outer))
            def _():
                self.step(0).wait_recv()
                total = self.zsrc[...].astype(f32) + self.zr1[...].astype(f32)
                self.zsrc[...] = total.astype(bf16)
                self.step(1).start()

        def outward(self):
            @pl.when(jnp.logical_not(outer))
            def _():
                self.step(1).wait()
                total = self.zsrc[...].astype(f32) + self.zr2[...].astype(f32)
                self.zsrc[...] = total.astype(bf16)
                self.step(2).start()

        def along_again(self):
            for copy in self.quarters():
                copy.wait_recv()
            mine = span(z, self.part)
            total = self.zsrc[:, mine].astype(f32)
            for step in range(seq - 1):
                total = total + self.zr1[step * self.height : (step + 1) * self.height].astype(f32)
            self.zr2[:, mine] = total.astype(bf16)
            for copy in self.totals():
                copy.start()

        def finish(self):
            if self.short:
                for copy in self.totals(True):
                    copy.wait_recv()
                self.result[:, self.cols] = self.zr2[...]
            else:

                @pl.when(outer)
                def _():
                    self.step(2).wait_recv()
                    self.result[:, self.cols] = self.zr2[...]

                @pl.when(jnp.logical_not(outer))
                def _():
                    self.result[:, self.cols] = self.zsrc[...]

        def drain(self):
            for copy in [self.across()] + self.sends():
                copy.wait_send()
            if self.short:
                for copy in self.quarters() + self.totals():
                    copy.wait_send()
            else:

                @pl.when(outer)
                def _():
                    self.step(0).wait_send()

                @pl.when(jnp.logical_not(outer))
                def _():
                    self.step(2).wait_send()

    scatters = [Scatter(item) for item in range(len(s.scatters))]
    up_items, down_item, out_item = scatters[:4], scatters[4], scatters[5]
    q_item, k_item, v_item = scatters[6:]

    for t in range(4):
        if t == 1:
            get_up[2].hand_on()
        if t == 2:
            get_up[3].hand_on()
        get_up[t].finish()
        cols = slice(t * tile, (t + 1) * tile)

        up = wu[:, :, :, cols].reshape(width, tile)
        down = wd[t * per : (t + 1) * per].reshape(tile, width)
        active, slope = gelu_pair(tn(n2t[...], up) + vecs[6:7, cols])
        active = active.astype(bf16)
        act[:, cols] = active
        grad = slope * hgrad[:, :, :, cols].reshape(rows, tile).astype(f32)
        grad = grad.astype(bf16)
        hgrad[:, :, :, cols] = grad.reshape(rows // (2 * tall), 2, tall, tile)
        collect(6, t * tile, grad.astype(f32))
        total[...] += nn(active, down)
        back = nt(grad, up)
        gmid[...] = back if t == 0 else gmid[...] + back
        get_up[t].drain()
        if t == 0:
            get_down.drain()
        grad = nn(n2t[...], hgrad[:, :, :, cols].reshape(rows, tile)).astype(bf16)
        wu[:, :, :, cols] = grad.reshape(chips, 2, width // dp, tile)
        up_items[t].start()
        grad = tn(act[:, cols], cot[...]).astype(bf16)
        wd[t * per : (t + 1) * per] = grad.reshape(per, 2, hidden // dp, width)
        if t > 0:
            up_items[t - 1].plane()
        if t == 3:
            down_item.start()
            up_items[0].along()

    def output_copy(c):
        here = span(c, TALL)
        return pltpu.make_async_copy(gone.at[here, :], out_any.at[here, :], io_sem.at[1 + c])

    def second_body(c, carry):
        here = span(c, TALL)
        gone[here, :] = total[here, :].astype(bf16)
        output_copy(c).start()
        hat, scale = normalised(middle_of(here))
        back = gmid[here, :]
        collect(4, 0, back * hat)
        collect(5, 0, back)
        gmid[here, :] = cot[here, :].astype(f32) + norm_back(back, gain_two, hat, scale)
        return carry

    lax.fori_loop(0, rows // TALL, second_body, 0)
    for gather in gathers[:3] + [get_out]:
        gather.drain()
    up_items[3].plane()
    down_item.plane()
    up_items[1].along()
    up_items[0].inner()

    bd_square = block_diag[:, :LANES].astype(bf16)
    head_sum = jnp.concatenate([bd_square, bd_square], axis=0)
    lane_hi = (lanes_of((CHUNK, LANES)) & 63) < 32

    def heads_body(c, carry):
        here = span(c, CHUNK)
        low = gmid[here, :].astype(bf16)
        gone[here, :] = low
        collect(3, 0, low.astype(f32))
        back = nt(low, wo[...].reshape(width, width)).astype(bf16).astype(f32)
        for p in range(s.pairs):
            first = 2 * p * LANES
            result = acc[here, first : first + LANES]
            inverse = acc[here, first + LANES : first + 2 * LANES]
            grad = back[:, p * LANES : (p + 1) * LANES]
            dnum[here, p * LANES : (p + 1) * LANES] = (grad * inverse).astype(bf16)
            product = grad * result
            upper = product.astype(bf16)
            lower = (product - upper.astype(f32)).astype(bf16)
            total = nn(jnp.concatenate([upper, lower], axis=1), head_sum)
            value = total * inverse * (-1.0 / 32.0)
            upper = value.astype(bf16)
            lower = value - upper.astype(f32)
            act[here, 3 * width + p * LANES : 3 * width + (p + 1) * LANES] = jnp.where(
                lane_hi, upper.astype(f32), lower
            ).astype(bf16)
        return carry

    for c in range(rows // TALL):
        output_copy(c).wait()
    lax.fori_loop(0, s.chunks, heads_body, 0)

    def grads_of(here, p):
        first = 3 * width + p * LANES
        return dnum[here, p * LANES : (p + 1) * LANES], act[here, first : first + LANES]

    for p in range(s.pairs):
        state[p] = jnp.zeros((LANES, 2 * LANES), f32)

    def gstate_body(step, carry):
        c = s.chunks - 1 - step
        here = span(c, CHUNK)
        keep = same(ending(c), before(c))
        live = in_segment(c, before(c)).astype(bf16)
        for p in range(s.pairs):
            now = state[p]
            state_in[state_at(c, p)] = now
            wide = jnp.concatenate(grads_of(here, p), axis=1)
            state[p] = keep * now + tn(cut(here, 0, p) * live, wide) * block_diag
        return carry

    up_items[2].along()
    up_items[1].inner()
    up_items[0].outward()
    lax.fori_loop(0, s.chunks, gstate_body, 0)
    send_states(1, False)

    wo[...] = tn(heard[...], gone[...]).astype(bf16).reshape(chips, 2, width // dp, width)
    out_item.start()
    up_items[3].along()
    up_items[2].inner()
    up_items[1].outward()

    def keep_grad(here, part, p, grad, feature):
        first = part * width + p * LANES
        slope = jnp.minimum(feature.astype(f32), 1.0)
        grad = (grad.astype(bf16).astype(f32) * slope).astype(bf16)
        collect(2, first, grad.astype(f32))
        act[here, first : first + LANES] = grad

    def back_body(c, carry):
        here = span(c, CHUNK)
        for at, work in (
            (0, out_item.plane),
            (4, down_item.along),
        ):
            pl.when(c == min(at, s.chunks - 1))(work)
        seen = mask[c]
        live = in_segment(c, before(c))
        raw = []
        extra = []
        for p in range(s.pairs):
            v = cut(here, 2, p)
            wide = jnp.concatenate(grads_of(here, p), axis=1)
            low = jnp.concatenate([v * ones_low, ones_low], axis=1)
            high = jnp.concatenate([v * ones_high, ones_high], axis=1)
            raw.append((nt(wide, low), nt(wide, high)))
            extra.append(nt(wide, state_b[c, p, :LANES]) + nt(wide, state_b[c, p, LANES:]))
        for p in range(s.pairs):
            q, k = cut(here, 0, p), cut(here, 1, p)
            low, high = (part.astype(bf16) * seen for part in raw[p])
            gq = live * extra[p] + nn(
                jnp.concatenate([low, high], axis=1),
                jnp.concatenate([k * ones_low, k * ones_high], axis=0),
            )
            first = width + p * LANES
            acc[here, first : first + LANES] = tn(
                jnp.concatenate([low, high], axis=0),
                jnp.concatenate([q * ones_low, q * ones_high], axis=0),
            )
            keep_grad(here, 0, p, gq, q)
        return carry

    lax.fori_loop(0, s.chunks, back_body, 0)

    def projection_grad(part):
        cols = slice(part * width, (part + 1) * width)
        grad = nn(n1t[...], act[:, cols]).astype(bf16)
        stage_q[:chips, :, :, cols] = grad.reshape(chips, 2, width // dp, width)

    projection_grad(0)
    q_item.start()


    def value_body(c, carry):
        here = span(c, CHUNK)
        seen_t = mask[c].T
        raw = []
        for p in range(s.pairs):
            q, k = cut(here, 0, p), cut(here, 1, p)
            raw.append((nt(k * ones_low, q), nt(k * ones_high, q)))
        for p in range(s.pairs):
            dn, _ = grads_of(here, p)
            scores = jnp.concatenate([part.astype(bf16) * seen_t for part in raw[p]], axis=1)
            acc[here, p * LANES : (p + 1) * LANES] = nn(
                scores, jnp.concatenate([dn * ones_low, dn * ones_high], axis=0)
            )
        return carry

    lax.fori_loop(0, s.chunks, value_body, 0)
    q_item.plane()
    out_item.along()
    take_states(1, False)

    def ahead_body(c, carry):
        here = span(c, CHUNK)
        chosen = in_segment(c, ending(c))
        carried = same(ending(c), last)
        for p in range(s.pairs):
            ahead = state_in[state_at(c, p)] + carried * state[p]
            sums = ahead[:, LANES:]
            sums = 2.0 * spread_ends(sums + pltpu.roll(sums, 64, 1)) * block_diag[:, LANES:]
            upper = sums.astype(bf16).astype(f32)
            sums = jnp.where(low_half, upper, sums - upper)
            ahead = jnp.concatenate([ahead[:, :LANES], sums], axis=1)
            upper = ahead.astype(bf16)
            lower = (ahead - upper.astype(f32)).astype(bf16)
            k, v = cut(here, 1, p), cut(here, 2, p)
            both = jnp.concatenate([v, jnp.ones_like(v)], axis=1)
            first = width + p * LANES
            grad = acc[here, first : first + LANES] + chosen * (
                nt(both, upper) + nt(v, lower[:, :LANES])
            )
            keep_grad(here, 1, p, grad, k)
            grad = acc[here, p * LANES : (p + 1) * LANES] + chosen * nn(
                k, upper[:, :LANES]
            )
            first = 2 * width + p * LANES
            act[here, first : first + LANES] = grad.astype(bf16)
        return carry

    lax.fori_loop(0, s.chunks, ahead_body, 0)
    up_items[3].inner()
    up_items[2].outward()
    projection_grad(1)
    k_item.start()
    down_item.inner()
    projection_grad(2)
    v_item.start()
    out_item.inner()
    up_items[3].outward()
    k_item.plane()
    v_item.plane()
    down_item.outward()
    q_item.along()

    def input_body(c, carry):
        here = span(c, TALL)

        @pl.when(c == 1)
        def _():
            q_item.inner()
            out_item.outward()

        grad = nt(act[here, : 3 * width], wq[...].reshape(width, 3 * width))
        hat, scale = normalised(x_ref[here, :].astype(f32))
        collect(0, 0, grad * hat)
        collect(1, 0, grad)
        gone[here, :] = (gmid[here, :] + norm_back(grad, gain_one, hat, scale)).astype(bf16)
        pltpu.make_async_copy(gone.at[here, :], gin_any.at[here, :], io_sem.at[1 + rows // TALL + c]).start()
        return carry

    lax.fori_loop(0, rows // TALL, input_body, 0)

    for k, n in enumerate(s.sizes):
        table = one_hot(n)
        row = jnp.sum(vsum[:, starts[k] : starts[k] + n], axis=0, keepdims=True)
        spread = jnp.where(owner_mask(n), jnp.broadcast_to(row, (dp, n)), 0.0).astype(bf16)
        pieces = nt(spread, table)
        if pieces.shape[1] < s.vec_lanes:
            pad = jnp.zeros((dp, s.vec_lanes - pieces.shape[1]), f32)
            pieces = jnp.concatenate([pieces, pad], axis=1)
        vstage[:, k, :] = pieces
    vec_back = []
    for step in range(1, dp):
        target = lax.rem(me + step, dp)
        vec_back.append(
            remote(
                vstage.at[target],
                vback.at[step - 1],
                v_send.at[dp - 2 + step],
                v_recv.at[dp - 2 + step],
                (target, z),
            )
        )
        vec_back[-1].start()
    q_item.outward()
    k_item.along()
    v_item.along()
    for copy in vec_back:
        copy.wait_recv()
    total = vstage[me]
    for step in range(dp - 1):
        total = total + vback[step]
    vz[...] = total
    vec_z = []
    for step in range(1, seq):
        vec_z.append(
            remote(
                vz,
                vzback.at[step - 1],
                v_send.at[2 * dp - 3 + step],
                v_recv.at[2 * dp - 3 + step],
                (me, lax.rem(z + step, seq)),
            )
        )
        vec_z[-1].start()
    k_item.along_again()
    v_item.along_again()
    for item in scatters[:-2]:
        item.finish()
    for copy in vec_z:
        copy.wait_recv()
    terms = [vz[...]] + [vzback[step] for step in range(seq - 1)]
    while len(terms) > 1:
        half = len(terms) // 2
        terms = [terms[i] + terms[i + half] for i in range(half)]
    vec_out[...] = terms[0]
    k_item.finish()
    v_item.finish()

    for c in range(rows // TALL):
        here = pl.ds(c * TALL, TALL)
        pltpu.make_async_copy(gone.at[here, :], gin_any.at[here, :], io_sem.at[1 + rows // TALL + c]).wait()
    drain_states(0, True)
    drain_states(1, False)
    for copy in vec_sends + vec_back + vec_z:
        copy.wait_send()
    for item in scatters:
        item.drain()


def widen_kernel(parts, *refs):
    count = 7
    ins, outs = refs[:count], refs[count : count + 14]
    got, made, in_sem, out_sem = refs[count + 14 :]
    out_in, gin_in, *grads_in, vec_in = ins
    out_out, gin_out, *rest = outs
    rows = out_in.shape[0] // parts
    here = [pl.ds(k * rows, rows) for k in range(parts)]
    loads = [
        [pltpu.make_async_copy(source.at[at], got.at[i, at], in_sem.at[i, k]) for k, at in enumerate(here)]
        for i, source in enumerate((gin_in, out_in))
    ]
    for copy in loads[0] + loads[1]:
        copy.start()
    stores = []
    for k, at in enumerate(here):
        loads[0][k].wait()
        made[at] = got[0, at].astype(f32)
        stores.append(pltpu.make_async_copy(made.at[at], gin_out.at[at], out_sem.at[0, k]))
        stores[-1].start()
    for k, at in enumerate(here):
        loads[1][k].wait()
        stores.append(pltpu.make_async_copy(got.at[1, at], out_out.at[at], out_sem.at[1, k]))
        stores[-1].start()
    for grad, result in zip(grads_in, rest[:4]):
        result[...] = grad[...].astype(f32)
    for k, result in enumerate(rest[4:]):
        result[...] = vec_in[k : k + 1, : result.shape[1]]
    for copy in stores:
        copy.wait()


def widen(s, vectors, results):
    parts = 4
    out, gin, *grads, vec = results
    vmem = pl.BlockSpec(memory_space=pltpu.VMEM)
    anywhere = pl.BlockSpec(memory_space=pl.ANY)
    return pl.pallas_call(
        functools.partial(widen_kernel, parts),
        out_shape=[jax.ShapeDtypeStruct(out.shape, bf16)]
        + [jax.ShapeDtypeStruct(value.shape, f32) for value in (gin, *grads)]
        + [jax.ShapeDtypeStruct((1, v.shape[0]), f32) for v in vectors],
        in_specs=[anywhere] * 2 + [vmem] * 5,
        out_specs=[anywhere] * 2 + [vmem] * 12,
        scratch_shapes=[
            pltpu.VMEM((2,) + out.shape, bf16),
            pltpu.VMEM(out.shape, f32),
            pltpu.SemaphoreType.DMA((2, parts)),
            pltpu.SemaphoreType.DMA((2, parts)),
        ],
        compiler_params=pltpu.CompilerParams(vmem_limit_bytes=63 << 20),
        name="widen",
    )(out, gin, *grads, vec)


def solution(mesh):
    def body(inputs, lengths, cotangent, *params):
        gain_one, shift_one, w_qkv, b_qk, w_out, b_out, gain_two, shift_two, w_up, b_up, w_down, b_down = params
        packs, rows, width = inputs.shape[1:]
        hidden = w_up.shape[1]
        s = Shape(mesh, rows, width, hidden)
        dp, seq, chips, pairs = s.dp, s.seq, s.chips, s.pairs
        nk = chips - 1
        vectors = (gain_one, shift_one, b_qk, b_out, gain_two, shift_two, b_up, b_down)
        vmem = pl.BlockSpec(memory_space=pltpu.VMEM)
        anywhere = pl.BlockSpec(memory_space=pl.ANY)
        grids = [(chips, 2) + shape for shape in s.weights]
        shapes = [(s.weights[index][0], columns) for index, _, columns in s.scatters]
        dma = pltpu.SemaphoreType.DMA
        short = (len(shapes) - 2, len(shapes) - 1) if seq == 4 else range(len(shapes))
        tall = s.weights[0][0]
        message_rows = pairs // 2 * LANES + -(-pairs // 8) * 8
        scratch = (
            [pltpu.VMEM(grid, bf16) for grid in grids]
            + [
                pltpu.VMEM((rows, width), bf16),
                pltpu.VMEM((rows, width), bf16),
                pltpu.VMEM((width, rows), bf16),
                pltpu.VMEM((rows, 3 * width), bf16),
                pltpu.VMEM((rows, 2 * width), f32),
                pltpu.VMEM((s.chunks, CHUNK, CHUNK), bf16),
                pltpu.VMEM((rows, width), f32),
                pltpu.VMEM((pairs, LANES, 2 * LANES), f32),
                pltpu.VMEM((s.chunks, pairs, 2 * LANES, 2 * LANES), bf16),
                pltpu.VMEM((width, rows), bf16),
                pltpu.VMEM((rows, hidden), bf16),
                pltpu.VMEM((rows // (2 * tall), 2, tall, hidden), bf16),
                pltpu.VMEM((rows, width), f32),
                pltpu.VMEM((rows, width), bf16),
                pltpu.VMEM((8, hidden), f32),
                pltpu.VMEM((8, s.vec_lanes), f32),
                pltpu.VMEM((dp, 8, s.vec_lanes), f32),
                pltpu.VMEM((8, sum(s.sizes)), f32),
                pltpu.VMEM((dp, 8, s.vec_lanes), f32),
                pltpu.VMEM((dp - 1, 8, s.vec_lanes), f32),
                pltpu.VMEM((8, s.vec_lanes), f32),
                pltpu.VMEM((seq - 1, 8, s.vec_lanes), f32),
                pltpu.VMEM((2, message_rows, LANES), f32),
                pltpu.VMEM((2, seq - 1, message_rows, LANES), f32),
                [pltpu.VMEM((chips,) + shape, bf16) for shape in shapes[:-3]],
                [pltpu.VMEM((nk,) + shape, bf16) for shape in shapes],
                [pltpu.VMEM(shape, bf16) for shape in shapes],
                [
                    pltpu.VMEM(((seq - 1) * shape[0], shape[1] // seq) if k in short else shape, bf16)
                    for k, shape in enumerate(shapes)
                ],
                [pltpu.VMEM(shape, bf16) for shape in shapes],
                dma((len(s.gathers),)),
                dma((len(s.gathers), nk + 1)),
                dma((len(s.gathers), nk + 1)),
                dma((2 * dp - 2 + seq - 1,)),
                dma((2 * dp - 2 + seq - 1,)),
                dma((2, seq - 1)),
                dma((2, seq - 1)),
                dma((len(s.scatters), nk + 2 * seq - 1)),
                dma((len(s.scatters), nk + 2 * seq - 1)),
                dma((1 + 2 * (rows // TALL),)),
            ]
        )
        outs = pl.pallas_call(
            functools.partial(kernel, s),
            out_shape=(
                jax.ShapeDtypeStruct((rows, width), bf16),
                jax.ShapeDtypeStruct((rows, width), bf16),
            )
            + tuple(jax.ShapeDtypeStruct(shape, bf16) for shape in s.weights)
            + (jax.ShapeDtypeStruct((8, s.vec_lanes), f32),),
            in_specs=[pl.BlockSpec(memory_space=pltpu.SMEM), vmem, anywhere, [vmem] * 8]
            + [anywhere] * 4,
            out_specs=(anywhere, anywhere) + (vmem,) * 5,
            scratch_shapes=scratch,
            compiler_params=pltpu.CompilerParams(
                collective_id=0, has_side_effects=True, vmem_limit_bytes=63 << 20
            ),
            name="layer",
        )(
            lengths.reshape(3),
            inputs.reshape(rows, width),
            cotangent.reshape(rows, width),
            [v.reshape(-1, min(v.shape[0], LANES)) for v in vectors],
            w_qkv,
            w_out,
            w_up,
            w_down,
        )
        out, gin, *grads = widen(s, vectors, outs)
        g_qkv, g_out, g_up, g_down, *pieces = grads
        pieces = [piece.reshape(piece.shape[1]) for piece in pieces]
        return (
            out.reshape(inputs.shape),
            gin.reshape(inputs.shape),
            pieces[0],
            pieces[1],
            g_qkv,
            pieces[2],
            g_out,
            pieces[3],
            pieces[4],
            pieces[5],
            g_up,
            pieces[6],
            g_down,
            pieces[7],
        )

    rows_spec = P("dp", None, "seq", None)
    one, two = P("dp"), P("dp", None)
    params = (one, one, two, one, two, one, one, one, two, one, two, one)
    return jax.shard_map(
        body,
        mesh=mesh,
        in_specs=(rows_spec, P("dp", None, None), rows_spec) + params,
        out_specs=(rows_spec, rows_spec) + params,
        check_vma=False,
    )
```

```python
import functools

import jax
import jax.numpy as jnp
from jax import lax
from jax.experimental import pallas as pl
from jax.experimental.pallas import tpu as pltpu
from jax.sharding import PartitionSpec as P

HEADS = 8
CHUNK = 256
TALL = 640
LANES = 128
eps_norm = 1e-05
eps_attn = 1e-06
MESH = pl.DeviceIdType.MESH
f32 = jnp.float32
bf16 = jnp.bfloat16


def dot(a, b, ca, cb):
    return lax.dot_general(a, b, (((ca,), (cb,)), ((), ())), preferred_element_type=f32)


def nn(a, b):
    return dot(a, b, 1, 0)


def nt(a, b):
    return dot(a, b, 1, 1)


def tn(a, b):
    return dot(a, b, 0, 0)


def span(index, size):
    return pl.ds(pl.multiple_of(index * size, size), size)


def lanes_of(shape):
    return lax.broadcasted_iota(jnp.int32, shape, len(shape) - 1)


def rows_of(shape):
    return lax.broadcasted_iota(jnp.int32, shape, len(shape) - 2)


def fold_rows(values):
    rows, width = values.shape
    return jnp.sum(values.reshape(rows // 8, 8, width), axis=0)


def normalised(values):
    width = values.shape[-1]
    mean = jnp.sum(values, axis=-1, keepdims=True) * (1.0 / width)
    centred = values - mean
    variance = jnp.sum(centred * centred, axis=-1, keepdims=True) * (1.0 / width)
    scale = lax.rsqrt(variance + eps_norm)
    return centred * scale, scale


def norm_back(grad, gain, hat, scale):
    width = grad.shape[-1]
    a = grad * gain
    mean_a = jnp.sum(a, axis=-1, keepdims=True) * (1.0 / width)
    mean_ah = jnp.sum(a * hat, axis=-1, keepdims=True) * (1.0 / width)
    return (a - mean_a - hat * mean_ah) * scale


def gelu_pair(x):
    cdf = 0.5 + 0.5 * lax.erf(x * 0.7071067811865476)
    return x * cdf, cdf + x * (0.3989422804014327 * jnp.exp2(x * x * -0.7213475204444817))


class Shape:
    def __init__(self, mesh, rows, width, hidden):
        self.dp = mesh.shape["dp"]
        self.seq = mesh.shape["seq"]
        self.chips = self.dp // 2
        self.side = max(k for k in range(1, self.chips + 1) if k * k <= self.chips and self.chips % k == 0)
        self.rows, self.width, self.hidden = rows, width, hidden
        self.chunks = rows // CHUNK
        self.pairs = width // LANES
        self.sizes = (width, width, 2 * width, width, width, width, hidden, width)
        self.vec_lanes = max(-(-n // self.dp // LANES) * LANES for n in self.sizes)
        w, h, d = width, hidden, self.dp
        self.weights = ((w // d, 3 * w), (w // d, w), (w // d, h), (h // d, w))
        self.gathers = (
            (0, w, w),
            (0, 2 * w, w),
            (0, 0, w),
            (3, 0, w),
            (1, 0, w),
        ) + tuple((2, t * (h // 4), h // 4) for t in range(4))
        self.scatters = tuple((2, t * (h // 4), h // 4) for t in range(4)) + (
            (3, 0, w),
            (1, 0, w),
            (0, 0, w),
            (0, w, w),
            (0, 2 * w, w),
        )


def kernel(
    s,
    lengths,
    x_ref,
    cot_any,
    vec_refs,
    wq_any,
    wo_any,
    wu_any,
    wd_any,
    out_any,
    gin_any,
    gq_out,
    go_out,
    gu_out,
    gd_out,
    vec_out,
    wq,
    wo,
    wu,
    wd,
    cot,
    n1,
    n1t,
    feat,
    acc,
    mask,
    state_in,
    state,
    state_b,
    n2t,
    act,
    hgrad,
    gmid,
    gone,
    vecs,
    vec_ref,
    vgot,
    vsum,
    vstage,
    vback,
    vz,
    vzback,
    msg,
    msg_in,
    rb0,
    rb1,
    zsrc,
    zr1,
    zr2,
    g_local,
    g_send,
    g_recv,
    v_send,
    v_recv,
    m_send,
    m_recv,
    r_send,
    r_recv,
    io_sem,
):
    dp, seq, chips, side = s.dp, s.seq, s.chips, s.side
    rows, width, hidden = s.rows, s.width, s.hidden
    me, z = lax.axis_index("dp"), lax.axis_index("seq")
    core, chip = lax.rem(me, 2), me // 2
    cy, cx = chip // side, lax.rem(chip, side)
    offsets = [(dy, dx) for dy in range(chips // side) for dx in range(side)][1:]

    def chip_at(dy, dx):
        ny = chips // side
        return lax.rem(cy + dy + ny, ny) * side + lax.rem(cx + dx + side, side)

    heard, dnum, stage_q = n1, cot, hgrad

    sibling = (chip * 2 + 1 - core, z)
    peers = [(chip_at(dy, dx) * 2 + core, z) for dy, dx in offsets]
    z_up, z_down = lax.rem(z + 1, seq), lax.rem(z + seq - 1, seq)

    def remote(src, dst, send, recv, device):
        return pltpu.make_async_remote_copy(
            src_ref=src,
            dst_ref=dst,
            send_sem=send,
            recv_sem=recv,
            device_id=device,
            device_id_type=MESH,
        )

    barrier = pltpu.get_barrier_semaphore()
    for step in range(1, dp):
        pl.semaphore_signal(
            barrier, inc=1, device_id=(lax.rem(me + step, dp), z), device_id_type=MESH
        )
    for step in range(1, seq):
        pl.semaphore_signal(
            barrier, inc=1, device_id=(me, lax.rem(z + step, seq)), device_id_type=MESH
        )
    pl.semaphore_wait(barrier, dp + seq - 2)

    vec_ref[...] = jnp.zeros_like(vec_ref)
    for k, ref in enumerate(vec_refs):
        lanes = ref.shape[1]
        for row in range(ref.shape[0]):
            vec_ref[k : k + 1, row * lanes : (row + 1) * lanes] = ref[row : row + 1, :].astype(f32)
    vec_sends = []
    for step in range(1, dp):
        vec_sends.append(
            remote(
                vec_ref,
                vgot.at[me],
                v_send.at[step - 1],
                v_recv.at[step - 1],
                (lax.rem(me + step, dp), z),
            )
        )
        vec_sends[-1].start()
    vgot[me] = vec_ref[...]

    sources = (wq_any, wo_any, wu_any, wd_any)
    weights = (wq, wo, wu, wd)
    nk = len(peers)

    class Gather:
        def __init__(self, item):
            index, first, columns = s.gathers[item]
            self.buffer, self.source = weights[index], sources[index]
            self.columns = pl.ds(first, columns)
            self.send, self.recv, self.local = g_send.at[item], g_recv.at[item], g_local.at[item]

        def start(self):
            src = self.source.at[:, self.columns]
            dst = self.buffer.at[chip, core, :, self.columns]
            self.own = pltpu.make_async_copy(src, dst, self.local)
            self.own.start()
            self.plane = [
                remote(src, dst, self.send.at[k], self.recv.at[k], peer)
                for k, peer in enumerate(peers)
            ]
            for copy in self.plane:
                copy.start()

        def hand_on(self):
            self.own.wait()
            for copy in self.plane:
                copy.wait_recv()
            mine = self.buffer.at[:, core, :, self.columns]
            self.across = remote(mine, mine, self.send.at[nk], self.recv.at[nk], sibling)
            self.across.start()

        def finish(self):
            theirs = self.buffer.at[:, 1 - core, :, self.columns]
            remote(theirs, theirs, self.send.at[nk], self.recv.at[nk], sibling).wait_recv()

        def drain(self):
            for copy in self.plane + [self.across]:
                copy.wait_send()

    gathers = [Gather(item) for item in range(len(s.gathers))]
    for item in range(3):
        gathers[item].start()
    cot_copy = pltpu.make_async_copy(cot_any, cot, io_sem.at[0])
    cot_copy.start()

    bound_0 = lengths[0]
    bound_1 = bound_0 + lengths[1]
    bound_2 = bound_1 + lengths[2]
    first_row = z * rows

    def segment(position):
        return sum((position >= bound).astype(jnp.int32) for bound in (bound_0, bound_1, bound_2))

    def same(a, b):
        return (a == b).astype(f32)

    prior = jnp.where(first_row > 0, segment(first_row - 1), -1)
    last = segment(first_row + rows - 1)

    def before(c):
        return jnp.where(first_row + c * CHUNK > 0, segment(first_row + c * CHUNK - 1), -1)

    def ending(c):
        return segment(first_row + (c + 1) * CHUNK - 1)

    def in_segment(c, which):
        shape = (CHUNK, LANES)
        return (segment(first_row + c * CHUNK + rows_of(shape)) == which).astype(f32)

    square = (CHUNK, CHUNK)
    pair = (LANES, LANES)
    lane_low = lanes_of((CHUNK, LANES)) < 64
    block_diag = (
        (lanes_of((LANES, 2 * LANES)) // 64) % 2 == rows_of((LANES, 2 * LANES)) // 64
    ).astype(f32)
    low_pair = lanes_of(pair) < 64
    diagonal = lanes_of(pair) == rows_of(pair)
    low_half = (lanes_of(pair) & 63) < 32
    ones_low = lane_low.astype(bf16)
    ones_high = 1.0 - ones_low

    def mask_body(c, carry):
        down, across = rows_of(square), lanes_of(square)
        base = first_row + c * CHUNK
        alike = segment(base + down) == segment(base + across)
        mask[c] = (alike & (across <= down)).astype(f32).astype(bf16)
        return carry

    lax.fori_loop(0, s.chunks, mask_body, 0)

    for step in range(1, dp):
        source = lax.rem(me - step + dp, dp)
        remote(
            vec_ref, vgot.at[source], v_send.at[step - 1], v_recv.at[step - 1], (source, z)
        ).wait_recv()

    def one_hot(n):
        piece = n // dp
        tall = -(-piece // LANES) * LANES
        shape = (tall, n)
        return ((lanes_of(shape) & (piece - 1)) == rows_of(shape)).astype(f32).astype(bf16)

    def owner_mask(n):
        piece = n // dp
        shape = (dp, n)
        low = rows_of(shape) * piece
        return (lanes_of(shape) >= low) & (lanes_of(shape) < low + piece)

    for k, n in enumerate(s.sizes):
        table = one_hot(n)
        pieces = vgot[:, k, : table.shape[0]].astype(bf16)
        spread = jnp.where(owner_mask(n), nn(pieces, table), 0.0)
        vecs[k : k + 1, :n] = jnp.sum(spread, axis=0, keepdims=True)

    starts = [sum(s.sizes[:k]) for k in range(len(s.sizes))]

    def collect(k, first, values):
        at = starts[k] + first
        vsum[:, at : at + values.shape[1]] += fold_rows(values)

    gain_one, shift_one = vecs[0:1, :width], vecs[1:2, :width]
    for k, n in enumerate(s.sizes):
        vsum[:, starts[k] : starts[k] + n] = jnp.zeros((8, n), f32)

    def norm_body(c, carry):
        here = span(c, CHUNK)
        hat, _ = normalised(x_ref[here, :].astype(f32))
        normed = (hat * gain_one + shift_one).astype(bf16)
        n1[here, :] = normed
        n1t[:, here] = normed.T
        return carry

    lax.fori_loop(0, s.chunks, norm_body, 0)

    get_down, get_out = gathers[3:5]
    get_up = gathers[5:]

    def project(get, part):
        get.finish()
        cols = slice(part * width, (part + 1) * width)
        weight = wq[:, :, :, cols].reshape(width, width)

        def project_body(c, carry):
            here = span(c, TALL)
            mixed = nn(n1[here, :], weight)
            if part < 2:
                mixed = mixed + vecs[2:3, cols]
                mixed = jnp.where(mixed > 0.0, mixed + 1.0, jnp.exp(jnp.minimum(mixed, 0.0)))
            feat[here, cols] = mixed.astype(bf16)
            return carry

        lax.fori_loop(0, rows // TALL, project_body, 0)

    gathers[0].hand_on()
    get_down.start()
    gathers[1].hand_on()
    get_out.start()
    project(gathers[0], 1)
    project(gathers[1], 2)

    def cut(here, part, p):
        first = part * width + p * LANES
        return feat[here, first : first + LANES]

    for p in range(s.pairs):
        state[p] = jnp.zeros((LANES, 2 * LANES), f32)

    def state_at(c, p):
        first = pl.multiple_of(c * (s.pairs // 2 * LANES), LANES) + p // 2 * LANES
        return pl.ds(first, LANES), slice(p % 2 * 2 * LANES, (p % 2 + 1) * 2 * LANES)

    def state_body(c, carry):
        here = span(c, CHUNK)
        keep = same(ending(c), before(c))
        chosen = in_segment(c, ending(c)).astype(bf16)
        for p in range(s.pairs):
            wide = jnp.concatenate([cut(here, 2, p) * chosen, chosen], axis=1)
            now = state[p]
            state_in[state_at(c, p)] = now
            state[p] = keep * now + tn(cut(here, 1, p), wide) * block_diag
        return carry

    lax.fori_loop(0, s.chunks, state_body, 0)

    def spread_ends(right):
        return 0.5 * (right + pltpu.roll(right, 32, 1))

    def packed(slot):
        halves = []
        ends = []
        for p in range(s.pairs):
            left = state[p, :, :LANES]
            right = state[p, :, LANES:]
            halves.append(left + pltpu.roll(left, 64, 1))
            ends.append(spread_ends(right + pltpu.roll(right, 64, 1)))
        for q in range(s.pairs // 2):
            msg[slot, q * LANES : (q + 1) * LANES] = jnp.where(
                low_pair, halves[2 * q], halves[2 * q + 1]
            )
        ends = [jnp.sum(jnp.where(diagonal, end, 0.0), axis=0, keepdims=True) for end in ends]
        ends.append(jnp.zeros((msg.shape[1] - s.pairs // 2 * LANES - s.pairs, LANES), f32))
        msg[slot, s.pairs // 2 * LANES :] = jnp.concatenate(ends, axis=0)

    def unpacked(slot, step, p):
        sums = msg_in[slot, step, p // 2 * LANES : (p // 2 + 1) * LANES]
        turned = pltpu.roll(sums, 64, 1)
        left = jnp.where(low_pair, sums, turned) if p % 2 == 0 else jnp.where(low_pair, turned, sums)
        first = s.pairs // 2 * LANES + p
        ends = jnp.where(diagonal, msg_in[slot, step, first : first + 1], 0.0)
        right = jnp.sum(ends, axis=1, keepdims=True)
        return jnp.concatenate([left, jnp.broadcast_to(right, pair)], axis=1) * block_diag

    def message(slot, step, forward):
        target = lax.rem(z + step, seq) if forward else lax.rem(z - step + seq, seq)
        return remote(
            msg.at[slot],
            msg_in.at[slot, step - 1],
            m_send.at[slot, step - 1],
            m_recv.at[slot, step - 1],
            (me, target),
        )

    def send_states(slot, forward):
        packed(slot)
        for step in range(1, seq):

            @pl.when((z + step < seq) if forward else (z - step >= 0))
            def _():
                message(slot, step, forward).start()

    def take_states(slot, forward):
        for p in range(s.pairs):
            state[p] = jnp.zeros((LANES, 2 * LANES), f32)
        for step in range(1, seq):

            @pl.when((z - step >= 0) if forward else (z + step < seq))
            def _():
                message(slot, step, forward).wait_recv()
                if forward:
                    weight = same(segment((z - step + 1) * rows - 1), prior)
                else:
                    weight = same(segment((z + step) * rows - 1), last)
                for p in range(s.pairs):
                    state[p] = state[p] + weight * unpacked(slot, step - 1, p)

    def drain_states(slot, forward):
        for step in range(1, seq):

            @pl.when((z + step < seq) if forward else (z - step >= 0))
            def _():
                message(slot, step, forward).wait_send()

    send_states(0, True)
    gathers[2].hand_on()
    get_up[0].start()
    project(gathers[2], 0)

    def inside_body(c, carry):
        here = span(c, CHUNK)
        seen = mask[c]
        raw = []
        for p in range(s.pairs):
            q, k = cut(here, 0, p), cut(here, 1, p)
            raw.append((nt(q, k * ones_low), nt(q, k * ones_high)))
        for p in range(s.pairs):
            v = cut(here, 2, p)
            scores = jnp.concatenate([part.astype(bf16) * seen for part in raw[p]], axis=1)
            low = jnp.concatenate([v * ones_low, ones_low], axis=1)
            high = jnp.concatenate([v * ones_high, ones_high], axis=1)
            acc[here, 2 * p * LANES : (2 * p + 2) * LANES] = nn(
                scores, jnp.concatenate([low, high], axis=0)
            )
        return carry

    lax.fori_loop(0, s.chunks, inside_body, 0)
    get_down.hand_on()
    get_up[1].start()
    get_out.hand_on()
    get_up[2].start()
    get_down.finish()
    cot_copy.wait()

    tile = hidden // 4
    tall = s.weights[0][0]
    per = chips // 4
    blocks = TALL // (2 * tall)

    def hidden_body(c, carry):
        here = span(c, TALL)
        branch = cot[here, :]
        collect(7, 0, branch.astype(f32))
        for t in range(4):
            down = wd[t * per : (t + 1) * per].reshape(tile, width)
            grad = nt(branch, down).astype(bf16).reshape(blocks, 2, tall, tile)
            hgrad[span(c, blocks), :, :, t * tile : (t + 1) * tile] = grad
        return carry

    lax.fori_loop(0, rows // TALL, hidden_body, 0)
    get_up[0].hand_on()
    get_up[3].start()
    take_states(0, True)

    def join_body(c, carry):
        here = span(c, CHUNK)
        live = in_segment(c, before(c))
        carried = same(before(c), prior)
        for p in range(s.pairs):
            whole = state_in[state_at(c, p)] + carried * state[p]
            upper = whole.astype(bf16)
            lower = (whole - upper.astype(f32)).astype(bf16)
            state_b[c, p, :LANES] = upper
            state_b[c, p, LANES:] = lower
            q = cut(here, 0, p)
            extra = nn(jnp.concatenate([q, q], axis=1), state_b[c, p])
            first = 2 * p * LANES
            numerator = acc[here, first : first + LANES] + live * extra[:, :LANES]
            denominator = acc[here, first + LANES : first + 2 * LANES] + live * extra[:, LANES:]
            inverse = 1.0 / (denominator + eps_attn)
            result = numerator * inverse
            acc[here, first : first + LANES] = result
            acc[here, first + LANES : first + 2 * LANES] = inverse
            heard[here, p * LANES : (p + 1) * LANES] = result.astype(bf16)
        return carry

    lax.fori_loop(0, s.chunks, join_body, 0)
    get_out.finish()
    get_up[1].hand_on()

    bias_out, gain_two, shift_two = (vecs[k : k + 1, :width] for k in (3, 4, 5))
    bias_down = vecs[7:8, :width]
    total = state_in

    def middle_of(here):
        projected = nn(heard[here, :], wo[...].reshape(width, width))
        return x_ref[here, :].astype(f32) + projected + bias_out

    def middle_body(c, carry):
        here = span(c, TALL)
        middle = middle_of(here)
        hat, _ = normalised(middle)
        n2t[:, here] = (hat * gain_two + shift_two).astype(bf16).T
        total[here, :] = middle + bias_down
        return carry

    lax.fori_loop(0, rows // TALL, middle_body, 0)

    outer = (z == 0) | (z == seq - 1)
    inward = jnp.where(z < seq // 2, z + 1, z - 1)
    outward = jnp.where(z < seq // 2, z - 1, z + 1)
    across = seq - 1 - z
    stages = (stage_q, wo, wu, wd)
    results = (gq_out, go_out, gu_out, gd_out)

    class Scatter:
        def __init__(self, item):
            index, first, columns = s.scatters[item]
            self.stage, self.result = stages[index], results[index]
            self.first, self.count, self.height = first, columns, s.weights[index][0]
            self.cols = pl.ds(first, columns)
            shared = item - len(s.scatters) + 3
            self.rb0 = rb0[shared if shared >= 0 else item]
            self.rb1 = rb1[item]
            self.zsrc, self.zr1, self.zr2 = zsrc[item], zr1[item], zr2[item]
            self.part = columns // seq
            self.short = seq != 4 or item >= len(s.scatters) - 2
            self.send, self.recv = r_send.at[item], r_recv.at[item]

        def across(self):
            return remote(
                self.stage.at[pl.ds(0, chips), 1 - core, :, self.cols],
                self.rb0,
                self.send.at[0],
                self.recv.at[0],
                sibling,
            )

        def sends(self):
            return [
                remote(
                    self.stage.at[peer[0] // 2, core, :, self.cols],
                    self.rb1.at[k],
                    self.send.at[1 + k],
                    self.recv.at[1 + k],
                    peer,
                )
                for k, peer in enumerate(peers)
            ]

        def quarters(self):
            return [
                remote(
                    self.zsrc.at[:, span(lax.rem(z + step, seq), self.part)],
                    self.zr1.at[pl.ds((step - 1) * self.height, self.height)],
                    self.send.at[nk + step],
                    self.recv.at[nk + step],
                    (me, lax.rem(z + step, seq)),
                )
                for step in range(1, seq)
            ]

        def totals(self, arriving=False):
            copies = []
            for step in range(1, seq):
                owner = lax.rem(z - step + seq, seq) if arriving else z
                piece = self.zr2.at[:, span(owner, self.part)]
                k = nk + seq - 1 + step
                target = (me, lax.rem(z + step, seq))
                copies.append(remote(piece, piece, self.send.at[k], self.recv.at[k], target))
            return copies

        def start(self):
            self.across().start()

        def plane(self):
            self.across().wait_recv()

            def add(k, carry):
                here = (k, core, slice(None), self.cols)
                self.stage[here] = (
                    self.stage[here].astype(f32) + self.rb0[k].astype(f32)
                ).astype(bf16)
                return carry

            lax.fori_loop(0, chips, add, 0)
            for copy in self.sends():
                copy.start()

        def along(self):
            for copy in self.sends():
                copy.wait_recv()
            total = self.stage[chip, core, :, self.cols].astype(f32)
            for k in range(nk):
                total = total + self.rb1[k].astype(f32)
            self.zsrc[...] = total.astype(bf16)
            if self.short:
                for copy in self.quarters():
                    copy.start()
            else:

                @pl.when(outer)
                def _():
                    self.step(0).start()

        def step(self, k):
            source, target = ((self.zsrc, self.zr1), (self.zsrc, self.zr2), (self.zsrc, self.zr2))[k]
            there = (inward, across, outward)[k]
            return remote(
                source, target, self.send.at[nk + 1 + k], self.recv.at[nk + 1 + k], (me, there)
            )

        def inner(self):
            @pl.when(jnp.logical_not(outer))
            def _():
                self.step(0).wait_recv()
                total = self.zsrc[...].astype(f32) + self.zr1[...].astype(f32)
                self.zsrc[...] = total.astype(bf16)
                self.step(1).start()

        def outward(self):
            @pl.when(jnp.logical_not(outer))
            def _():
                self.step(1).wait()
                total = self.zsrc[...].astype(f32) + self.zr2[...].astype(f32)
                self.zsrc[...] = total.astype(bf16)
                self.step(2).start()

        def along_again(self):
            for copy in self.quarters():
                copy.wait_recv()
            mine = span(z, self.part)
            total = self.zsrc[:, mine].astype(f32)
            for step in range(seq - 1):
                total = total + self.zr1[step * self.height : (step + 1) * self.height].astype(f32)
            self.zr2[:, mine] = total.astype(bf16)
            for copy in self.totals():
                copy.start()

        def finish(self):
            if self.short:
                for copy in self.totals(True):
                    copy.wait_recv()
                self.result[:, self.cols] = self.zr2[...]
            else:

                @pl.when(outer)
                def _():
                    self.step(2).wait_recv()
                    self.result[:, self.cols] = self.zr2[...]

                @pl.when(jnp.logical_not(outer))
                def _():
                    self.result[:, self.cols] = self.zsrc[...]

        def drain(self):
            for copy in [self.across()] + self.sends():
                copy.wait_send()
            if self.short:
                for copy in self.quarters() + self.totals():
                    copy.wait_send()
            else:

                @pl.when(outer)
                def _():
                    self.step(0).wait_send()

                @pl.when(jnp.logical_not(outer))
                def _():
                    self.step(2).wait_send()

    scatters = [Scatter(item) for item in range(len(s.scatters))]
    up_items, down_item, out_item = scatters[:4], scatters[4], scatters[5]
    q_item, k_item, v_item = scatters[6:]

    for t in range(4):
        if t == 1:
            get_up[2].hand_on()
        if t == 2:
            get_up[3].hand_on()
        get_up[t].finish()
        cols = slice(t * tile, (t + 1) * tile)

        up = wu[:, :, :, cols].reshape(width, tile)
        down = wd[t * per : (t + 1) * per].reshape(tile, width)
        active, slope = gelu_pair(tn(n2t[...], up) + vecs[6:7, cols])
        active = active.astype(bf16)
        act[:, cols] = active
        grad = slope * hgrad[:, :, :, cols].reshape(rows, tile).astype(f32)
        grad = grad.astype(bf16)
        hgrad[:, :, :, cols] = grad.reshape(rows // (2 * tall), 2, tall, tile)
        collect(6, t * tile, grad.astype(f32))
        total[...] += nn(active, down)
        back = nt(grad, up)
        gmid[...] = back if t == 0 else gmid[...] + back
        get_up[t].drain()
        if t == 0:
            get_down.drain()
        grad = nn(n2t[...], hgrad[:, :, :, cols].reshape(rows, tile)).astype(bf16)
        wu[:, :, :, cols] = grad.reshape(chips, 2, width // dp, tile)
        up_items[t].start()
        grad = tn(act[:, cols], cot[...]).astype(bf16)
        wd[t * per : (t + 1) * per] = grad.reshape(per, 2, hidden // dp, width)
        if t > 0:
            up_items[t - 1].plane()
        if t == 3:
            down_item.start()

    def output_copy(c):
        here = span(c, TALL)
        return pltpu.make_async_copy(gone.at[here, :], out_any.at[here, :], io_sem.at[1 + c])

    def second_body(c, carry):
        here = span(c, TALL)
        gone[here, :] = total[here, :].astype(bf16)
        output_copy(c).start()
        hat, scale = normalised(middle_of(here))
        back = gmid[here, :]
        collect(4, 0, back * hat)
        collect(5, 0, back)
        gmid[here, :] = cot[here, :].astype(f32) + norm_back(back, gain_two, hat, scale)
        return carry

    lax.fori_loop(0, rows // TALL, second_body, 0)
    for gather in gathers[:3] + [get_out]:
        gather.drain()
    up_items[3].plane()
    down_item.plane()
    up_items[0].along()
    up_items[1].along()

    bd_square = block_diag[:, :LANES].astype(bf16)
    head_sum = jnp.concatenate([bd_square, bd_square], axis=0)
    lane_hi = (lanes_of((CHUNK, LANES)) & 63) < 32

    def heads_body(c, carry):
        here = span(c, CHUNK)
        low = gmid[here, :].astype(bf16)
        gone[here, :] = low
        collect(3, 0, low.astype(f32))
        back = nt(low, wo[...].reshape(width, width)).astype(bf16).astype(f32)
        for p in range(s.pairs):
            first = 2 * p * LANES
            result = acc[here, first : first + LANES]
            inverse = acc[here, first + LANES : first + 2 * LANES]
            grad = back[:, p * LANES : (p + 1) * LANES]
            dnum[here, p * LANES : (p + 1) * LANES] = (grad * inverse).astype(bf16)
            product = grad * result
            upper = product.astype(bf16)
            lower = (product - upper.astype(f32)).astype(bf16)
            total = nn(jnp.concatenate([upper, lower], axis=1), head_sum)
            value = total * inverse * (-1.0 / 32.0)
            upper = value.astype(bf16)
            lower = value - upper.astype(f32)
            act[here, 3 * width + p * LANES : 3 * width + (p + 1) * LANES] = jnp.where(
                lane_hi, upper.astype(f32), lower
            ).astype(bf16)
        return carry

    for c in range(rows // TALL):
        output_copy(c).wait()
    lax.fori_loop(0, s.chunks, heads_body, 0)

    def grads_of(here, p):
        first = 3 * width + p * LANES
        return dnum[here, p * LANES : (p + 1) * LANES], act[here, first : first + LANES]

    for p in range(s.pairs):
        state[p] = jnp.zeros((LANES, 2 * LANES), f32)

    def gstate_body(step, carry):
        c = s.chunks - 1 - step
        here = span(c, CHUNK)
        keep = same(ending(c), before(c))
        live = in_segment(c, before(c)).astype(bf16)
        for p in range(s.pairs):
            now = state[p]
            state_in[state_at(c, p)] = now
            wide = jnp.concatenate(grads_of(here, p), axis=1)
            state[p] = keep * now + tn(cut(here, 0, p) * live, wide) * block_diag
        return carry

    up_items[0].inner()
    up_items[1].inner()
    up_items[2].along()
    lax.fori_loop(0, s.chunks, gstate_body, 0)
    send_states(1, False)

    wo[...] = tn(heard[...], gone[...]).astype(bf16).reshape(chips, 2, width // dp, width)
    out_item.start()
    up_items[0].outward()
    up_items[1].outward()
    up_items[3].along()

    def keep_grad(here, part, p, grad, feature):
        first = part * width + p * LANES
        slope = jnp.minimum(feature.astype(f32), 1.0)
        grad = (grad.astype(bf16).astype(f32) * slope).astype(bf16)
        collect(2, first, grad.astype(f32))
        act[here, first : first + LANES] = grad

    def back_body(c, carry):
        here = span(c, CHUNK)
        for at, work in (
            (0, out_item.plane),
            (4, down_item.along),
        ):
            pl.when(c == min(at, s.chunks - 1))(work)
        seen = mask[c]
        live = in_segment(c, before(c))
        raw = []
        extra = []
        for p in range(s.pairs):
            v = cut(here, 2, p)
            wide = jnp.concatenate(grads_of(here, p), axis=1)
            low = jnp.concatenate([v * ones_low, ones_low], axis=1)
            high = jnp.concatenate([v * ones_high, ones_high], axis=1)
            raw.append((nt(wide, low), nt(wide, high)))
            extra.append(nt(wide, state_b[c, p, :LANES]) + nt(wide, state_b[c, p, LANES:]))
        for p in range(s.pairs):
            q, k = cut(here, 0, p), cut(here, 1, p)
            low, high = (part.astype(bf16) * seen for part in raw[p])
            gq = live * extra[p] + nn(
                jnp.concatenate([low, high], axis=1),
                jnp.concatenate([k * ones_low, k * ones_high], axis=0),
            )
            first = width + p * LANES
            acc[here, first : first + LANES] = tn(
                jnp.concatenate([low, high], axis=0),
                jnp.concatenate([q * ones_low, q * ones_high], axis=0),
            )
            keep_grad(here, 0, p, gq, q)
        return carry

    lax.fori_loop(0, s.chunks, back_body, 0)

    def projection_grad(part):
        cols = slice(part * width, (part + 1) * width)
        grad = nn(n1t[...], act[:, cols]).astype(bf16)
        stage_q[:chips, :, :, cols] = grad.reshape(chips, 2, width // dp, width)

    projection_grad(0)
    q_item.start()


    def value_body(c, carry):
        here = span(c, CHUNK)
        seen_t = mask[c].T
        raw = []
        for p in range(s.pairs):
            q, k = cut(here, 0, p), cut(here, 1, p)
            raw.append((nt(k * ones_low, q), nt(k * ones_high, q)))
        for p in range(s.pairs):
            dn, _ = grads_of(here, p)
            scores = jnp.concatenate([part.astype(bf16) * seen_t for part in raw[p]], axis=1)
            acc[here, p * LANES : (p + 1) * LANES] = nn(
                scores, jnp.concatenate([dn * ones_low, dn * ones_high], axis=0)
            )
        return carry

    lax.fori_loop(0, s.chunks, value_body, 0)
    q_item.plane()
    out_item.along()
    take_states(1, False)

    def ahead_body(c, carry):
        here = span(c, CHUNK)
        chosen = in_segment(c, ending(c))
        carried = same(ending(c), last)
        for p in range(s.pairs):
            ahead = state_in[state_at(c, p)] + carried * state[p]
            sums = ahead[:, LANES:]
            sums = 2.0 * spread_ends(sums + pltpu.roll(sums, 64, 1)) * block_diag[:, LANES:]
            upper = sums.astype(bf16).astype(f32)
            sums = jnp.where(low_half, upper, sums - upper)
            ahead = jnp.concatenate([ahead[:, :LANES], sums], axis=1)
            upper = ahead.astype(bf16)
            lower = (ahead - upper.astype(f32)).astype(bf16)
            k, v = cut(here, 1, p), cut(here, 2, p)
            both = jnp.concatenate([v, jnp.ones_like(v)], axis=1)
            first = width + p * LANES
            grad = acc[here, first : first + LANES] + chosen * (
                nt(both, upper) + nt(v, lower[:, :LANES])
            )
            keep_grad(here, 1, p, grad, k)
            grad = acc[here, p * LANES : (p + 1) * LANES] + chosen * nn(
                k, upper[:, :LANES]
            )
            first = 2 * width + p * LANES
            act[here, first : first + LANES] = grad.astype(bf16)
        return carry

    lax.fori_loop(0, s.chunks, ahead_body, 0)
    up_items[2].inner()
    up_items[3].inner()
    projection_grad(1)
    k_item.start()
    down_item.inner()
    projection_grad(2)
    v_item.start()
    out_item.inner()
    up_items[2].outward()
    up_items[3].outward()
    k_item.plane()
    v_item.plane()
    down_item.outward()
    q_item.along()

    def input_body(c, carry):
        here = span(c, TALL)

        @pl.when(c == 1)
        def _():
            q_item.inner()
            out_item.outward()

        grad = nt(act[here, : 3 * width], wq[...].reshape(width, 3 * width))
        hat, scale = normalised(x_ref[here, :].astype(f32))
        collect(0, 0, grad * hat)
        collect(1, 0, grad)
        gone[here, :] = (gmid[here, :] + norm_back(grad, gain_one, hat, scale)).astype(bf16)
        pltpu.make_async_copy(gone.at[here, :], gin_any.at[here, :], io_sem.at[1 + rows // TALL + c]).start()
        return carry

    lax.fori_loop(0, rows // TALL, input_body, 0)

    for k, n in enumerate(s.sizes):
        table = one_hot(n)
        row = jnp.sum(vsum[:, starts[k] : starts[k] + n], axis=0, keepdims=True)
        spread = jnp.where(owner_mask(n), jnp.broadcast_to(row, (dp, n)), 0.0).astype(bf16)
        pieces = nt(spread, table)
        if pieces.shape[1] < s.vec_lanes:
            pad = jnp.zeros((dp, s.vec_lanes - pieces.shape[1]), f32)
            pieces = jnp.concatenate([pieces, pad], axis=1)
        vstage[:, k, :] = pieces
    vec_back = []
    for step in range(1, dp):
        target = lax.rem(me + step, dp)
        vec_back.append(
            remote(
                vstage.at[target],
                vback.at[step - 1],
                v_send.at[dp - 2 + step],
                v_recv.at[dp - 2 + step],
                (target, z),
            )
        )
        vec_back[-1].start()
    q_item.outward()
    k_item.along()
    v_item.along()
    for copy in vec_back:
        copy.wait_recv()
    total = vstage[me]
    for step in range(dp - 1):
        total = total + vback[step]
    vz[...] = total
    vec_z = []
    for step in range(1, seq):
        vec_z.append(
            remote(
                vz,
                vzback.at[step - 1],
                v_send.at[2 * dp - 3 + step],
                v_recv.at[2 * dp - 3 + step],
                (me, lax.rem(z + step, seq)),
            )
        )
        vec_z[-1].start()
    k_item.along_again()
    v_item.along_again()
    for item in scatters[:-2]:
        item.finish()
    for copy in vec_z:
        copy.wait_recv()
    terms = [vz[...]] + [vzback[step] for step in range(seq - 1)]
    while len(terms) > 1:
        half = len(terms) // 2
        terms = [terms[i] + terms[i + half] for i in range(half)]
    vec_out[...] = terms[0]
    k_item.finish()
    v_item.finish()

    for c in range(rows // TALL):
        here = pl.ds(c * TALL, TALL)
        pltpu.make_async_copy(gone.at[here, :], gin_any.at[here, :], io_sem.at[1 + rows // TALL + c]).wait()
    drain_states(0, True)
    drain_states(1, False)
    for copy in vec_sends + vec_back + vec_z:
        copy.wait_send()
    for item in scatters:
        item.drain()


def widen_kernel(parts, *refs):
    count = 7
    ins, outs = refs[:count], refs[count : count + 14]
    got, made, in_sem, out_sem = refs[count + 14 :]
    out_in, gin_in, *grads_in, vec_in = ins
    out_out, gin_out, *rest = outs
    rows = out_in.shape[0] // parts
    here = [pl.ds(k * rows, rows) for k in range(parts)]
    loads = [
        [pltpu.make_async_copy(source.at[at], got.at[i, at], in_sem.at[i, k]) for k, at in enumerate(here)]
        for i, source in enumerate((gin_in, out_in))
    ]
    for copy in loads[0] + loads[1]:
        copy.start()
    stores = []
    for k, at in enumerate(here):
        loads[0][k].wait()
        made[at] = got[0, at].astype(f32)
        stores.append(pltpu.make_async_copy(made.at[at], gin_out.at[at], out_sem.at[0, k]))
        stores[-1].start()
    for k, at in enumerate(here):
        loads[1][k].wait()
        stores.append(pltpu.make_async_copy(got.at[1, at], out_out.at[at], out_sem.at[1, k]))
        stores[-1].start()
    for grad, result in zip(grads_in, rest[:4]):
        result[...] = grad[...].astype(f32)
    for k, result in enumerate(rest[4:]):
        result[...] = vec_in[k : k + 1, : result.shape[1]]
    for copy in stores:
        copy.wait()


def widen(s, vectors, results):
    parts = 4
    out, gin, *grads, vec = results
    vmem = pl.BlockSpec(memory_space=pltpu.VMEM)
    anywhere = pl.BlockSpec(memory_space=pl.ANY)
    return pl.pallas_call(
        functools.partial(widen_kernel, parts),
        out_shape=[jax.ShapeDtypeStruct(out.shape, bf16)]
        + [jax.ShapeDtypeStruct(value.shape, f32) for value in (gin, *grads)]
        + [jax.ShapeDtypeStruct((1, v.shape[0]), f32) for v in vectors],
        in_specs=[anywhere] * 2 + [vmem] * 5,
        out_specs=[anywhere] * 2 + [vmem] * 12,
        scratch_shapes=[
            pltpu.VMEM((2,) + out.shape, bf16),
            pltpu.VMEM(out.shape, f32),
            pltpu.SemaphoreType.DMA((2, parts)),
            pltpu.SemaphoreType.DMA((2, parts)),
        ],
        compiler_params=pltpu.CompilerParams(vmem_limit_bytes=63 << 20),
        name="widen",
    )(out, gin, *grads, vec)


def solution(mesh):
    def body(inputs, lengths, cotangent, *params):
        gain_one, shift_one, w_qkv, b_qk, w_out, b_out, gain_two, shift_two, w_up, b_up, w_down, b_down = params
        packs, rows, width = inputs.shape[1:]
        hidden = w_up.shape[1]
        s = Shape(mesh, rows, width, hidden)
        dp, seq, chips, pairs = s.dp, s.seq, s.chips, s.pairs
        nk = chips - 1
        vectors = (gain_one, shift_one, b_qk, b_out, gain_two, shift_two, b_up, b_down)
        vmem = pl.BlockSpec(memory_space=pltpu.VMEM)
        anywhere = pl.BlockSpec(memory_space=pl.ANY)
        grids = [(chips, 2) + shape for shape in s.weights]
        shapes = [(s.weights[index][0], columns) for index, _, columns in s.scatters]
        dma = pltpu.SemaphoreType.DMA
        short = (len(shapes) - 2, len(shapes) - 1) if seq == 4 else range(len(shapes))
        tall = s.weights[0][0]
        message_rows = pairs // 2 * LANES + -(-pairs // 8) * 8
        scratch = (
            [pltpu.VMEM(grid, bf16) for grid in grids]
            + [
                pltpu.VMEM((rows, width), bf16),
                pltpu.VMEM((rows, width), bf16),
                pltpu.VMEM((width, rows), bf16),
                pltpu.VMEM((rows, 3 * width), bf16),
                pltpu.VMEM((rows, 2 * width), f32),
                pltpu.VMEM((s.chunks, CHUNK, CHUNK), bf16),
                pltpu.VMEM((rows, width), f32),
                pltpu.VMEM((pairs, LANES, 2 * LANES), f32),
                pltpu.VMEM((s.chunks, pairs, 2 * LANES, 2 * LANES), bf16),
                pltpu.VMEM((width, rows), bf16),
                pltpu.VMEM((rows, hidden), bf16),
                pltpu.VMEM((rows // (2 * tall), 2, tall, hidden), bf16),
                pltpu.VMEM((rows, width), f32),
                pltpu.VMEM((rows, width), bf16),
                pltpu.VMEM((8, hidden), f32),
                pltpu.VMEM((8, s.vec_lanes), f32),
                pltpu.VMEM((dp, 8, s.vec_lanes), f32),
                pltpu.VMEM((8, sum(s.sizes)), f32),
                pltpu.VMEM((dp, 8, s.vec_lanes), f32),
                pltpu.VMEM((dp - 1, 8, s.vec_lanes), f32),
                pltpu.VMEM((8, s.vec_lanes), f32),
                pltpu.VMEM((seq - 1, 8, s.vec_lanes), f32),
                pltpu.VMEM((2, message_rows, LANES), f32),
                pltpu.VMEM((2, seq - 1, message_rows, LANES), f32),
                [pltpu.VMEM((chips,) + shape, bf16) for shape in shapes[:-3]],
                [pltpu.VMEM((nk,) + shape, bf16) for shape in shapes],
                [pltpu.VMEM(shape, bf16) for shape in shapes],
                [
                    pltpu.VMEM(((seq - 1) * shape[0], shape[1] // seq) if k in short else shape, bf16)
                    for k, shape in enumerate(shapes)
                ],
                [pltpu.VMEM(shape, bf16) for shape in shapes],
                dma((len(s.gathers),)),
                dma((len(s.gathers), nk + 1)),
                dma((len(s.gathers), nk + 1)),
                dma((2 * dp - 2 + seq - 1,)),
                dma((2 * dp - 2 + seq - 1,)),
                dma((2, seq - 1)),
                dma((2, seq - 1)),
                dma((len(s.scatters), nk + 2 * seq - 1)),
                dma((len(s.scatters), nk + 2 * seq - 1)),
                dma((1 + 2 * (rows // TALL),)),
            ]
        )
        outs = pl.pallas_call(
            functools.partial(kernel, s),
            out_shape=(
                jax.ShapeDtypeStruct((rows, width), bf16),
                jax.ShapeDtypeStruct((rows, width), bf16),
            )
            + tuple(jax.ShapeDtypeStruct(shape, bf16) for shape in s.weights)
            + (jax.ShapeDtypeStruct((8, s.vec_lanes), f32),),
            in_specs=[pl.BlockSpec(memory_space=pltpu.SMEM), vmem, anywhere, [vmem] * 8]
            + [anywhere] * 4,
            out_specs=(anywhere, anywhere) + (vmem,) * 5,
            scratch_shapes=scratch,
            compiler_params=pltpu.CompilerParams(
                collective_id=0, has_side_effects=True, vmem_limit_bytes=63 << 20
            ),
            name="layer",
        )(
            lengths.reshape(3),
            inputs.reshape(rows, width),
            cotangent.reshape(rows, width),
            [v.reshape(-1, min(v.shape[0], LANES)) for v in vectors],
            w_qkv,
            w_out,
            w_up,
            w_down,
        )
        out, gin, *grads = widen(s, vectors, outs)
        g_qkv, g_out, g_up, g_down, *pieces = grads
        pieces = [piece.reshape(piece.shape[1]) for piece in pieces]
        return (
            out.reshape(inputs.shape),
            gin.reshape(inputs.shape),
            pieces[0],
            pieces[1],
            g_qkv,
            pieces[2],
            g_out,
            pieces[3],
            pieces[4],
            pieces[5],
            g_up,
            pieces[6],
            g_down,
            pieces[7],
        )

    rows_spec = P("dp", None, "seq", None)
    one, two = P("dp"), P("dp", None)
    params = (one, one, two, one, two, one, one, one, two, one, two, one)
    return jax.shard_map(
        body,
        mesh=mesh,
        in_specs=(rows_spec, P("dp", None, None), rows_spec) + params,
        out_specs=(rows_spec, rows_spec) + params,
        check_vma=False,
    )
```
